32 devices in a mesh: ctx: 8 (over y, x, core), shard: 4 (over z).
Axes of the slice: x: 2, y: 2, z: 4, core: 2. Of those that a mesh axis runs over, the one named last changes fastest.
Arguments:
- layer_input: bfloat16 [4, 1024, 2048], P('shard', 'ctx'), may hold values from -6 to 6
- out_grad: bfloat16 [4, 1024, 2048], P('shard', 'ctx'), may hold values from -6 to 6
- positions: int32 [4, 1024], P('shard'), may hold values from 0 to 1023, as said below
- w_qkv: float32 [2048, 6144], P(('ctx', 'shard')), may hold values from -0.1875 to 0.1875
- w_dense: float32 [2048, 2048], P(('ctx', 'shard')), may hold values from -0.75 to 0.75
- w_up: float32 [2048, 8192], P(('ctx', 'shard')), may hold values from -0.125 to 0.125
- w_down: float32 [8192, 2048], P(('ctx', 'shard')), may hold values from -0.0625 to 0.0625
- vectors: float32 [13, 2048], P(None, ('ctx', 'shard')), may hold values from -0.6 to 1.3
- m_qkv: float32 [2048, 6144], P(('ctx', 'shard')), may hold values from -128 to 128
- m_dense: float32 [2048, 2048], P(('ctx', 'shard')), may hold values from -8 to 8
- m_up: float32 [2048, 8192], P(('ctx', 'shard')), may hold values from -10 to 10
- m_down: float32 [8192, 2048], P(('ctx', 'shard')), may hold values from -20 to 20
- m_vectors: float32 [13, 2048], P(None, ('ctx', 'shard')), may hold values from -80 to 80
- v_qkv: float32 [2048, 6144], P(('ctx', 'shard')), may hold values from 970.752 to 15523.84
- v_dense: float32 [2048, 2048], P(('ctx', 'shard')), may hold values from 4.3008 to 68.8128
- v_up: float32 [2048, 8192], P(('ctx', 'shard')), may hold values from 6.71744 to 107.7248
- v_down: float32 [8192, 2048], P(('ctx', 'shard')), may hold values from 27.0336 to 430.08
- v_vectors: float32 [13, 2048], P(None, ('ctx', 'shard')), may hold values from 430.08 to 6881.28
Outputs:
- layer_output: bfloat16 [4, 1024, 2048], P('shard', 'ctx')
- grad_input: float32 [4, 1024, 2048], P('shard', 'ctx')
- grad_qkv: float32 [2048, 6144], P(('ctx', 'shard'))
- grad_dense: float32 [2048, 2048], P(('ctx', 'shard'))
- grad_up: float32 [2048, 8192], P(('ctx', 'shard'))
- grad_down: float32 [8192, 2048], P(('ctx', 'shard'))
- grad_vectors: float32 [13, 2048], P(None, ('ctx', 'shard'))
- second_qkv: float32 [2048, 6144], P(('ctx', 'shard'))
- second_dense: float32 [2048, 2048], P(('ctx', 'shard'))
- second_up: float32 [2048, 8192], P(('ctx', 'shard'))
- second_down: float32 [8192, 2048], P(('ctx', 'shard'))
- second_vectors: float32 [13, 2048], P(None, ('ctx', 'shard'))
- new_qkv: float32 [2048, 6144], P(('ctx', 'shard'))
- new_dense: float32 [2048, 2048], P(('ctx', 'shard'))
- new_up: float32 [2048, 8192], P(('ctx', 'shard'))
- new_down: float32 [8192, 2048], P(('ctx', 'shard'))
- new_vectors: float32 [13, 2048], P(None, ('ctx', 'shard'))
The draws below stay inside these ranges and needn't reach their ends.
Inputs may be any that keep to these rules, and one draw needn't show every extreme that they name: `positions`: each sequence holds every place once; stored rows k * 128 to (k + 1) * 128 - 1 hold 128 rising places that begin at a multiple of 128.
All inputs are finite; a program needn't handle non-finite values.
Results may differ from the reference program's by a relative error of at most 0.012.
The reference program's roundings to bfloat16 on the way count: a program that leaves them out, or rounds other values in their place, can miss the bound.
Values may be sent and summed in bfloat16 or wider, within the bound.
A program may use at most 640 MiB of HBM per device.

```python
import math
import jax
import jax.numpy as jnp
from jax import lax

D = 2048
H = 8
HD = 256
ROT = 64
FF = 8192
BLK = 128
STEP = 10
SEQ_LEN = 1024
SEQS = 4
ROWS_ALL = 4096


def draw_positions(key, part):
    key = jax.random.fold_in(key, 5)
    blocks = SEQ_LEN // BLK
    subkeys = jax.random.split(key, SEQS)

    def one_order(subkey):
        return jax.random.permutation(subkey, blocks)
    orders = jax.vmap(one_order)(subkeys).astype(jnp.int32)
    offsets = jnp.arange(BLK, dtype=jnp.int32)
    return (orders[:, :, None] * BLK + offsets[None, None, :]).reshape(SEQS, SEQ_LEN)


def draw_vectors(key, part):
    key = jax.random.fold_in(key, 11)
    noise = jnp.clip(jax.random.normal(key, (13, D), jnp.float32), -3.0, 3.0)
    row_ids = jnp.arange(13)[:, None]
    is_gain = (row_ids == 0) | (row_ids == 2)
    return jnp.where(is_gain, 1.0 + 0.1 * noise, 0.2 * noise)


def block_scale(stream_key, extent, shards, least, high):
    loudness = 1.0
    for axis_at, parts in shards:
        draws = jax.random.uniform(jax.random.fold_in(jax.random.fold_in(stream_key, 6), axis_at), (parts,), jnp.float32, least / len(shards), high / len(shards))
        loudness = loudness * jnp.repeat(jnp.exp(draws), extent[axis_at] // parts).reshape((-1,) + (1,) * (len(extent) - 1 - axis_at))
    return loudness


def bell_draw(rng, extent, scale, reach, shards=(), kind=jnp.bfloat16):
    entries = jax.random.normal(rng, extent, jnp.float32) * scale
    if len(shards) > 0:
        entries = block_scale(rng, extent, shards, -0.22, 0.18) * entries
    return jnp.clip(entries, min=-reach, max=reach).astype(kind)


def setup_inputs(seed: int = 0) -> dict:
    seeds = jax.random.split(jax.random.key(seed), 19)
    layer_input = bell_draw(seeds[0], (SEQS, SEQ_LEN, D), 1.0, 6.0, ((0, 4), (1, 8)))
    out_grad = bell_draw(seeds[1], (SEQS, SEQ_LEN, D), 1.0, 6.0, ((0, 4), (1, 8)))
    positions = draw_positions(jax.random.fold_in(seeds[18], 71), 0)
    w_qkv = bell_draw(seeds[3], (D, 3 * D), (D // 2) ** -0.5, 0.1875, ((0, 32),), jnp.float32)
    w_dense = bell_draw(seeds[4], (D, D), (D // 32) ** -0.5, 0.75, ((0, 32),), jnp.float32)
    w_up = bell_draw(seeds[5], (D, FF), D ** -0.5, 0.125, ((0, 32),), jnp.float32)
    w_down = bell_draw(seeds[6], (FF, D), FF ** -0.5, 0.0625, ((0, 32),), jnp.float32)
    vectors = draw_vectors(jax.random.fold_in(seeds[18], 71), 0)
    m_qkv = bell_draw(seeds[8], (D, 3 * D), (0.333 * ROWS_ALL ** 0.5), 128.0, ((0, 32),), jnp.float32)
    m_dense = bell_draw(seeds[9], (D, D), (0.0222 * ROWS_ALL ** 0.5), 8.0, ((0, 32),), jnp.float32)
    m_up = bell_draw(seeds[10], (D, FF), (0.0278 * ROWS_ALL ** 0.5), 10.0, ((0, 32),), jnp.float32)
    m_down = bell_draw(seeds[11], (FF, D), (0.0556 * ROWS_ALL ** 0.5), 20.0, ((0, 32),), jnp.float32)
    m_vectors = bell_draw(seeds[12], (13, D), (0.222 * ROWS_ALL ** 0.5), 80.0, ((1, 32),), jnp.float32)
    v_qkv = jnp.clip(jnp.exp(math.log(15523.84) - 2.772061 * jax.random.uniform(seeds[13], (D, 3 * D), jnp.float32) ** block_scale(seeds[13], (D, 3 * D), ((0, 32),), -0.2, 0.2)), 970.752, 15523.84)
    v_dense = jnp.clip(jnp.exp(math.log(68.8128) - 2.7725887 * jax.random.uniform(seeds[14], (D, D), jnp.float32) ** block_scale(seeds[14], (D, D), ((0, 32),), -0.2, 0.2)), 4.3008, 68.8128)
    v_up = jnp.clip(jnp.exp(math.log(107.7248) - 2.7748727 * jax.random.uniform(seeds[15], (D, FF), jnp.float32) ** block_scale(seeds[15], (D, FF), ((0, 32),), -0.2, 0.2)), 6.71744, 107.7248)
    v_down = jnp.clip(jnp.exp(math.log(430.08) - 2.7668907 * jax.random.uniform(seeds[16], (FF, D), jnp.float32) ** block_scale(seeds[16], (FF, D), ((0, 32),), -0.2, 0.2)), 27.0336, 430.08)
    v_vectors = jnp.clip(jnp.exp(math.log(6881.28) - 2.7725887 * jax.random.uniform(seeds[17], (13, D), jnp.float32) ** block_scale(seeds[17], (13, D), ((1, 32),), -0.2, 0.2)), 430.08, 6881.28)
    return dict(layer_input=layer_input, out_grad=out_grad, positions=positions, w_qkv=w_qkv, w_dense=w_dense, w_up=w_up, w_down=w_down, vectors=vectors, m_qkv=m_qkv, m_dense=m_dense, m_up=m_up, m_down=m_down, m_vectors=m_vectors, v_qkv=v_qkv, v_dense=v_dense, v_up=v_up, v_down=v_down, v_vectors=v_vectors)


@jax.custom_vjp
def low(v):
    return lax.optimization_barrier(v.astype(jnp.bfloat16)).astype(jnp.float32)

@jax.custom_vjp
def low_back(v):
    return v

def low_keep(v):
    return (low(v), None)

def low_pass(kept, grad):
    return (grad,)

def back_keep(v):
    return (v, None)

def back_low(kept, grad):
    return (low(grad),)
low.defvjp(low_keep, low_pass)
low_back.defvjp(back_keep, back_low)

def layer_norm(values, gain, shift):
    center = values - lax.optimization_barrier(jnp.mean(values, axis=-1, keepdims=True))
    spread = lax.optimization_barrier(jnp.mean(center * center, axis=-1, keepdims=True))
    return center * lax.rsqrt(spread + 1e-05) * gain + shift

def angles(places):
    inverse = 10000.0 ** (-jnp.arange(0, ROT, 2).astype(jnp.float32) / ROT)
    phases = places.astype(jnp.float32)[:, None] * inverse[None, :]
    return (jnp.cos(phases), jnp.sin(phases))

def rotate(values, cosine, sine):
    half_rot = cosine.shape[-1]
    front = values[..., :half_rot]
    second = values[..., half_rot:2 * half_rot]
    others = values[..., 2 * half_rot:]
    cos_b = cosine[:, None, :]
    sin_b = sine[:, None, :]
    return jnp.concatenate([front * cos_b - second * sin_b, second * cos_b + front * sin_b, others], axis=-1)

def matmul_exact(left, right):
    return jnp.dot(left, right, precision=lax.Precision.HIGHEST, preferred_element_type=jnp.float32)

def attend(q_rot, k_rot, v_low, places):
    length = places.shape[0]
    size_rows = min(512, length)
    count_blocks = length // size_rows

    def score_block(pair):
        q_blk, p_blk = pair
        scores = jnp.einsum('qhd,khd->qhk', q_blk, k_rot, precision=lax.Precision.HIGHEST) * HD ** (-0.5)
        scores = low_back(scores)
        allowed = (places[None, :] <= p_blk[:, None])[:, None, :]
        scores = jnp.where(allowed, scores, -1e+30)
        weights = low(jax.nn.softmax(scores, axis=-1))
        return jnp.einsum('qhk,khd->qhd', weights, v_low, precision=lax.Precision.HIGHEST)
    result = lax.map(jax.checkpoint(score_block), (q_rot.reshape(count_blocks, size_rows, H, HD), places.reshape(count_blocks, size_rows)))
    return result.reshape(length, H, HD)

def block_layer(tokens, places, w_qkv, w_dense, w_up, w_down, vectors):
    length = tokens.shape[0]
    normed_one = low(layer_norm(tokens, vectors[0], vectors[1]))
    normed_two = low(layer_norm(tokens, vectors[2], vectors[3]))
    projection = low_back(matmul_exact(normed_one, w_qkv) + vectors[4:7].reshape(-1))
    queries = projection[:, :D].reshape(length, H, HD)
    keys_raw = projection[:, D:2 * D].reshape(length, H, HD)
    values_raw = projection[:, 2 * D:].reshape(length, H, HD)
    cosine, sine = angles(places)
    q_rot = low(rotate(queries, cosine, sine))
    k_rot = low(rotate(keys_raw, cosine, sine))
    v_low = low(values_raw)
    attention = attend(q_rot, k_rot, v_low, places).reshape(length, D)
    attn_low = low_back(low(attention))
    up_value = low_back(matmul_exact(normed_two, w_up) + vectors[8:12].reshape(-1))
    hid_low = low(jax.nn.gelu(up_value, approximate=False))
    return tokens + matmul_exact(attn_low, w_dense) + vectors[7] + matmul_exact(hid_low, w_down) + vectors[12]

def adam_step(weight, gradient, moment, second, rate, decay):
    moment = 0.9 * moment + 0.1 * gradient
    second = 0.95 * second + 0.05 * gradient * gradient
    unbiased = moment / (1.0 - 0.9 ** STEP)
    scaled = second / (1.0 - 0.95 ** STEP)
    return (weight - rate * (unbiased / (jnp.sqrt(scaled) + 1e-08) + decay * weight), second)

def reference(layer_input, out_grad, positions, w_qkv, w_dense, w_up, w_down, vectors, m_qkv, m_dense, m_up, m_down, m_vectors, v_qkv, v_dense, v_up, v_down, v_vectors):

    def forward(tokens, weight_qkv, weight_dense, weight_up, weight_down, vector_rows):
        low_qkv = low(weight_qkv)
        low_dense = low(weight_dense)
        low_up = low(weight_up)
        low_down = low(weight_down)

        def one_sequence(pair):
            return block_layer(pair[0], pair[1], low_qkv, low_dense, low_up, low_down, vector_rows)
        return lax.map(jax.checkpoint(one_sequence), (tokens, positions))
    result, pullback = jax.vjp(forward, layer_input.astype(jnp.float32), w_qkv, w_dense, w_up, w_down, vectors)
    grad_input, grad_qkv, grad_dense, grad_up, grad_down, grad_vectors = pullback(out_grad.astype(jnp.float32))
    new_qkv, second_qkv = adam_step(w_qkv, grad_qkv, m_qkv, v_qkv, 4.0 * (D // 2) ** (-0.5), 0.1)
    new_dense, second_dense = adam_step(w_dense, grad_dense, m_dense, v_dense, 4.0 * (D // 32) ** (-0.5), 0.1)
    new_up, second_up = adam_step(w_up, grad_up, m_up, v_up, 4.0 * D ** (-0.5), 0.1)
    new_down, second_down = adam_step(w_down, grad_down, m_down, v_down, 4.0 * FF ** (-0.5), 0.1)
    new_vectors, second_vectors = adam_step(vectors, grad_vectors, m_vectors, v_vectors, 1.0, 0.0)
    return (result.astype(jnp.bfloat16), grad_input, grad_qkv, grad_dense, grad_up, grad_down, grad_vectors, second_qkv, second_dense, second_up, second_down, second_vectors, new_qkv, new_dense, new_up, new_down, new_vectors)
```

```python
from functools import partial

import jax
import jax.numpy as jnp
from jax import lax
from jax.experimental import pallas as pl
from jax.experimental.pallas import tpu as pltpu
from jax.sharding import Mesh, PartitionSpec as P

D = 2048
H = 8
HD = 256
ROT = 64
FF = 8192
STEP = 10


def from_behind(value, axis, steps):
    count = lax.axis_size(axis)
    pairs = [(source, (source + steps) % count) for source in range(count)]
    return lax.ppermute(value, axis, pairs)


def layer_norm(values, gain, shift):
    center = values - jnp.mean(values, axis=-1, keepdims=True)
    spread = jnp.mean(center * center, axis=-1, keepdims=True)
    return center * lax.rsqrt(spread + 1e-05) * gain + shift


def angles(places):
    inverse = 10000.0 ** (-jnp.arange(0, ROT, 2).astype(jnp.float32) / ROT)
    phases = places.astype(jnp.float32)[:, None] * inverse[None, :]
    return (jnp.cos(phases), jnp.sin(phases))


def rotate(values, cosine, sine):
    half_rot = cosine.shape[-1]
    front = values[..., :half_rot]
    second = values[..., half_rot : 2 * half_rot]
    others = values[..., 2 * half_rot :]
    cos_b = cosine[:, None, :]
    sin_b = sine[:, None, :]
    return jnp.concatenate(
        [front * cos_b - second * sin_b, second * cos_b + front * sin_b, others], axis=-1
    )


def adam_step(weight, gradient, moment, second, rate, decay):
    moment = 0.9 * moment + 0.1 * gradient
    second = 0.95 * second + 0.05 * gradient * gradient
    unbiased = moment / (1.0 - 0.9**STEP)
    scaled = second / (1.0 - 0.95**STEP)
    return (weight - rate * (unbiased / (jnp.sqrt(scaled) + 1e-08) + decay * weight), second)


def general_device(
    layer_input,
    out_grad,
    positions,
    w_qkv,
    w_dense,
    w_up,
    w_down,
    vectors,
    m_qkv,
    m_dense,
    m_up,
    m_down,
    m_vectors,
    v_qkv,
    v_dense,
    v_up,
    v_down,
    v_vectors,
):
    block_rows = layer_input.shape[1]
    model_width = layer_input.shape[2]
    hidden = w_up.shape[1]
    rows_in = w_qkv.shape[0]
    rows_down = w_down.shape[0]
    n_ctx = lax.axis_size("ctx")
    score_scale = HD ** (-0.5)
    ctx_index = lax.axis_index("ctx")
    all_pos = positions[0]
    own_pos = lax.dynamic_slice_in_dim(all_pos, ctx_index * block_rows, block_rows)
    last_own = jnp.max(own_pos)
    cosine, sine = angles(own_pos)
    full_vec = lax.all_gather(vectors, ("ctx", "shard"), axis=1, tiled=True)
    tokens = layer_input[0].astype(jnp.float32)
    normed_one = layer_norm(tokens, full_vec[0], full_vec[1]).astype(jnp.bfloat16)
    normed_two = layer_norm(tokens, full_vec[2], full_vec[3]).astype(jnp.bfloat16)
    qkv_low = w_qkv.astype(jnp.bfloat16)
    dense_low = w_dense.astype(jnp.bfloat16)
    up_low = w_up.astype(jnp.bfloat16)
    down_low = w_down.astype(jnp.bfloat16)
    grad_low = out_grad[0]
    grad_rows = grad_low.astype(jnp.float32)
    pieces = (
        lax.all_gather(qkv_low, ("ctx", "shard"), axis=0, tiled=True),
        lax.all_gather(up_low, ("ctx", "shard"), axis=0, tiled=True),
    )
    left_one = normed_one
    left_two = normed_two
    proj_sum = jnp.dot(left_one, pieces[0], preferred_element_type=jnp.float32)
    up_sum = jnp.dot(left_two, pieces[1], preferred_element_type=jnp.float32)
    projection = proj_sum + full_vec[4:7].reshape(-1)
    up_value = up_sum + full_vec[8:12].reshape(-1)
    queries = projection[:, :model_width].reshape(block_rows, H, HD)
    keys_raw = projection[:, model_width : 2 * model_width].reshape(block_rows, H, HD)
    values_raw = projection[:, 2 * model_width :].reshape(block_rows, H, HD)
    q_rot = rotate(queries, cosine, sine).astype(jnp.bfloat16)
    k_rot = rotate(keys_raw, cosine, sine).astype(jnp.bfloat16)
    v_low = values_raw.astype(jnp.bfloat16)
    start_state = (
        jnp.full((block_rows, H), -1e30, jnp.float32),
        jnp.zeros((block_rows, H), jnp.float32),
        jnp.zeros((block_rows, H, HD), jnp.float32),
    )
    pieces = (
        lax.all_gather(k_rot, "ctx", axis=0, tiled=True),
        lax.all_gather(v_low, "ctx", axis=0, tiled=True),
    )
    key_pos = all_pos
    allowed = (key_pos[None, :] <= own_pos[:, None])[:, None, :]

    def attend_compute(states):
        running_top, totals, accum = states
        scores = (
            jnp.einsum("qhd,khd->qhk", q_rot, pieces[0], preferred_element_type=jnp.float32)
            * score_scale
        )
        scores = jnp.where(allowed, scores, -1e30)
        new_top = jnp.maximum(running_top, jnp.max(scores, axis=-1))
        weights = jnp.where(allowed, jnp.exp(scores - new_top[..., None]), 0.0)
        totals = jnp.sum(weights, axis=-1)
        accum = jnp.einsum(
            "qhk,khd->qhd",
            weights.astype(jnp.bfloat16),
            pieces[1],
            preferred_element_type=jnp.float32,
        )
        return (new_top, totals, accum)

    skipped = jnp.min(key_pos) > last_own
    running_top, totals, accum = lax.cond(
        skipped, lambda states: states, attend_compute, start_state
    )
    attention = accum / totals[..., None]
    log_sum = running_top + jnp.log(totals)
    attn_low = attention.reshape(block_rows, model_width).astype(jnp.bfloat16)
    gelu_exact = partial(jax.nn.gelu, approximate=False)
    hid_low = gelu_exact(up_value).astype(jnp.bfloat16)
    add_pieces = (
        lax.all_gather(dense_low, ("ctx", "shard"), axis=0, tiled=True),
        lax.all_gather(down_low, ("ctx", "shard"), axis=0, tiled=True),
    )
    second_count = add_pieces[1].shape[0]
    second_begin = jnp.int32(0) // rows_in * rows_down
    left_attn = attn_low
    left_hid = lax.dynamic_slice_in_dim(hid_low, second_begin, second_count, 1)
    branches = jnp.dot(left_attn, add_pieces[0], preferred_element_type=jnp.float32) + jnp.dot(
        left_hid, add_pieces[1], preferred_element_type=jnp.float32
    )
    back_pieces = lax.all_gather((dense_low, down_low), ("ctx", "shard"), axis=0, tiled=True)
    shard_count = back_pieces[0].shape[0] // rows_in
    first_part = jnp.einsum(
        "td,rd->tr", grad_low, back_pieces[0], preferred_element_type=jnp.float32
    ).reshape(block_rows, shard_count, rows_in)
    second_part = jnp.einsum(
        "td,rd->tr", grad_low, back_pieces[1], preferred_element_type=jnp.float32
    ).reshape(block_rows, shard_count, rows_down)
    merged_out = jnp.concatenate([first_part, second_part], axis=2).reshape(
        block_rows, shard_count * (rows_in + rows_down)
    )
    merged_out = merged_out.reshape(block_rows, -1, rows_in + rows_down)
    grad_attn = merged_out[:, :, :rows_in].reshape(block_rows, model_width)
    grad_hid = merged_out[:, :, rows_in:].reshape(block_rows, hidden)
    layer_output = (tokens + branches + full_vec[7] + full_vec[12]).astype(jnp.bfloat16)[None]
    gelu_pull = jax.vjp(gelu_exact, up_value)[1]
    grad_upval = gelu_pull(grad_hid)[0].astype(jnp.bfloat16)
    grad_heads = grad_attn.astype(jnp.bfloat16).reshape(block_rows, H, HD)
    delta_rows = jnp.sum(grad_heads.astype(jnp.float32) * attention, axis=-1)

    def key_turn(turn_index, states):
        pair_now, pair_grad, query_grad = states
        owner_index = (ctx_index - turn_index) % n_ctx
        key_pos = lax.dynamic_slice_in_dim(all_pos, owner_index * block_rows, block_rows)
        allowed = (key_pos[None, :] <= own_pos[:, None])[:, None, :]

        def key_compute(partials):
            grads_held, query_held = partials
            scores = (
                jnp.einsum("qhd,khd->qhk", q_rot, pair_now[0], preferred_element_type=jnp.float32)
                * score_scale
            )
            weights_now = jnp.where(allowed, jnp.exp(scores - log_sum[..., None]), 0.0)
            grad_prob = jnp.einsum(
                "qhd,khd->qhk", grad_heads, pair_now[1], preferred_element_type=jnp.float32
            )
            dscore = (weights_now * (grad_prob - delta_rows[..., None])).astype(jnp.bfloat16)
            query_held = (
                query_held
                + jnp.einsum(
                    "qhk,khd->qhd", dscore, pair_now[0], preferred_element_type=jnp.float32
                )
                * score_scale
            )
            key_term = (
                jnp.einsum("qhk,qhd->khd", dscore, q_rot, preferred_element_type=jnp.float32)
                * score_scale
            )
            value_term = jnp.einsum(
                "qhk,qhd->khd",
                weights_now.astype(jnp.bfloat16),
                grad_heads,
                preferred_element_type=jnp.float32,
            )
            return (grads_held + jnp.stack([key_term, value_term]), query_held)

        skipped = jnp.min(key_pos) > last_own
        pair_grad, query_grad = lax.cond(
            skipped, lambda partials: partials, key_compute, (pair_grad, query_grad)
        )
        pair_now = from_behind(pair_now, "ctx", 1)
        pair_grad = from_behind(pair_grad.astype(jnp.bfloat16), "ctx", 1).astype(pair_grad.dtype)
        return (pair_now, pair_grad, query_grad)

    loop_start = (
        jnp.stack([k_rot, v_low]),
        jnp.zeros((2, block_rows, H, HD), jnp.float32),
        jnp.zeros((block_rows, H, HD), jnp.float32),
    )
    loop_end = lax.fori_loop(0, n_ctx, key_turn, loop_start)
    pair_grad = loop_end[1]
    query_grad = loop_end[2]

    def turn_values(values):
        return rotate(values, cosine, sine)

    rot_pull = jax.vjp(turn_values, queries)[1]
    grad_proj = jnp.concatenate(
        [
            rot_pull(query_grad)[0].reshape(block_rows, model_width),
            rot_pull(pair_grad[0])[0].reshape(block_rows, model_width),
            pair_grad[1].reshape(block_rows, model_width),
        ],
        axis=1,
    ).astype(jnp.bfloat16)

    def back_inputs(pieces):
        shard_count = pieces[0].shape[0] // rows_in
        first_part = jnp.einsum(
            "tc,rc->tr", grad_proj, pieces[0], preferred_element_type=jnp.float32
        ).reshape(block_rows, shard_count, 1, rows_in)
        second_part = jnp.einsum(
            "tc,rc->tr", grad_upval, pieces[1], preferred_element_type=jnp.float32
        ).reshape(block_rows, shard_count, 1, rows_in)
        return jnp.concatenate([first_part, second_part], axis=2).reshape(
            block_rows, shard_count * 2 * rows_in
        )

    merged_in = back_inputs(lax.all_gather((qkv_low, up_low), ("ctx", "shard"), axis=0, tiled=True))
    merged_in = merged_in.reshape(block_rows, -1, 2, rows_in)
    grad_norm_one = merged_in[:, :, 0].reshape(block_rows, model_width)
    grad_norm_two = merged_in[:, :, 1].reshape(block_rows, model_width)
    norm_pull_one = jax.vjp(layer_norm, tokens, full_vec[0], full_vec[1])[1]
    norm_pull_two = jax.vjp(layer_norm, tokens, full_vec[2], full_vec[3])[1]
    back_one, gain_one, shift_one = norm_pull_one(grad_norm_one)
    back_two, gain_two, shift_two = norm_pull_two(grad_norm_two)
    grad_input = (grad_rows + back_one + back_two)[None]
    column_out = jnp.sum(grad_rows, axis=0)
    vector_terms = jnp.concatenate(
        [
            jnp.stack([gain_one, shift_one, gain_two, shift_two]),
            jnp.sum(grad_proj.astype(jnp.float32), axis=0).reshape(3, model_width),
            column_out[None],
            jnp.sum(grad_upval.astype(jnp.float32), axis=0).reshape(4, model_width),
            column_out[None],
        ],
        axis=0,
    )
    grad_vectors = lax.psum_scatter(vector_terms, ("ctx", "shard"), scatter_dimension=1, tiled=True)
    block_count = (rows_in + rows_down) * lax.axis_size(("ctx", "shard")) // (rows_in + rows_down)
    first_block = jnp.int32(0) // (rows_in + rows_down)
    left_attn = attn_low
    left_hid = lax.dynamic_slice_in_dim(
        hid_low, first_block * rows_down, block_count * rows_down, 1
    )
    dense_part = jnp.einsum(
        "tr,td->rd", left_attn, grad_low, preferred_element_type=jnp.float32
    ).reshape(block_count, rows_in, model_width)
    down_part = jnp.einsum(
        "tr,td->rd", left_hid, grad_low, preferred_element_type=jnp.float32
    ).reshape(block_count, rows_down, model_width)
    out_grads = lax.psum_scatter(
        jnp.concatenate([dense_part, down_part], axis=1).reshape(
            (rows_in + rows_down) * lax.axis_size(("ctx", "shard")), model_width
        ),
        ("ctx", "shard"),
        scatter_dimension=0,
        tiled=True,
    )
    left_one = normed_one
    left_two = normed_two
    in_grads = lax.psum_scatter(
        jnp.concatenate(
            [
                jnp.einsum("tr,tc->rc", left_one, grad_proj, preferred_element_type=jnp.float32),
                jnp.einsum("tr,tc->rc", left_two, grad_upval, preferred_element_type=jnp.float32),
            ],
            axis=1,
        ),
        ("ctx", "shard"),
        scatter_dimension=0,
        tiled=True,
    )
    grad_qkv = in_grads[:, : 3 * model_width]
    grad_up = in_grads[:, 3 * model_width :]
    grad_dense = out_grads[:rows_in]
    grad_down = out_grads[rows_in:]
    new_qkv, second_qkv = adam_step(w_qkv, grad_qkv, m_qkv, v_qkv, 4.0 * (D // 2) ** (-0.5), 0.1)
    new_dense, second_dense = adam_step(
        w_dense, grad_dense, m_dense, v_dense, 4.0 * (D // 32) ** (-0.5), 0.1
    )
    new_up, second_up = adam_step(w_up, grad_up, m_up, v_up, 4.0 * D ** (-0.5), 0.1)
    new_down, second_down = adam_step(w_down, grad_down, m_down, v_down, 4.0 * FF ** (-0.5), 0.1)
    new_vectors, second_vectors = adam_step(vectors, grad_vectors, m_vectors, v_vectors, 1.0, 0.0)
    return (
        layer_output,
        grad_input,
        grad_qkv,
        grad_dense,
        grad_up,
        grad_down,
        grad_vectors,
        second_qkv,
        second_dense,
        second_up,
        second_down,
        second_vectors,
        new_qkv,
        new_dense,
        new_up,
        new_down,
        new_vectors,
    )


MESH = pl.DeviceIdType.MESH
VMEM_BYTES = 62 * 1024 * 1024


def push(source, target, sent, arrived, **device):
    return pltpu.make_async_remote_copy(
        src_ref=source,
        dst_ref=target,
        send_sem=sent,
        recv_sem=arrived,
        device_id=device,
        device_id_type=MESH,
    )


class Spot:
    def __init__(self, n_plane, n_shard):
        self.n_plane, self.n_shard = n_plane, n_shard
        self.plane = lax.axis_index("plane")
        self.core = lax.axis_index("core")
        self.shard = lax.axis_index("shard")
        self.slot = self.core * n_shard + self.shard
        head = 2 * self.plane + self.core
        self.head_core = lax.div(head, n_shard)
        self.head_shard = lax.rem(head, n_shard)
        self.owner_plane = lax.div(self.slot, 2)
        self.owner_core = lax.rem(self.slot, 2)
        self.head_here = jnp.logical_and(self.slot == head, self.plane == self.shard)

    def group(self):
        for turn in range(1, 2 * self.n_shard):
            yield turn - 1, self.turned(turn)

    def turned(self, turn):
        core = lax.rem(self.core + turn // self.n_shard, 2)
        shard = lax.rem(self.shard + turn % self.n_shard, self.n_shard)
        return dict(core=core, shard=shard)

    def beside(self):
        across = self.plane + 1 - 2 * lax.rem(self.plane, 2)
        return across, lax.rem(self.plane + 2, 4), 3 - self.plane

    def along(self):
        for step in range(1, self.n_shard):
            yield step - 1, lax.rem(self.shard + step, self.n_shard)

    def planes(self):
        for step in range(1, self.n_plane):
            yield step - 1, lax.rem(self.plane + step, self.n_plane)

    def keeper(self):
        return dict(plane=self.shard, core=self.head_core, shard=self.head_shard)

    def owner(self):
        return dict(plane=self.owner_plane, core=self.owner_core, shard=self.plane)

    def greet(self, sender):
        barrier = pltpu.get_barrier_semaphore()
        count = 0
        for _, device in self.group():
            pl.semaphore_signal(barrier, inc=1, device_id=device, device_id_type=MESH)
            count += 1
        for _, plane in self.planes():
            pl.semaphore_signal(barrier, inc=1, device_id=dict(plane=plane), device_id_type=MESH)
            count += 1

        @pl.when(jnp.logical_not(self.head_here))
        def _():
            pl.semaphore_signal(barrier, inc=1, device_id=sender, device_id_type=MESH)
            pl.semaphore_wait(barrier, count + 1)

        @pl.when(self.head_here)
        def _():
            pl.semaphore_wait(barrier, count)


def turn_tables(pos_row, freq):
    n_pos = pos_row.shape[1]
    places = jnp.broadcast_to(pos_row.astype(jnp.float32), (n_pos, n_pos)).T
    phase = places * freq
    return jnp.cos(phase), jnp.sin(phase), places


def turn(head, cosine, sine):
    half = ROT // 2
    lanes = cosine.shape[1]
    front = head[:, :lanes]
    lane = lax.broadcasted_iota(jnp.int32, front.shape, 1)
    first = jnp.where(lane < half, -sine, 0.0)
    second = jnp.where((lane >= half) & (lane < ROT), sine, 0.0)
    turned = (
        front * cosine
        + pltpu.roll(front, lanes - half, 1) * first
        + pltpu.roll(front, half, 1) * second
    )
    return jnp.concatenate([turned, head[:, lanes:]], axis=1)


def dot(left, right, left_dim=1, right_dim=0):
    return lax.dot_general(
        left, right, (((left_dim,), (right_dim,)), ((), ())), preferred_element_type=jnp.float32
    )


class Spread:
    def __init__(self, spot, ref, size, sent, here):
        self.spot, self.ref, self.size, self.sent, self.here = spot, ref, size, sent, here
        self.across, self.along, self.diagonal = spot.beside()

    def rows(self, plane, part=None):
        size = self.size
        if part is None:
            return self.ref.at[pl.ds(pl.multiple_of(plane * size, size), size)]
        half = size // 2
        return self.ref.at[pl.ds(pl.multiple_of(plane * size + part * half, half), half)]

    def send(self, rows, place, plane):
        return push(rows, rows, self.sent.at[place], self.here.at[place], plane=plane)

    def first(self):
        own = self.rows(self.spot.plane)
        return [self.send(own, 0, self.across), self.send(own, 1, self.along)]

    def second(self):
        return [
            self.send(self.rows(self.along, 0), 2, self.across),
            self.send(self.rows(self.across, 1), 3, self.along),
        ]

    def start(self):
        for copy in self.first():
            copy.start()

    def relay(self):
        first, second = self.first(), self.second()
        first[1].wait_recv()
        second[0].start()
        first[0].wait_recv()
        second[1].start()

    def finish(self):
        for copy in self.second():
            copy.wait_recv()

    def finish_sends(self):
        for copy in self.first() + self.second():
            copy.wait_send()


class Gather:
    def __init__(self, spot, part, size, landed, sent, here):
        self.spot, self.part, self.size, self.landed = spot, part, size, landed
        self.sent, self.here = sent, here
        self.across, self.along, self.diagonal = spot.beside()

    def rows(self, plane, side):
        half = self.size // 2
        return self.part.at[pl.ds(pl.multiple_of(plane * self.size + side * half, half), half)]

    def send(self, rows, place, plane):
        return push(
            rows, self.landed.at[place], self.sent.at[place], self.here.at[place], plane=plane
        )

    def first(self):
        return [
            self.send(self.rows(self.diagonal, 0), 0, self.across),
            self.send(self.rows(self.diagonal, 1), 1, self.along),
            self.send(self.rows(self.across, 0), 2, self.across),
            self.send(self.rows(self.along, 1), 3, self.along),
        ]

    def second(self):
        return [
            self.send(self.rows(self.along, 0), 4, self.along),
            self.send(self.rows(self.across, 1), 5, self.across),
        ]

    def start(self):
        for copy in self.first():
            copy.start()

    def relay(self):
        first, second = self.first(), self.second()
        for side in range(2):
            first[side].wait_recv()
            held = self.rows(self.along if side == 0 else self.across, side)
            add_rows(held, [held, self.landed.at[side]], self.size // 2)
            second[side].start()

    def own(self):
        size = self.size
        return self.part.at[pl.ds(pl.multiple_of(self.spot.plane * size, size), size)]

    def finish(self):
        first, second = self.first(), self.second()
        half = self.size // 2
        for side in range(2):
            first[2 + side].wait_recv()
            second[side].wait_recv()
            held = self.rows(self.spot.plane, side)
            add_rows(held, [held, self.landed.at[2 + side], self.landed.at[4 + side]], half)

    def finish_sends(self):
        for copy in self.first() + self.second():
            copy.wait_send()


class RowSum:
    def __init__(self, spot, part, landed, sent, here):
        self.spot, self.part, self.landed = spot, part, landed
        self.sent, self.here = sent, here

    def rows(self, shard):
        return self.part.at[shard]

    def place(self, side, at, shard):
        if side == 0:
            return shard
        return jnp.where(shard == at, self.spot.n_shard, shard)

    def hop(self, side, shard):
        spot = self.spot
        to = spot.shard + (1 if side == 0 else -1)
        return push(
            self.rows(shard),
            self.landed.at[self.place(side, to, shard)],
            self.sent.at[side, shard],
            self.here.at[side, shard],
            shard=to,
        )

    def wait(self, side, shard):
        spot = self.spot
        push(
            self.rows(shard),
            self.landed.at[self.place(side, spot.shard, shard)],
            self.sent.at[side, shard],
            self.here.at[side, shard],
            shard=spot.shard,
        ).wait_recv()

    def start(self):
        spot, last = self.spot, self.spot.n_shard - 1
        for side in range(2):

            @pl.when(spot.shard == (0 if side == 0 else last))
            def _():
                for step in range(last):
                    self.hop(side, last - step if side == 0 else step).start()

    def relay(self, turn):
        spot, last = self.spot, self.spot.n_shard - 1
        for side in range(2):
            depth = spot.shard if side == 0 else last - spot.shard
            shard = last - turn + spot.shard if side == 0 else turn - last + spot.shard

            @pl.when(jnp.logical_and(depth >= 1, depth <= turn))
            def _():
                self.wait(side, shard)
                held = self.rows(shard)
                came = self.landed.at[self.place(side, spot.shard, shard)]
                add_rows(held, [held, came], held.shape[0])
                self.hop(side, shard).start()

    def finish(self, target):
        spot, last = self.spot, self.spot.n_shard - 1
        held = self.rows(spot.shard)
        first = self.landed.at[self.place(0, spot.shard, spot.shard)]
        second = self.landed.at[self.place(1, spot.shard, spot.shard)]

        @pl.when(spot.shard >= 1)
        def _():
            self.wait(0, spot.shard)

        @pl.when(spot.shard < last)
        def _():
            self.wait(1, spot.shard)

        @pl.when(spot.shard == 0)
        def _():
            add_rows(target, [held, second], held.shape[0])

        @pl.when(spot.shard == last)
        def _():
            add_rows(target, [held, first], held.shape[0])

        @pl.when(jnp.logical_and(spot.shard >= 1, spot.shard < last))
        def _():
            add_rows(target, [held, first, second], held.shape[0])

    def finish_sends(self):
        spot = self.spot
        for shard in range(spot.n_shard):
            for side in range(2):

                @pl.when(spot.shard < shard if side == 0 else spot.shard > shard)
                def _():
                    self.hop(side, shard).wait_send()


class Chain:
    def __init__(self, spot, ref, block, sent, here, pair_sent, pair_here):
        self.spot, self.ref, self.block = spot, ref, block
        self.sent, self.here = sent, here
        self.pair_sent, self.pair_here = pair_sent, pair_here

    def rows(self, shard, core):
        start = pl.multiple_of((shard * 2 + core) * self.block, self.block)
        return self.ref.at[pl.ds(start, self.block)]

    def hop(self, side, dist):
        spot = self.spot
        sign = 1 if side == 0 else -1
        rows = self.rows(spot.shard - sign * dist, spot.core)
        return push(
            rows, rows, self.sent.at[side, dist], self.here.at[side, dist], shard=spot.shard + sign
        )

    def pair(self, side, dist):
        spot = self.spot
        sign = 1 if side == 0 else -1
        rows = self.rows(spot.shard - sign * dist, spot.core)
        return push(
            rows,
            rows,
            self.pair_sent.at[side, dist],
            self.pair_here.at[side, dist],
            core=1 - spot.core,
        )

    def holds(self, side, dist):
        spot = self.spot
        return spot.shard >= dist if side == 0 else spot.shard + dist < spot.n_shard

    def goes(self, side, dist):
        spot = self.spot
        more = spot.shard + 1 < spot.n_shard if side == 0 else spot.shard >= 1
        return jnp.logical_and(self.holds(side, dist), more)

    def start(self):
        for side in range(2):

            @pl.when(self.goes(side, 0))
            def _():
                self.hop(side, 0).start()

        self.pair(0, 0).start()

    def step(self, dist):
        for side in range(2):

            @pl.when(self.holds(side, dist))
            def _():
                self.hop(side, dist - 1).wait_recv()
                if dist + 1 < self.spot.n_shard:

                    @pl.when(self.goes(side, dist))
                    def _():
                        self.hop(side, dist).start()

                self.pair(side, dist).start()

    def finish_pairs(self):
        self.pair(0, 0).wait_recv()
        for dist in range(1, self.spot.n_shard):
            for side in range(2):

                @pl.when(self.holds(side, dist))
                def _():
                    self.pair(side, dist).wait_recv()

    def finish_sends(self):
        self.pair(0, 0).wait_send()
        for side in range(2):
            for dist in range(self.spot.n_shard - 1):

                @pl.when(self.goes(side, dist))
                def _():
                    self.hop(side, dist).wait_send()

            for dist in range(1, self.spot.n_shard):

                @pl.when(self.holds(side, dist))
                def _():
                    self.pair(side, dist).wait_send()


def forward_kernel(
    n_plane,
    n_shard,
    x_ref,
    dy_ref,
    pos_ref,
    vec_ref,
    freq_ref,
    wq_ref,
    wu_ref,
    wd_ref,
    wo_ref,
    x_out,
    dy_out,
    one_out,
    two_out,
    hid_out,
    gup_out,
    back_out,
    wq_out,
    wu_out,
    wd_out,
    wo_out,
    vec_out,
    moments_out,
    x_all,
    dy_all,
    one,
    two,
    wq_all,
    wu_all,
    wd_all,
    wo_all,
    vec_all,
    pos_all,
    full_vec,
    wu_raw,
    wd_raw,
    wo_raw,
    wq_cut,
    wu_cut,
    wo_cut,
    to_heads,
    heads,
    from_heads,
    back,
    grad_k,
    grad_v,
    cos_head,
    sin_head,
    place_head,
    cos_row,
    sin_row,
    key_row,
    probs,
    attention,
    moments,
    loads,
    stores,
    local,
    x_sent,
    x_here,
    x_pair_sent,
    x_pair_here,
    dy_sent,
    dy_here,
    dy_pair_sent,
    dy_pair_here,
    pos_sent,
    pos_here,
    cols_sent,
    cols_here,
    flat_sent,
    flat_here,
    spread_sent,
    spread_here,
    swap_sent,
    swap_here,
    head_sent,
    head_here,
):
    spot = Spot(n_plane, n_shard)
    plane, core, shard, slot = spot.plane, spot.core, spot.shard, spot.slot
    f32, bf16 = jnp.float32, jnp.bfloat16
    block = x_ref.shape[0]
    pair = 2 * block
    n_slice = 2 * n_shard
    rows_in, rows_down = wq_ref.shape[0], wd_ref.shape[0]
    width = x_ref.shape[1]
    n_group = n_slice * block

    def piece(ref, at, size):
        return ref.at[pl.ds(pl.multiple_of(at * size, size), size)]

    chain_x = Chain(spot, x_all, block, x_sent, x_here, x_pair_sent, x_pair_here)
    chain_dy = Chain(spot, dy_all, block, dy_sent, dy_here, dy_pair_sent, dy_pair_here)

    raw = [
        pltpu.make_async_copy(source, held, loads.at[place])
        for place, (source, held) in enumerate(
            [
                (wq_ref, wu_raw.at[:, pl.ds(0, wq_ref.shape[1])]),
                (wu_ref, wu_raw),
                (wd_ref, wd_raw),
                (wo_ref, wo_raw),
                (x_ref, chain_x.rows(shard, core)),
                (dy_ref, chain_dy.rows(shard, core)),
                (pos_ref, pos_all.at[shard]),
                (vec_ref, vec_all.at[plane, slot]),
            ]
        )
    ]
    for place, copy in enumerate(raw):
        if place != 1:
            copy.start()
    spot.greet(spot.owner())

    index = plane * n_slice + slot
    wq_own = piece(wq_all, index, rows_in)
    wu_own = piece(wu_all, index, rows_in)

    def to_group(place, source, target):
        return [
            push(
                source(device["core"] * n_shard + device["shard"]),
                target,
                cols_sent.at[place, turn_at],
                cols_here.at[place, turn_at],
                **device,
            )
            for turn_at, device in spot.group()
        ]

    cols_q = to_group(0, lambda to: wq_cut.at[to], wq_own)
    cols_u = to_group(1, lambda to: wu_cut.at[to], wu_own)
    cols_v = to_group(2, lambda to: vec_all.at[plane, slot], vec_all.at[plane, slot])

    def to_planes(place, ref):
        return [
            push(ref, ref, flat_sent.at[place, turn_at], flat_here.at[place, turn_at], plane=to)
            for turn_at, to in spot.planes()
        ]

    group_rows = n_slice * rows_in
    spread_d = Spread(spot, wd_all, rows_down, spread_sent.at[0], spread_here.at[0])
    spread_q = Spread(spot, wq_all, group_rows, spread_sent.at[1], spread_here.at[1])
    spread_u = Spread(spot, wu_all, group_rows, spread_sent.at[2], spread_here.at[2])
    flat_v = to_planes(0, vec_all.at[plane])
    flat_o = to_planes(1, piece(wo_all, plane, rows_in))
    pos_push = [
        push(
            pos_all.at[shard],
            pos_all.at[shard],
            pos_sent.at[turn_at],
            pos_here.at[turn_at],
            shard=to,
        )
        for turn_at, to in spot.along()
    ]

    raw[6].wait()
    raw[7].wait()
    for copy in cols_v + pos_push:
        copy.start()

    raw[4].wait()
    chain_x.start()
    raw[5].wait()
    chain_dy.start()
    raw[0].wait()
    for to in range(n_slice):
        for part in range(3):
            wq_cut[to, :, part * HD : (part + 1) * HD] = wu_raw[
                :, part * width + to * HD : part * width + (to + 1) * HD
            ].astype(bf16)
    raw[1].start()
    for copy in cols_q:
        copy.start()
    keep_q = pltpu.make_async_copy(wq_cut.at[slot], wq_own, local.at[0])
    keep_q.start()
    for copy in cols_v:
        copy.wait_recv()
    for copy in flat_v:
        copy.start()
    raw[2].wait()

    down_at = plane * rows_down

    @pl.loop(0, rows_down // 32)
    def _(step):
        at = pl.multiple_of(step * 32, 32)
        wd_all[pl.ds(pl.multiple_of(down_at + at, 32), 32), :] = wd_raw[pl.ds(at, 32), :].astype(bf16)

    spread_d.start()
    raw[1].wait()
    for to in range(n_slice):
        for part in range(n_plane):
            wu_cut[to, :, part * rows_down : (part + 1) * rows_down] = wu_raw[
                :, part * width + to * rows_down : part * width + (to + 1) * rows_down
            ].astype(bf16)
    for copy in cols_u:
        copy.start()
    keep_u = pltpu.make_async_copy(wu_cut.at[slot], wu_own, local.at[1])
    keep_u.start()
    raw[3].wait()
    wo_cut[...] = wo_raw[...].astype(bf16)
    head_rows = piece(wo_all, shard, rows_in)
    to_head = push(wo_cut, head_rows, head_sent, head_here, **spot.keeper())
    own_head = pltpu.make_async_copy(wo_cut, head_rows, head_sent)

    @pl.when(spot.head_here)
    def _():
        own_head.start()

    @pl.when(jnp.logical_not(spot.head_here))
    def _():
        to_head.start()

    for copy in pos_push:
        copy.wait_recv()
    freq = freq_ref[...]
    own_blocks = 2 * plane

    @pl.loop(0, n_shard)
    def _(seq):
        for half in range(2):
            at = pl.ds(pl.multiple_of(seq * pair + half * block, block), block)
            cosine, sine, _ = turn_tables(pos_all[seq, pl.ds(own_blocks + half, 1), :], freq)
            cos_row[at, :] = cosine
            sin_row[at, :] = sine

    chain_x.step(1)
    spread_d.relay()
    keep_q.wait()
    for copy in cols_q:
        copy.wait_recv()
    spread_q.start()
    chain_dy.step(1)
    keep_u.wait()
    for copy in cols_u:
        copy.wait_recv()
    spread_u.start()
    chain_x.step(2)

    @pl.when(spot.head_here)
    def _():
        own_head.wait()

    @pl.when(jnp.logical_not(spot.head_here))
    def _():
        to_head.wait_recv()

    for copy in flat_o:
        copy.start()
    chain_dy.step(2)
    spread_q.relay()
    for dist in range(3, n_shard):
        chain_x.step(dist)

    for copy in flat_v:
        copy.wait_recv()
    n_vec, lanes = vec_all.shape[2:]
    lane = lax.broadcasted_iota(jnp.int32, (n_vec, lanes), 1)
    for p in range(n_plane):
        for t in range(0, n_slice, 2):
            at = (p * n_slice + t) * (lanes // 2)
            full_vec[:, at : at + lanes] = jnp.where(
                lane < lanes // 2, vec_all[p, t], pltpu.roll(vec_all[p, t + 1], lanes // 2, 1)
            )
    save_vec = pltpu.make_async_copy(full_vec, vec_out, stores.at[0])
    save_vec.start()

    chain_x.finish_pairs()
    save_x = pltpu.make_async_copy(x_all, x_out, stores.at[1])
    save_x.start()

    def norm_rows(seq):
        @pl.loop(0, pair // 32)
        def _(step):
            at = pl.ds(pl.multiple_of(seq * pair + step * 32, 32), 32)
            tokens = x_all[at, :].astype(f32)
            mean = jnp.mean(tokens, axis=-1, keepdims=True)
            center = tokens - mean
            scale = lax.rsqrt(jnp.mean(center * center, axis=-1, keepdims=True) + 1e-05)
            lane = lax.broadcasted_iota(jnp.int32, (32, moments.shape[1]), 1)
            moments[at, :] = jnp.where(lane < 1, mean, scale)
            hat = center * scale
            one[at, :] = (hat * full_vec[0:1, :] + full_vec[1:2, :]).astype(bf16)
            two[at, :] = (hat * full_vec[2:3, :] + full_vec[3:4, :]).astype(bf16)

    for seq in range(n_shard):
        norm_rows(seq)
        if seq == 1:
            spread_u.relay()
    save_moments = pltpu.make_async_copy(moments, moments_out, stores.at[12])
    save_moments.start()
    save_one = pltpu.make_async_copy(one, one_out, stores.at[2])
    save_one.start()
    save_two = pltpu.make_async_copy(two, two_out, stores.at[3])
    save_two.start()

    spread_q.finish()
    save_wq = pltpu.make_async_copy(wq_all, wq_out, stores.at[4])
    save_wq.start()
    head_lanes = pl.ds(pl.multiple_of(slot * HD, HD), HD)

    def swap(place, source, target, cols, to, turn_at):
        def piece_of(ref, at):
            return ref.at[pl.ds(pl.multiple_of(at * pair, pair), pair), cols]

        return push(
            piece_of(source, to),
            piece_of(target, plane),
            swap_sent.at[place, turn_at - 1],
            swap_here.at[place, turn_at - 1],
            plane=to,
        )

    def keep_own(place, source, target, cols):
        at = pl.ds(pl.multiple_of(plane * pair, pair), pair)
        return pltpu.make_async_copy(source.at[at, cols], target.at[at, cols], local.at[place])

    def swaps(place, source, target, cols):
        return [
            swap(place, source, target, cols, lax.rem(plane + turn_at, n_plane), turn_at)
            for turn_at in range(1, n_plane)
        ]

    qkv_cols = pl.ds(0, 3 * HD)
    q_cols, kv_cols, o_cols = pl.ds(0, HD), pl.ds(HD, 2 * HD), pl.ds(3 * HD, HD)

    for step in range(2):
        at = slice(step * 2 * pair, (step + 1) * 2 * pair)
        heads_now = dot(one[at, :], wq_all[...])
        for part in range(3):
            cols = slice(part * HD, (part + 1) * HD)
            value = heads_now[:, cols] + full_vec[4 + part : 5 + part, head_lanes]
            if part < 2:
                value = turn(value, cos_row[at, :], sin_row[at, :])
            to_heads[at, cols] = value.astype(bf16)
        if step == 0:
            for dist in range(3, n_shard):
                chain_dy.step(dist)

    for copy in swaps(0, to_heads, heads, qkv_cols):
        copy.start()
    keep_qkv = keep_own(2, to_heads, heads, qkv_cols)
    keep_qkv.start()

    @pl.loop(0, n_plane)
    def _(part):
        for half in range(2):
            at = pl.ds(pl.multiple_of(part * pair + half * block, block), block)
            cosine, sine, places = turn_tables(pos_all[plane, pl.ds(2 * part + half, 1), :], freq)
            cos_head[at, :] = cosine
            sin_head[at, :] = sine
            place_head[at, :] = places

    for at in range(pos_all.shape[1]):
        key_row[:, at * block : (at + 1) * block] = pos_all[plane, pl.ds(at, 1), :].astype(f32)

    chain_dy.finish_pairs()
    save_dy = pltpu.make_async_copy(dy_all, dy_out, stores.at[5])
    save_dy.start()
    for copy in flat_o:
        copy.wait_recv()
    save_wo = pltpu.make_async_copy(wo_all, wo_out, stores.at[6])
    save_wo.start()

    @pl.loop(0, 2)
    def _(step):
        at = pl.ds(pl.multiple_of(step * 2 * pair, 2 * pair), 2 * pair)
        to_heads[at, 3 * HD : 4 * HD] = dot(dy_all[at, :], wo_all[...], 1, 1).astype(bf16)

    for copy in swaps(1, to_heads, heads, o_cols):
        copy.start()
    keep_o = keep_own(3, to_heads, heads, o_cols)
    keep_o.start()

    grad_k[...] = jnp.zeros_like(grad_k)
    grad_v[...] = jnp.zeros_like(grad_v)
    scale = HD ** (-0.5)
    keep_qkv.wait()
    for copy in swaps(0, to_heads, heads, qkv_cols):
        copy.wait_recv()

    @pl.loop(0, n_plane)
    def _(part):
        at = pl.ds(pl.multiple_of(part * pair, pair), pair)
        places = place_head[at, 0:1]
        scores = dot(heads[at, 0:HD], heads[:, HD : 2 * HD], 1, 1) * scale
        scores = jnp.where(key_row[...] <= places, scores, -1e30)
        weights = jnp.exp(scores - jnp.max(scores, axis=-1, keepdims=True))
        share = weights / jnp.sum(weights, axis=-1, keepdims=True)
        probs[at, :] = share
        value = dot(share.astype(bf16), heads[:, 2 * HD : 3 * HD])
        attention[at, :] = value
        from_heads[at, 3 * HD : 4 * HD] = value.astype(bf16)

    for copy in swaps(2, from_heads, back, o_cols):
        copy.start()

    keep_o.wait()
    for copy in swaps(1, to_heads, heads, o_cols):
        copy.wait_recv()

    @pl.loop(0, n_plane)
    def _(step):
        turn_at = lax.rem(step + 1, n_plane)
        part = lax.rem(plane + turn_at, n_plane)
        at = pl.ds(pl.multiple_of(part * pair, pair), pair)
        grad_out = heads[at, 3 * HD : 4 * HD]
        delta = jnp.sum(grad_out.astype(f32) * attention[at, :], axis=-1, keepdims=True)
        grad_prob = dot(grad_out, heads[:, 2 * HD : 3 * HD], 1, 1)
        share = probs[at, :]
        dscore = (share * (grad_prob - delta)).astype(bf16)
        grad_q = dot(dscore, heads[:, HD : 2 * HD]) * scale
        from_heads[at, 0:HD] = turn(grad_q, cos_head[at, :], -sin_head[at, :]).astype(bf16)

        @pl.when(turn_at > 0)
        def _():
            swap(3, from_heads, back, q_cols, part, turn_at).start()

        grad_k[...] += dot(dscore, heads[at, 0:HD], 0, 0)
        grad_v[...] += dot(share.astype(bf16), grad_out, 0, 0)

    @pl.loop(0, n_plane)
    def _(step):
        turn_at = lax.rem(step + 1, n_plane)
        part = lax.rem(plane + turn_at, n_plane)
        at = pl.ds(pl.multiple_of(part * pair, pair), pair)
        turned = turn(grad_k[at, :] * scale, cos_head[at, :], -sin_head[at, :])
        from_heads[at, HD : 2 * HD] = turned.astype(bf16)
        from_heads[at, 2 * HD : 3 * HD] = grad_v[at, :].astype(bf16)

        @pl.when(turn_at > 0)
        def _():
            swap(4, from_heads, back, kv_cols, part, turn_at).start()

    keep_back = keep_own(2, from_heads, back, pl.ds(0, 4 * HD))
    keep_back.start()

    spread_u.finish()
    save_wu = pltpu.make_async_copy(wu_all, wu_out, stores.at[8])
    save_wu.start()
    spread_d.finish()
    save_wd = pltpu.make_async_copy(wd_all, wd_out, stores.at[7])
    save_wd.start()
    save_one.wait()
    up_lanes = pl.ds(pl.multiple_of(slot * rows_down, rows_down), rows_down)
    n_hid = n_plane * rows_down

    @pl.loop(0, n_shard)
    def _(step):
        at = pl.ds(pl.multiple_of(step * pair, pair), pair)
        hidden = dot(two[at, :], wu_all[...])
        grad = dot(dy_all[at, :], wd_all[...], 1, 1)
        for part in range(n_plane):
            cols = slice(part * rows_down, (part + 1) * rows_down)
            grad_cols = slice(n_hid + part * rows_down, n_hid + (part + 1) * rows_down)
            value = hidden[:, cols] + full_vec[8 + part : 9 + part, up_lanes]
            half = 0.5 + 0.5 * lax.erf(value * 0.7071067811865476)
            slope = half + value * (0.3989422804014327 * jnp.exp(-0.5 * value * value))
            one[at, cols] = (value * half).astype(bf16)
            one[at, grad_cols] = (grad[:, cols] * slope).astype(bf16)

    save_hid = pltpu.make_async_copy(one.at[:, 0:n_hid], hid_out, stores.at[9])
    save_hid.start()
    save_gup = pltpu.make_async_copy(one.at[:, n_hid : 2 * n_hid], gup_out, stores.at[10])
    save_gup.start()
    keep_back.wait()
    again = (
        swaps(2, from_heads, back, o_cols)
        + swaps(3, from_heads, back, q_cols)
        + swaps(4, from_heads, back, kv_cols)
    )
    for copy in again:
        copy.wait_recv()
    save_back = pltpu.make_async_copy(back, back_out, stores.at[11])
    save_back.start()

    @pl.when(jnp.logical_not(spot.head_here))
    def _():
        to_head.wait_send()

    chain_x.finish_sends()
    chain_dy.finish_sends()
    for copy in cols_q + cols_u + cols_v + pos_push:
        copy.wait_send()
    for spread in [spread_d, spread_q, spread_u]:
        spread.finish_sends()
    again += swaps(0, to_heads, heads, qkv_cols) + swaps(1, to_heads, heads, o_cols)
    for copy in flat_v + flat_o + again:
        copy.wait_send()
    for copy in [
        save_vec,
        save_moments,
        save_x,
        save_two,
        save_wq,
        save_dy,
        save_wo,
        save_wd,
        save_wu,
        save_hid,
        save_gup,
        save_back,
    ]:
        copy.wait()


def forward_all(n_plane, n_shard, x, dy, pos, vec, freq, wq, wu, wd, wo):
    f32, bf16 = jnp.float32, jnp.bfloat16
    n_slice = 2 * n_shard
    block, width = x.shape
    rows_in, rows_down = wq.shape[0], wd.shape[0]
    group = n_slice * block
    n_hid = n_plane * rows_down
    cols_q = 3 * HD
    n_vec, lanes = vec.shape
    dma = pltpu.SemaphoreType.DMA
    vmem = pltpu.VMEM
    shape = jax.ShapeDtypeStruct
    anywhere = pl.BlockSpec(memory_space=pl.ANY)
    far, near = n_shard - 1, n_plane - 1
    return pl.pallas_call(
        partial(forward_kernel, n_plane, n_shard),
        out_shape=[
            shape((group, width), bf16),
            shape((group, width), bf16),
            shape((group, width), bf16),
            shape((group, width), bf16),
            shape((group, n_hid), bf16),
            shape((group, n_hid), bf16),
            shape((group, 4 * HD), bf16),
            shape((width, cols_q), bf16),
            shape((width, n_hid), bf16),
            shape((n_hid, width), bf16),
            shape((HD, width), bf16),
            shape((n_vec, width), f32),
            shape((group, block), f32),
        ],
        in_specs=[anywhere] * 4 + [pl.BlockSpec(memory_space=vmem)] + [anywhere] * 4,
        out_specs=[anywhere] * 13,
        scratch_shapes=[
            vmem((group, width), bf16),
            vmem((group, width), bf16),
            vmem((group, width), bf16),
            vmem((group, width), bf16),
            vmem((width, cols_q), bf16),
            vmem((width, n_hid), bf16),
            vmem((n_hid, width), bf16),
            vmem((HD, width), bf16),
            vmem((n_plane, n_slice, n_vec, lanes), f32),
            vmem((n_shard, *pos.shape), jnp.int32),
            vmem((n_vec, width), f32),
            vmem(wu.shape, f32),
            vmem(wd.shape, f32),
            vmem(wo.shape, f32),
            vmem((n_slice, rows_in, cols_q), bf16),
            vmem((n_slice, rows_in, n_hid), bf16),
            vmem(wo.shape, bf16),
            vmem((group, 4 * HD), bf16),
            vmem((group, 4 * HD), bf16),
            vmem((group, 4 * HD), bf16),
            vmem((group, 4 * HD), bf16),
            vmem((group, HD), f32),
            vmem((group, HD), f32),
            *([vmem((group, block), f32)] * 5),
            vmem((1, group), f32),
            vmem((group, group), f32),
            vmem((group, HD), f32),
            vmem((group, block), f32),
            dma((8,)),
            dma((13,)),
            dma((4,)),
            *([dma((2, n_shard))] * 8),
            dma((far,)),
            dma((far,)),
            dma((3, n_slice - 1)),
            dma((3, n_slice - 1)),
            dma((2, near)),
            dma((2, near)),
            dma((3, 4)),
            dma((3, 4)),
            dma((5, near)),
            dma((5, near)),
            dma,
            dma,
        ],
        compiler_params=pltpu.CompilerParams(
            collective_id=0, has_side_effects=True, vmem_limit_bytes=VMEM_BYTES
        ),
        name="forward_all",
    )(x, dy, pos, vec, freq, wq, wu, wd, wo)


def add_rows(target, terms, rows):
    columns = target.shape[1]
    chunk = min(rows, 64 if columns <= 1024 else 32)

    @pl.loop(0, rows // chunk)
    def _(step):
        at = pl.ds(pl.multiple_of(step * chunk, chunk), chunk)
        for start in range(0, columns, 256):
            cols = slice(start, start + 256)
            total = terms[0][at, cols].astype(jnp.float32)
            for term in terms[1:]:
                total = total + term[at, cols].astype(jnp.float32)
            target[at, cols] = total.astype(target.dtype)


def backward_kernel(
    n_plane,
    n_shard,
    hat_ref,
    du_ref,
    gains_ref,
    dy_ref,
    one_ref,
    hid_ref,
    gup_ref,
    back_ref,
    wd_ref,
    wo_ref,
    out_sum,
    hat_sum,
    dq_sum,
    du_sum,
    dd_sum,
    do_sum,
    vec_sum,
    big_one,
    big_two,
    big_three,
    hid,
    gup,
    back,
    wo,
    rows_part,
    other_half,
    theirs,
    parts,
    q_part,
    u_part,
    o_part,
    v_part,
    gains,
    q_in,
    u_in,
    d_in,
    o_in,
    v_in,
    o_mid,
    v_mid,
    v_end,
    loads,
    local,
    pair_sent,
    pair_here,
    rows_sent,
    rows_here,
    flat_sent,
    flat_here,
    sum_sent,
    sum_here,
    cols_sent,
    cols_here,
    head_sent,
    head_here,
):
    spot = Spot(n_plane, n_shard)
    plane, core, shard, slot = spot.plane, spot.core, spot.shard, spot.slot
    f32, bf16 = jnp.float32, jnp.bfloat16
    n_slice = 2 * n_shard
    n_group, width = dy_ref.shape
    block = n_group // n_slice
    pair = 2 * block
    rows_down = width // n_slice
    cols_q = 3 * HD
    n_hid = hid_ref.shape[1]
    rows_plane = width // n_plane
    rows_in = rows_plane // n_slice

    def load(source, target, place):
        copy = pltpu.make_async_copy(source, target, loads.at[place])
        copy.start()
        return copy

    load_u = load(du_ref, u_part, 0)
    load_hat = load(hat_ref.at[:, core], rows_part.at[1], 1)
    load_back = load(back_ref, back, 2)
    load_hid = load(hid_ref, hid, 3)
    load_wo = load(wo_ref, wo, 4)
    load_wd = load(wd_ref, big_two, 5)
    load_one = load(one_ref, big_three, 6)
    load_dy = load(dy_ref, big_one, 7)
    load_gup = load(gup_ref, gup, 8)
    load_gains = load(gains_ref, gains, 9)
    spot.greet(spot.keeper())

    def flat(place, source, target):
        return [
            push(
                source(to),
                target.at[turn_at],
                flat_sent.at[place, turn_at],
                flat_here.at[place, turn_at],
                plane=to,
            )
            for turn_at, to in spot.planes()
        ]

    def at_plane(ref, size):
        return lambda to: ref.at[pl.ds(pl.multiple_of(to * size, size), size)]

    sum_u = Gather(spot, u_part, rows_plane, u_in, sum_sent.at[0], sum_here.at[0])
    sum_q = Gather(spot, q_part, rows_plane, q_in, sum_sent.at[1], sum_here.at[1])
    sum_d = Gather(spot, big_two, rows_down, d_in, sum_sent.at[2], sum_here.at[2])
    flat_o = flat(0, at_plane(o_part, rows_in), o_in)
    flat_v = flat(
        1,
        lambda to: v_part.at[:, pl.ds(pl.multiple_of(to * rows_plane, rows_plane), rows_plane)],
        v_in,
    )

    def weight_grad(left, right, target, columns):
        @pl.loop(0, left.shape[1] // 512)
        def _(step):
            at = pl.ds(pl.multiple_of(step * 512, 512), 512)
            turned = left[:, at].T
            for start in range(0, columns, n_group):
                cols = slice(start, min(start + n_group, columns))
                target[at, cols] = dot(turned, right[:, cols]).astype(bf16)

    sums = [
        RowSum(spot, rows_part.at[place], parts.at[place], rows_sent.at[place], rows_here.at[place])
        for place in range(2)
    ]

    pair_hat = push(
        hat_ref.at[:, 1 - core], theirs.at[1], pair_sent.at[1, 0], pair_here.at[1, 0], core=1 - core
    )

    def pair_out(seq):
        return push(
            other_half.at[seq],
            theirs.at[0, seq],
            pair_sent.at[0, seq],
            pair_here.at[0, seq],
            core=1 - core,
        )

    def add_pairs(place):
        @pl.loop(0, n_shard)
        def _(seq):
            if place == 0:
                pair_out(seq).wait_recv()
            held = rows_part.at[place, seq]
            add_rows(held, [held, theirs.at[place, seq]], block)

        sums[place].start()

    def add_shards(place, target):
        sums[place].finish(sums[place].rows(shard))
        copy = pltpu.make_async_copy(sums[place].rows(shard), target, local.at[2, 1 + place])
        copy.start()
        return copy

    def regroup(place, held, target, wide):
        base = pl.multiple_of(plane * rows_plane, rows_plane)
        parts_here = held.shape[1] // wide

        def rows(to, part):
            start = pl.multiple_of(base + to * rows_in, rows_in)
            return held.at[pl.ds(start, rows_in), pl.ds(part * wide, wide)]

        def lands(part):
            start = pl.multiple_of(part * width + slot * wide, wide)
            return target.at[:, pl.ds(start, wide)]

        copies = []
        for turn_at, device in spot.group():
            to = device["core"] * n_shard + device["shard"]
            for part in range(parts_here):
                copies.append(
                    push(
                        rows(to, part),
                        lands(part),
                        cols_sent.at[place, turn_at, part],
                        cols_here.at[place, turn_at, part],
                        **device,
                    )
                )
        keeps = [
            pltpu.make_async_copy(rows(slot, part), lands(part), local.at[place, part])
            for part in range(parts_here)
        ]
        for copy in copies + keeps:
            copy.start()
        return copies, keeps

    load_u.wait()
    sum_u.start()
    pair_hat.start()
    load_hat.wait()
    pair_hat.wait_recv()
    add_pairs(1)

    load_back.wait()
    load_hid.wait()
    load_wo.wait()
    load_wd.wait()

    @pl.loop(0, n_shard)
    def _(seq):
        at = pl.ds(pl.multiple_of(seq * pair, pair), pair)
        for start in range(0, width, n_group):
            cols = slice(start, start + n_group)
            total = dot(back[at, cols_q : cols_q + HD], wo[:, cols]) + dot(
                hid[at, :], big_two[:, cols]
            )
            first, second = total[:block], total[block:]
            rows_part[0, seq, :, cols] = jnp.where(core == 0, first, second).astype(bf16)
            other_half[seq, :, cols] = jnp.where(core == 0, second, first).astype(bf16)
        pair_out(seq).start()

    add_pairs(0)
    sums[1].relay(1)
    sum_u.relay()

    load_one.wait()
    weight_grad(big_three, back, q_part, cols_q)
    sum_q.start()
    sums[1].relay(2)
    sum_u.finish()
    cols_u, keep_u = regroup(0, u_part, du_sum, rows_down)
    sums[0].relay(1)

    load_dy.wait()
    weight_grad(hid, big_one, big_two, width)
    attn = back[:, cols_q : cols_q + HD]
    half = width // 2
    for part in range(2):
        cols = slice(part * half, (part + 1) * half)
        o_part[:, cols] = dot(attn, big_one[:, cols], 0, 0).astype(bf16)
    for copy in flat_o:
        copy.start()
    sum_q.relay()
    sum_d.start()
    sums[0].relay(2)

    v_part[...] = jnp.zeros_like(v_part)
    load_gains.wait()
    load_gup.wait()
    v_part[0:4, :] = gains[0:4, :]
    own = pl.ds(pl.multiple_of((shard * 2 + core) * block, block), block)
    column_out = jnp.sum(big_one[own, :].astype(f32), axis=0, keepdims=True)
    v_part[7:8, :] = column_out
    v_part[12:13, :] = column_out
    lanes = pl.ds(pl.multiple_of(slot * HD, HD), HD)
    for part in range(3):
        cols = slice(part * HD, (part + 1) * HD)
        v_part[4 + part : 5 + part, lanes] = jnp.sum(
            back[:, cols].astype(f32), axis=0, keepdims=True
        )
    lanes = pl.ds(pl.multiple_of(slot * rows_down, rows_down), rows_down)
    for part in range(n_plane):
        cols = slice(part * rows_down, (part + 1) * rows_down)
        v_part[8 + part : 9 + part, lanes] = jnp.sum(
            gup[:, cols].astype(f32), axis=0, keepdims=True
        )
    for copy in flat_v:
        copy.start()
    sum_q.finish()
    cols_q_copies, keep_q = regroup(1, q_part, dq_sum, HD)
    save_out = add_shards(1, hat_sum)
    sum_d.relay()

    for copy in flat_o:
        copy.wait_recv()
    mine = o_part.at[pl.ds(pl.multiple_of(plane * rows_in, rows_in), rows_in)]
    add_rows(o_mid, [mine] + [o_in.at[turn_at] for turn_at in range(n_plane - 1)], rows_in)
    to_owner = push(
        o_mid,
        do_sum,
        head_sent,
        head_here,
        plane=spot.owner_plane,
        core=spot.owner_core,
        shard=plane,
    )
    own_rows = pltpu.make_async_copy(o_mid, do_sum, head_sent)

    @pl.when(spot.head_here)
    def _():
        own_rows.start()

    @pl.when(jnp.logical_not(spot.head_here))
    def _():
        to_owner.start()

    for copy in flat_v:
        copy.wait_recv()
    total = v_part[:, pl.ds(pl.multiple_of(plane * rows_plane, rows_plane), rows_plane)]
    for turn_at in range(n_plane - 1):
        total = total + v_in[turn_at]
    v_mid[...] = total
    wide = 2 * rows_in

    def lanes_of(device):
        half_slot = device["core"] * n_shard + device["shard"]
        return pl.ds(pl.multiple_of(lax.div(half_slot, 2) * wide, wide), wide)

    v_end[slot] = v_mid[:, lanes_of(spot.turned(0))]
    cols_v = []
    for turn_at, device in spot.group():
        cols_v.append(
            push(
                v_mid.at[:, lanes_of(device)],
                v_end.at[slot],
                cols_sent.at[2, turn_at, 0],
                cols_here.at[2, turn_at, 0],
                **device,
            )
        )
    for copy in cols_v:
        copy.start()

    save_sums = [save_out, add_shards(0, out_sum)]
    sum_d.finish()
    save_d = pltpu.make_async_copy(sum_d.own(), dd_sum, local.at[2, 0])
    save_d.start()
    for copy in cols_v:
        copy.wait_recv()
    total = v_end[0]
    for other in range(1, n_slice):
        total = total + v_end[other]
    odd = lax.rem(slot, 2) == 1
    vec_sum[...] = jnp.where(odd, pltpu.roll(total, rows_in, 1), total)

    for copy in keep_u + keep_q:
        copy.wait()
    for copy in cols_u + cols_q_copies:
        copy.wait_recv()

    @pl.when(spot.head_here)
    def _():
        own_rows.wait()

    @pl.when(jnp.logical_not(spot.head_here))
    def _():
        to_owner.wait_recv()
        to_owner.wait_send()

    pair_hat.wait_send()
    for seq in range(n_shard):
        pair_out(seq).wait_send()
    for place in range(2):
        sums[place].finish_sends()
    for copy in save_sums + [save_d]:
        copy.wait()
    for total in [sum_u, sum_q, sum_d]:
        total.finish_sends()
    for copy in flat_o + flat_v + cols_u + cols_q_copies + cols_v:
        copy.wait_send()


def backward_all(n_plane, n_shard, *arrays):
    hat, du, gains, dy, one, hid, gup, back, wd, wo = arrays
    f32, bf16 = jnp.float32, jnp.bfloat16
    n_slice = 2 * n_shard
    group, width = dy.shape
    block = group // n_slice
    rows_down = width // n_slice
    rows_plane = width // n_plane
    rows_in = rows_plane // n_slice
    cols_q, n_hid = 3 * HD, hid.shape[1]
    n_vec = 16
    dma = pltpu.SemaphoreType.DMA
    vmem = pltpu.VMEM
    shape = jax.ShapeDtypeStruct
    near = n_plane - 1
    inside = pl.BlockSpec(memory_space=vmem)
    anywhere = pl.BlockSpec(memory_space=pl.ANY)
    return pl.pallas_call(
        partial(backward_kernel, n_plane, n_shard),
        out_shape=[
            shape((block, width), bf16),
            shape((block, width), bf16),
            shape((rows_in, n_slice * cols_q), bf16),
            shape((rows_in, n_slice * n_hid), bf16),
            shape((rows_down, width), bf16),
            shape((rows_in, width), bf16),
            shape((n_vec, 2 * rows_in), f32),
        ],
        in_specs=[anywhere] * 10,
        out_specs=[anywhere] * 6 + [inside],
        scratch_shapes=[
            vmem((group, width), bf16),
            vmem((group, width), bf16),
            vmem((group, width), bf16),
            vmem(hid.shape, bf16),
            vmem(hid.shape, bf16),
            vmem(back.shape, bf16),
            vmem(wo.shape, bf16),
            vmem((2, n_shard, block, width), bf16),
            vmem((n_shard, block, width), bf16),
            vmem((2, n_shard, block, width), bf16),
            vmem((2, n_shard + 1, block, width), bf16),
            vmem((width, cols_q), bf16),
            vmem((width, n_hid), bf16),
            vmem(wo.shape, bf16),
            vmem((n_vec, width), f32),
            vmem(gains.shape, f32),
            vmem((6, rows_plane // 2, cols_q), bf16),
            vmem((6, rows_plane // 2, n_hid), bf16),
            vmem((6, rows_down // 2, width), bf16),
            vmem((near, rows_in, width), bf16),
            vmem((near, n_vec, rows_plane), f32),
            vmem((rows_in, width), bf16),
            vmem((n_vec, rows_plane), f32),
            vmem((n_slice, n_vec, 2 * rows_in), f32),
            dma((10,)),
            dma((3, n_plane)),
            dma((2, n_shard)),
            dma((2, n_shard)),
            dma((2, 2, n_shard)),
            dma((2, 2, n_shard)),
            dma((2, near)),
            dma((2, near)),
            dma((3, 6)),
            dma((3, 6)),
            dma((3, n_slice - 1, n_plane)),
            dma((3, n_slice - 1, n_plane)),
            dma,
            dma,
        ],
        compiler_params=pltpu.CompilerParams(
            collective_id=1, has_side_effects=True, vmem_limit_bytes=VMEM_BYTES
        ),
        name="backward_all",
    )(*arrays)


def fast_device(
    layer_input,
    out_grad,
    positions,
    w_qkv,
    w_dense,
    w_up,
    w_down,
    vectors,
    m_qkv,
    m_dense,
    m_up,
    m_down,
    m_vectors,
    v_qkv,
    v_dense,
    v_up,
    v_down,
    v_vectors,
):
    bf16 = jnp.bfloat16
    f32 = jnp.float32
    n_plane = lax.axis_size("plane")
    n_shard = lax.axis_size("shard")
    block_rows = layer_input.shape[1]
    n_vec, vec_cols = vectors.shape

    half_rot = ROT // 2
    inverse = 10000.0 ** (-jnp.arange(0, ROT, 2).astype(f32) / ROT)
    freq = jnp.pad(jnp.concatenate([inverse, inverse]), (0, 128 - 2 * half_rot))[None]
    kept = forward_all(
        n_plane,
        n_shard,
        layer_input[0],
        out_grad[0],
        positions.reshape(-1, block_rows),
        jnp.pad(vectors, ((0, 16 - n_vec), (0, 128 - vec_cols))),
        freq,
        w_qkv,
        w_up,
        w_down,
        w_dense,
    )
    x_all, dy_all, one_all, two_all, hid_all, gup_all, heads_back = kept[:7]
    wq_all, wu_all, wd_all, wo_all, full_vec, moments = kept[7:]
    xhat = (x_all.astype(f32) - moments[:, 0:1]) * moments[:, 1:2]
    norm_one_part = lax.dot_general(
        heads_back[:, : 3 * HD], wq_all, (((1,), (1,)), ((), ())), preferred_element_type=f32
    )
    norm_two_part = lax.dot_general(
        gup_all, wu_all, (((1,), (1,)), ((), ())), preferred_element_type=f32
    )
    gains = jnp.stack(
        [
            jnp.sum(norm_one_part * xhat, axis=0),
            jnp.sum(norm_one_part, axis=0),
            jnp.sum(norm_two_part * xhat, axis=0),
            jnp.sum(norm_two_part, axis=0),
        ]
    )
    hat_part = (norm_one_part * full_vec[0] + norm_two_part * full_vec[2]).astype(bf16)
    up_part = lax.dot_general(
        two_all, gup_all, (((0,), (0,)), ((), ())), preferred_element_type=f32
    ).astype(bf16)
    width = x_all.shape[1]
    branches, grad_hat, part_qkv, part_up, part_down, part_dense, part_vec = backward_all(
        n_plane,
        n_shard,
        hat_part.reshape(n_shard, 2, block_rows, width),
        up_part,
        jnp.pad(gains, ((0, 4), (0, 0))),
        dy_all,
        one_all,
        hid_all,
        gup_all,
        heads_back,
        wd_all,
        wo_all,
    )
    branches = branches.astype(f32)
    grad_hat = grad_hat.astype(f32)
    own_tokens = layer_input[0].astype(f32)
    grad_rows = out_grad[0].astype(f32)
    layer_output = (own_tokens + branches + full_vec[7] + full_vec[12]).astype(bf16)[None]
    own_center = own_tokens - jnp.mean(own_tokens, axis=-1, keepdims=True)
    own_inv = lax.rsqrt(jnp.mean(own_center * own_center, axis=-1, keepdims=True) + 1e-05)
    own_hat = own_center * own_inv
    grad_input = (
        grad_rows
        + own_inv
        * (
            grad_hat
            - jnp.mean(grad_hat, axis=-1, keepdims=True)
            - own_hat * jnp.mean(grad_hat * own_hat, axis=-1, keepdims=True)
        )
    )[None]
    grad_vectors = part_vec[:n_vec, :vec_cols]
    grad_dense = part_dense.astype(f32)
    grad_down = part_down.astype(f32)
    grad_qkv = part_qkv.astype(f32)
    grad_up = part_up.astype(f32)
    new_qkv, second_qkv = adam_step(w_qkv, grad_qkv, m_qkv, v_qkv, 4.0 * (D // 2) ** (-0.5), 0.1)
    new_dense, second_dense = adam_step(
        w_dense, grad_dense, m_dense, v_dense, 4.0 * (D // 32) ** (-0.5), 0.1
    )
    new_up, second_up = adam_step(w_up, grad_up, m_up, v_up, 4.0 * D ** (-0.5), 0.1)
    new_down, second_down = adam_step(w_down, grad_down, m_down, v_down, 4.0 * FF ** (-0.5), 0.1)
    new_vectors, second_vectors = adam_step(vectors, grad_vectors, m_vectors, v_vectors, 1.0, 0.0)
    return (
        layer_output,
        grad_input,
        grad_qkv,
        grad_dense,
        grad_up,
        grad_down,
        grad_vectors,
        second_qkv,
        second_dense,
        second_up,
        second_down,
        second_vectors,
        new_qkv,
        new_dense,
        new_up,
        new_down,
        new_vectors,
    )


def solution(mesh):
    n_ctx, n_shard = mesh.devices.shape
    if n_ctx == 2 * n_shard and n_ctx == H:
        device_mesh = Mesh(
            mesh.devices.reshape(n_shard, 2, n_shard), ("plane", "core", "shard")
        )
        ctx, body = ("plane", "core"), fast_device
    else:
        device_mesh, ctx, body = mesh, ("ctx",), general_device
    rows = P("shard", ctx, None)
    weight = P((*ctx, "shard"), None)
    vector = P(None, (*ctx, "shard"))
    matrices = (weight,) * 4 + (vector,)
    in_specs = (rows, rows, P("shard", None)) + matrices * 3
    out_specs = (rows, rows) + matrices * 3
    return jax.shard_map(
        body, mesh=device_mesh, in_specs=in_specs, out_specs=out_specs, check_vma=False
    )
```

```python
from functools import partial

import jax
import jax.numpy as jnp
from jax import lax
from jax.experimental import pallas as pl
from jax.experimental.pallas import tpu as pltpu
from jax.sharding import Mesh, PartitionSpec as P

D = 2048
H = 8
HD = 256
ROT = 64
FF = 8192
STEP = 10


def from_behind(value, axis, steps):
    count = lax.axis_size(axis)
    pairs = [(source, (source + steps) % count) for source in range(count)]
    return lax.ppermute(value, axis, pairs)


def layer_norm(values, gain, shift):
    center = values - jnp.mean(values, axis=-1, keepdims=True)
    spread = jnp.mean(center * center, axis=-1, keepdims=True)
    return center * lax.rsqrt(spread + 1e-05) * gain + shift


def angles(places):
    inverse = 10000.0 ** (-jnp.arange(0, ROT, 2).astype(jnp.float32) / ROT)
    phases = places.astype(jnp.float32)[:, None] * inverse[None, :]
    return (jnp.cos(phases), jnp.sin(phases))


def rotate(values, cosine, sine):
    half_rot = cosine.shape[-1]
    front = values[..., :half_rot]
    second = values[..., half_rot : 2 * half_rot]
    others = values[..., 2 * half_rot :]
    cos_b = cosine[:, None, :]
    sin_b = sine[:, None, :]
    return jnp.concatenate(
        [front * cos_b - second * sin_b, second * cos_b + front * sin_b, others], axis=-1
    )


def adam_step(weight, gradient, moment, second, rate, decay):
    moment = 0.9 * moment + 0.1 * gradient
    second = 0.95 * second + 0.05 * gradient * gradient
    unbiased = moment / (1.0 - 0.9**STEP)
    scaled = second / (1.0 - 0.95**STEP)
    return (weight - rate * (unbiased / (jnp.sqrt(scaled) + 1e-08) + decay * weight), second)


def general_device(
    layer_input,
    out_grad,
    positions,
    w_qkv,
    w_dense,
    w_up,
    w_down,
    vectors,
    m_qkv,
    m_dense,
    m_up,
    m_down,
    m_vectors,
    v_qkv,
    v_dense,
    v_up,
    v_down,
    v_vectors,
):
    block_rows = layer_input.shape[1]
    model_width = layer_input.shape[2]
    hidden = w_up.shape[1]
    rows_in = w_qkv.shape[0]
    rows_down = w_down.shape[0]
    n_ctx = lax.axis_size("ctx")
    score_scale = HD ** (-0.5)
    ctx_index = lax.axis_index("ctx")
    all_pos = positions[0]
    own_pos = lax.dynamic_slice_in_dim(all_pos, ctx_index * block_rows, block_rows)
    last_own = jnp.max(own_pos)
    cosine, sine = angles(own_pos)
    full_vec = lax.all_gather(vectors, ("ctx", "shard"), axis=1, tiled=True)
    tokens = layer_input[0].astype(jnp.float32)
    normed_one = layer_norm(tokens, full_vec[0], full_vec[1]).astype(jnp.bfloat16)
    normed_two = layer_norm(tokens, full_vec[2], full_vec[3]).astype(jnp.bfloat16)
    qkv_low = w_qkv.astype(jnp.bfloat16)
    dense_low = w_dense.astype(jnp.bfloat16)
    up_low = w_up.astype(jnp.bfloat16)
    down_low = w_down.astype(jnp.bfloat16)
    grad_low = out_grad[0]
    grad_rows = grad_low.astype(jnp.float32)
    pieces = (
        lax.all_gather(qkv_low, ("ctx", "shard"), axis=0, tiled=True),
        lax.all_gather(up_low, ("ctx", "shard"), axis=0, tiled=True),
    )
    left_one = normed_one
    left_two = normed_two
    proj_sum = jnp.dot(left_one, pieces[0], preferred_element_type=jnp.float32)
    up_sum = jnp.dot(left_two, pieces[1], preferred_element_type=jnp.float32)
    projection = proj_sum + full_vec[4:7].reshape(-1)
    up_value = up_sum + full_vec[8:12].reshape(-1)
    queries = projection[:, :model_width].reshape(block_rows, H, HD)
    keys_raw = projection[:, model_width : 2 * model_width].reshape(block_rows, H, HD)
    values_raw = projection[:, 2 * model_width :].reshape(block_rows, H, HD)
    q_rot = rotate(queries, cosine, sine).astype(jnp.bfloat16)
    k_rot = rotate(keys_raw, cosine, sine).astype(jnp.bfloat16)
    v_low = values_raw.astype(jnp.bfloat16)
    start_state = (
        jnp.full((block_rows, H), -1e30, jnp.float32),
        jnp.zeros((block_rows, H), jnp.float32),
        jnp.zeros((block_rows, H, HD), jnp.float32),
    )
    pieces = (
        lax.all_gather(k_rot, "ctx", axis=0, tiled=True),
        lax.all_gather(v_low, "ctx", axis=0, tiled=True),
    )
    key_pos = all_pos
    allowed = (key_pos[None, :] <= own_pos[:, None])[:, None, :]

    def attend_compute(states):
        running_top, totals, accum = states
        scores = (
            jnp.einsum("qhd,khd->qhk", q_rot, pieces[0], preferred_element_type=jnp.float32)
            * score_scale
        )
        scores = jnp.where(allowed, scores, -1e30)
        new_top = jnp.maximum(running_top, jnp.max(scores, axis=-1))
        weights = jnp.where(allowed, jnp.exp(scores - new_top[..., None]), 0.0)
        totals = jnp.sum(weights, axis=-1)
        accum = jnp.einsum(
            "qhk,khd->qhd",
            weights.astype(jnp.bfloat16),
            pieces[1],
            preferred_element_type=jnp.float32,
        )
        return (new_top, totals, accum)

    skipped = jnp.min(key_pos) > last_own
    running_top, totals, accum = lax.cond(
        skipped, lambda states: states, attend_compute, start_state
    )
    attention = accum / totals[..., None]
    log_sum = running_top + jnp.log(totals)
    attn_low = attention.reshape(block_rows, model_width).astype(jnp.bfloat16)
    gelu_exact = partial(jax.nn.gelu, approximate=False)
    hid_low = gelu_exact(up_value).astype(jnp.bfloat16)
    add_pieces = (
        lax.all_gather(dense_low, ("ctx", "shard"), axis=0, tiled=True),
        lax.all_gather(down_low, ("ctx", "shard"), axis=0, tiled=True),
    )
    second_count = add_pieces[1].shape[0]
    second_begin = jnp.int32(0) // rows_in * rows_down
    left_attn = attn_low
    left_hid = lax.dynamic_slice_in_dim(hid_low, second_begin, second_count, 1)
    branches = jnp.dot(left_attn, add_pieces[0], preferred_element_type=jnp.float32) + jnp.dot(
        left_hid, add_pieces[1], preferred_element_type=jnp.float32
    )
    back_pieces = lax.all_gather((dense_low, down_low), ("ctx", "shard"), axis=0, tiled=True)
    shard_count = back_pieces[0].shape[0] // rows_in
    first_part = jnp.einsum(
        "td,rd->tr", grad_low, back_pieces[0], preferred_element_type=jnp.float32
    ).reshape(block_rows, shard_count, rows_in)
    second_part = jnp.einsum(
        "td,rd->tr", grad_low, back_pieces[1], preferred_element_type=jnp.float32
    ).reshape(block_rows, shard_count, rows_down)
    merged_out = jnp.concatenate([first_part, second_part], axis=2).reshape(
        block_rows, shard_count * (rows_in + rows_down)
    )
    merged_out = merged_out.reshape(block_rows, -1, rows_in + rows_down)
    grad_attn = merged_out[:, :, :rows_in].reshape(block_rows, model_width)
    grad_hid = merged_out[:, :, rows_in:].reshape(block_rows, hidden)
    layer_output = (tokens + branches + full_vec[7] + full_vec[12]).astype(jnp.bfloat16)[None]
    gelu_pull = jax.vjp(gelu_exact, up_value)[1]
    grad_upval = gelu_pull(grad_hid)[0].astype(jnp.bfloat16)
    grad_heads = grad_attn.astype(jnp.bfloat16).reshape(block_rows, H, HD)
    delta_rows = jnp.sum(grad_heads.astype(jnp.float32) * attention, axis=-1)

    def key_turn(turn_index, states):
        pair_now, pair_grad, query_grad = states
        owner_index = (ctx_index - turn_index) % n_ctx
        key_pos = lax.dynamic_slice_in_dim(all_pos, owner_index * block_rows, block_rows)
        allowed = (key_pos[None, :] <= own_pos[:, None])[:, None, :]

        def key_compute(partials):
            grads_held, query_held = partials
            scores = (
                jnp.einsum("qhd,khd->qhk", q_rot, pair_now[0], preferred_element_type=jnp.float32)
                * score_scale
            )
            weights_now = jnp.where(allowed, jnp.exp(scores - log_sum[..., None]), 0.0)
            grad_prob = jnp.einsum(
                "qhd,khd->qhk", grad_heads, pair_now[1], preferred_element_type=jnp.float32
            )
            dscore = (weights_now * (grad_prob - delta_rows[..., None])).astype(jnp.bfloat16)
            query_held = (
                query_held
                + jnp.einsum(
                    "qhk,khd->qhd", dscore, pair_now[0], preferred_element_type=jnp.float32
                )
                * score_scale
            )
            key_term = (
                jnp.einsum("qhk,qhd->khd", dscore, q_rot, preferred_element_type=jnp.float32)
                * score_scale
            )
            value_term = jnp.einsum(
                "qhk,qhd->khd",
                weights_now.astype(jnp.bfloat16),
                grad_heads,
                preferred_element_type=jnp.float32,
            )
            return (grads_held + jnp.stack([key_term, value_term]), query_held)

        skipped = jnp.min(key_pos) > last_own
        pair_grad, query_grad = lax.cond(
            skipped, lambda partials: partials, key_compute, (pair_grad, query_grad)
        )
        pair_now = from_behind(pair_now, "ctx", 1)
        pair_grad = from_behind(pair_grad.astype(jnp.bfloat16), "ctx", 1).astype(pair_grad.dtype)
        return (pair_now, pair_grad, query_grad)

    loop_start = (
        jnp.stack([k_rot, v_low]),
        jnp.zeros((2, block_rows, H, HD), jnp.float32),
        jnp.zeros((block_rows, H, HD), jnp.float32),
    )
    loop_end = lax.fori_loop(0, n_ctx, key_turn, loop_start)
    pair_grad = loop_end[1]
    query_grad = loop_end[2]

    def turn_values(values):
        return rotate(values, cosine, sine)

    rot_pull = jax.vjp(turn_values, queries)[1]
    grad_proj = jnp.concatenate(
        [
            rot_pull(query_grad)[0].reshape(block_rows, model_width),
            rot_pull(pair_grad[0])[0].reshape(block_rows, model_width),
            pair_grad[1].reshape(block_rows, model_width),
        ],
        axis=1,
    ).astype(jnp.bfloat16)

    def back_inputs(pieces):
        shard_count = pieces[0].shape[0] // rows_in
        first_part = jnp.einsum(
            "tc,rc->tr", grad_proj, pieces[0], preferred_element_type=jnp.float32
        ).reshape(block_rows, shard_count, 1, rows_in)
        second_part = jnp.einsum(
            "tc,rc->tr", grad_upval, pieces[1], preferred_element_type=jnp.float32
        ).reshape(block_rows, shard_count, 1, rows_in)
        return jnp.concatenate([first_part, second_part], axis=2).reshape(
            block_rows, shard_count * 2 * rows_in
        )

    merged_in = back_inputs(lax.all_gather((qkv_low, up_low), ("ctx", "shard"), axis=0, tiled=True))
    merged_in = merged_in.reshape(block_rows, -1, 2, rows_in)
    grad_norm_one = merged_in[:, :, 0].reshape(block_rows, model_width)
    grad_norm_two = merged_in[:, :, 1].reshape(block_rows, model_width)
    norm_pull_one = jax.vjp(layer_norm, tokens, full_vec[0], full_vec[1])[1]
    norm_pull_two = jax.vjp(layer_norm, tokens, full_vec[2], full_vec[3])[1]
    back_one, gain_one, shift_one = norm_pull_one(grad_norm_one)
    back_two, gain_two, shift_two = norm_pull_two(grad_norm_two)
    grad_input = (grad_rows + back_one + back_two)[None]
    column_out = jnp.sum(grad_rows, axis=0)
    vector_terms = jnp.concatenate(
        [
            jnp.stack([gain_one, shift_one, gain_two, shift_two]),
            jnp.sum(grad_proj.astype(jnp.float32), axis=0).reshape(3, model_width),
            column_out[None],
            jnp.sum(grad_upval.astype(jnp.float32), axis=0).reshape(4, model_width),
            column_out[None],
        ],
        axis=0,
    )
    grad_vectors = lax.psum_scatter(vector_terms, ("ctx", "shard"), scatter_dimension=1, tiled=True)
    block_count = (rows_in + rows_down) * lax.axis_size(("ctx", "shard")) // (rows_in + rows_down)
    first_block = jnp.int32(0) // (rows_in + rows_down)
    left_attn = attn_low
    left_hid = lax.dynamic_slice_in_dim(
        hid_low, first_block * rows_down, block_count * rows_down, 1
    )
    dense_part = jnp.einsum(
        "tr,td->rd", left_attn, grad_low, preferred_element_type=jnp.float32
    ).reshape(block_count, rows_in, model_width)
    down_part = jnp.einsum(
        "tr,td->rd", left_hid, grad_low, preferred_element_type=jnp.float32
    ).reshape(block_count, rows_down, model_width)
    out_grads = lax.psum_scatter(
        jnp.concatenate([dense_part, down_part], axis=1).reshape(
            (rows_in + rows_down) * lax.axis_size(("ctx", "shard")), model_width
        ),
        ("ctx", "shard"),
        scatter_dimension=0,
        tiled=True,
    )
    left_one = normed_one
    left_two = normed_two
    in_grads = lax.psum_scatter(
        jnp.concatenate(
            [
                jnp.einsum("tr,tc->rc", left_one, grad_proj, preferred_element_type=jnp.float32),
                jnp.einsum("tr,tc->rc", left_two, grad_upval, preferred_element_type=jnp.float32),
            ],
            axis=1,
        ),
        ("ctx", "shard"),
        scatter_dimension=0,
        tiled=True,
    )
    grad_qkv = in_grads[:, : 3 * model_width]
    grad_up = in_grads[:, 3 * model_width :]
    grad_dense = out_grads[:rows_in]
    grad_down = out_grads[rows_in:]
    new_qkv, second_qkv = adam_step(w_qkv, grad_qkv, m_qkv, v_qkv, 4.0 * (D // 2) ** (-0.5), 0.1)
    new_dense, second_dense = adam_step(
        w_dense, grad_dense, m_dense, v_dense, 4.0 * (D // 32) ** (-0.5), 0.1
    )
    new_up, second_up = adam_step(w_up, grad_up, m_up, v_up, 4.0 * D ** (-0.5), 0.1)
    new_down, second_down = adam_step(w_down, grad_down, m_down, v_down, 4.0 * FF ** (-0.5), 0.1)
    new_vectors, second_vectors = adam_step(vectors, grad_vectors, m_vectors, v_vectors, 1.0, 0.0)
    return (
        layer_output,
        grad_input,
        grad_qkv,
        grad_dense,
        grad_up,
        grad_down,
        grad_vectors,
        second_qkv,
        second_dense,
        second_up,
        second_down,
        second_vectors,
        new_qkv,
        new_dense,
        new_up,
        new_down,
        new_vectors,
    )


MESH = pl.DeviceIdType.MESH
VMEM_BYTES = 62 * 1024 * 1024


def push(source, target, sent, arrived, **device):
    return pltpu.make_async_remote_copy(
        src_ref=source,
        dst_ref=target,
        send_sem=sent,
        recv_sem=arrived,
        device_id=device,
        device_id_type=MESH,
    )


class Spot:
    def __init__(self, n_plane, n_shard):
        self.n_plane, self.n_shard = n_plane, n_shard
        self.plane = lax.axis_index("plane")
        self.core = lax.axis_index("core")
        self.shard = lax.axis_index("shard")
        self.slot = self.core * n_shard + self.shard
        head = 2 * self.plane + self.core
        self.head_core = lax.div(head, n_shard)
        self.head_shard = lax.rem(head, n_shard)
        self.owner_plane = lax.div(self.slot, 2)
        self.owner_core = lax.rem(self.slot, 2)
        self.head_here = jnp.logical_and(self.slot == head, self.plane == self.shard)

    def group(self):
        for turn in range(1, 2 * self.n_shard):
            yield turn - 1, self.turned(turn)

    def turned(self, turn):
        core = lax.rem(self.core + turn // self.n_shard, 2)
        shard = lax.rem(self.shard + turn % self.n_shard, self.n_shard)
        return dict(core=core, shard=shard)

    def beside(self):
        across = self.plane + 1 - 2 * lax.rem(self.plane, 2)
        return across, lax.rem(self.plane + 2, 4), 3 - self.plane

    def along(self):
        for step in range(1, self.n_shard):
            yield step - 1, lax.rem(self.shard + step, self.n_shard)

    def planes(self):
        for step in range(1, self.n_plane):
            yield step - 1, lax.rem(self.plane + step, self.n_plane)

    def keeper(self):
        return dict(plane=self.shard, core=self.head_core, shard=self.head_shard)

    def owner(self):
        return dict(plane=self.owner_plane, core=self.owner_core, shard=self.plane)

    def greet(self, sender):
        barrier = pltpu.get_barrier_semaphore()
        count = 0
        for _, device in self.group():
            pl.semaphore_signal(barrier, inc=1, device_id=device, device_id_type=MESH)
            count += 1
        for _, plane in self.planes():
            pl.semaphore_signal(barrier, inc=1, device_id=dict(plane=plane), device_id_type=MESH)
            count += 1

        @pl.when(jnp.logical_not(self.head_here))
        def _():
            pl.semaphore_signal(barrier, inc=1, device_id=sender, device_id_type=MESH)
            pl.semaphore_wait(barrier, count + 1)

        @pl.when(self.head_here)
        def _():
            pl.semaphore_wait(barrier, count)


def turn_tables(pos_row, freq):
    n_pos = pos_row.shape[1]
    places = jnp.broadcast_to(pos_row.astype(jnp.float32), (n_pos, n_pos)).T
    phase = places * freq
    return jnp.cos(phase), jnp.sin(phase), places


def turn(head, cosine, sine):
    half = ROT // 2
    lanes = cosine.shape[1]
    front = head[:, :lanes]
    lane = lax.broadcasted_iota(jnp.int32, front.shape, 1)
    first = jnp.where(lane < half, -sine, 0.0)
    second = jnp.where((lane >= half) & (lane < ROT), sine, 0.0)
    turned = (
        front * cosine
        + pltpu.roll(front, lanes - half, 1) * first
        + pltpu.roll(front, half, 1) * second
    )
    return jnp.concatenate([turned, head[:, lanes:]], axis=1)


def dot(left, right, left_dim=1, right_dim=0):
    return lax.dot_general(
        left, right, (((left_dim,), (right_dim,)), ((), ())), preferred_element_type=jnp.float32
    )


class Spread:
    def __init__(self, spot, ref, size, sent, here):
        self.spot, self.ref, self.size, self.sent, self.here = spot, ref, size, sent, here
        self.across, self.along, self.diagonal = spot.beside()

    def rows(self, plane, part=None):
        size = self.size
        if part is None:
            return self.ref.at[pl.ds(pl.multiple_of(plane * size, size), size)]
        half = size // 2
        return self.ref.at[pl.ds(pl.multiple_of(plane * size + part * half, half), half)]

    def send(self, rows, place, plane):
        return push(rows, rows, self.sent.at[place], self.here.at[place], plane=plane)

    def first(self):
        own = self.rows(self.spot.plane)
        return [self.send(own, 0, self.across), self.send(own, 1, self.along)]

    def second(self):
        return [
            self.send(self.rows(self.along, 0), 2, self.across),
            self.send(self.rows(self.across, 1), 3, self.along),
        ]

    def start(self):
        for copy in self.first():
            copy.start()

    def relay(self):
        first, second = self.first(), self.second()
        first[1].wait_recv()
        second[0].start()
        first[0].wait_recv()
        second[1].start()

    def finish(self):
        for copy in self.second():
            copy.wait_recv()

    def finish_sends(self):
        for copy in self.first() + self.second():
            copy.wait_send()


class Gather:
    def __init__(self, spot, part, size, landed, sent, here):
        self.spot, self.part, self.size, self.landed = spot, part, size, landed
        self.sent, self.here = sent, here
        self.across, self.along, self.diagonal = spot.beside()

    def rows(self, plane, side):
        half = self.size // 2
        return self.part.at[pl.ds(pl.multiple_of(plane * self.size + side * half, half), half)]

    def send(self, rows, place, plane):
        return push(
            rows, self.landed.at[place], self.sent.at[place], self.here.at[place], plane=plane
        )

    def first(self):
        return [
            self.send(self.rows(self.diagonal, 0), 0, self.across),
            self.send(self.rows(self.diagonal, 1), 1, self.along),
            self.send(self.rows(self.across, 0), 2, self.across),
            self.send(self.rows(self.along, 1), 3, self.along),
        ]

    def second(self):
        return [
            self.send(self.rows(self.along, 0), 4, self.along),
            self.send(self.rows(self.across, 1), 5, self.across),
        ]

    def start(self):
        for copy in self.first():
            copy.start()

    def relay(self):
        first, second = self.first(), self.second()
        for side in range(2):
            first[side].wait_recv()
            held = self.rows(self.along if side == 0 else self.across, side)
            add_rows(held, [held, self.landed.at[side]], self.size // 2)
            second[side].start()

    def own(self):
        size = self.size
        return self.part.at[pl.ds(pl.multiple_of(self.spot.plane * size, size), size)]

    def finish(self):
        first, second = self.first(), self.second()
        half = self.size // 2
        for side in range(2):
            first[2 + side].wait_recv()
            second[side].wait_recv()
            held = self.rows(self.spot.plane, side)
            add_rows(held, [held, self.landed.at[2 + side], self.landed.at[4 + side]], half)

    def finish_sends(self):
        for copy in self.first() + self.second():
            copy.wait_send()


class RowSum:
    def __init__(self, spot, part, landed, sent, here):
        self.spot, self.part, self.landed = spot, part, landed
        self.sent, self.here = sent, here

    def rows(self, shard):
        return self.part.at[shard]

    def place(self, side, at, shard):
        if side == 0:
            return shard
        return jnp.where(shard == at, self.spot.n_shard, shard)

    def hop(self, side, shard):
        spot = self.spot
        to = spot.shard + (1 if side == 0 else -1)
        return push(
            self.rows(shard),
            self.landed.at[self.place(side, to, shard)],
            self.sent.at[side, shard],
            self.here.at[side, shard],
            shard=to,
        )

    def wait(self, side, shard):
        spot = self.spot
        push(
            self.rows(shard),
            self.landed.at[self.place(side, spot.shard, shard)],
            self.sent.at[side, shard],
            self.here.at[side, shard],
            shard=spot.shard,
        ).wait_recv()

    def start(self):
        spot, last = self.spot, self.spot.n_shard - 1
        for side in range(2):

            @pl.when(spot.shard == (0 if side == 0 else last))
            def _():
                for step in range(last):
                    self.hop(side, last - step if side == 0 else step).start()

    def relay(self, turn):
        spot, last = self.spot, self.spot.n_shard - 1
        for side in range(2):
            depth = spot.shard if side == 0 else last - spot.shard
            shard = last - turn + spot.shard if side == 0 else turn - last + spot.shard

            @pl.when(jnp.logical_and(depth >= 1, depth <= turn))
            def _():
                self.wait(side, shard)
                held = self.rows(shard)
                came = self.landed.at[self.place(side, spot.shard, shard)]
                add_rows(held, [held, came], held.shape[0])
                self.hop(side, shard).start()

    def finish(self, target):
        spot, last = self.spot, self.spot.n_shard - 1
        held = self.rows(spot.shard)
        first = self.landed.at[self.place(0, spot.shard, spot.shard)]
        second = self.landed.at[self.place(1, spot.shard, spot.shard)]

        @pl.when(spot.shard >= 1)
        def _():
            self.wait(0, spot.shard)

        @pl.when(spot.shard < last)
        def _():
            self.wait(1, spot.shard)

        @pl.when(spot.shard == 0)
        def _():
            add_rows(target, [held, second], held.shape[0])

        @pl.when(spot.shard == last)
        def _():
            add_rows(target, [held, first], held.shape[0])

        @pl.when(jnp.logical_and(spot.shard >= 1, spot.shard < last))
        def _():
            add_rows(target, [held, first, second], held.shape[0])

    def finish_sends(self):
        spot = self.spot
        for shard in range(spot.n_shard):
            for side in range(2):

                @pl.when(spot.shard < shard if side == 0 else spot.shard > shard)
                def _():
                    self.hop(side, shard).wait_send()


class Chain:
    def __init__(self, spot, ref, block, sent, here, pair_sent, pair_here):
        self.spot, self.ref, self.block = spot, ref, block
        self.sent, self.here = sent, here
        self.pair_sent, self.pair_here = pair_sent, pair_here

    def rows(self, shard, core):
        start = pl.multiple_of((shard * 2 + core) * self.block, self.block)
        return self.ref.at[pl.ds(start, self.block)]

    def hop(self, side, dist):
        spot = self.spot
        sign = 1 if side == 0 else -1
        rows = self.rows(spot.shard - sign * dist, spot.core)
        return push(
            rows, rows, self.sent.at[side, dist], self.here.at[side, dist], shard=spot.shard + sign
        )

    def pair(self, side, dist):
        spot = self.spot
        sign = 1 if side == 0 else -1
        rows = self.rows(spot.shard - sign * dist, spot.core)
        return push(
            rows,
            rows,
            self.pair_sent.at[side, dist],
            self.pair_here.at[side, dist],
            core=1 - spot.core,
        )

    def holds(self, side, dist):
        spot = self.spot
        return spot.shard >= dist if side == 0 else spot.shard + dist < spot.n_shard

    def goes(self, side, dist):
        spot = self.spot
        more = spot.shard + 1 < spot.n_shard if side == 0 else spot.shard >= 1
        return jnp.logical_and(self.holds(side, dist), more)

    def start(self):
        for side in range(2):

            @pl.when(self.goes(side, 0))
            def _():
                self.hop(side, 0).start()

        self.pair(0, 0).start()

    def step(self, dist):
        for side in range(2):

            @pl.when(self.holds(side, dist))
            def _():
                self.hop(side, dist - 1).wait_recv()
                if dist + 1 < self.spot.n_shard:

                    @pl.when(self.goes(side, dist))
                    def _():
                        self.hop(side, dist).start()

                self.pair(side, dist).start()

    def finish_pairs(self):
        self.pair(0, 0).wait_recv()
        for dist in range(1, self.spot.n_shard):
            for side in range(2):

                @pl.when(self.holds(side, dist))
                def _():
                    self.pair(side, dist).wait_recv()

    def finish_sends(self):
        self.pair(0, 0).wait_send()
        for side in range(2):
            for dist in range(self.spot.n_shard - 1):

                @pl.when(self.goes(side, dist))
                def _():
                    self.hop(side, dist).wait_send()

            for dist in range(1, self.spot.n_shard):

                @pl.when(self.holds(side, dist))
                def _():
                    self.pair(side, dist).wait_send()


def forward_kernel(
    n_plane,
    n_shard,
    x_ref,
    dy_ref,
    pos_ref,
    vec_ref,
    freq_ref,
    wq_ref,
    wu_ref,
    wd_ref,
    wo_ref,
    x_out,
    dy_out,
    one_out,
    two_out,
    hid_out,
    gup_out,
    back_out,
    wq_out,
    wu_out,
    wd_out,
    wo_out,
    vec_out,
    moments_out,
    x_all,
    dy_all,
    one,
    two,
    wq_all,
    wu_all,
    wd_all,
    wo_all,
    vec_all,
    pos_all,
    full_vec,
    wu_raw,
    wd_raw,
    wo_raw,
    wq_cut,
    wu_cut,
    wo_cut,
    to_heads,
    heads,
    from_heads,
    back,
    grad_k,
    grad_v,
    cos_head,
    sin_head,
    place_head,
    cos_row,
    sin_row,
    key_row,
    probs,
    slope,
    attention,
    moments,
    loads,
    stores,
    local,
    x_sent,
    x_here,
    x_pair_sent,
    x_pair_here,
    dy_sent,
    dy_here,
    dy_pair_sent,
    dy_pair_here,
    pos_sent,
    pos_here,
    cols_sent,
    cols_here,
    flat_sent,
    flat_here,
    spread_sent,
    spread_here,
    swap_sent,
    swap_here,
    head_sent,
    head_here,
):
    spot = Spot(n_plane, n_shard)
    plane, core, shard, slot = spot.plane, spot.core, spot.shard, spot.slot
    f32, bf16 = jnp.float32, jnp.bfloat16
    block = x_ref.shape[0]
    pair = 2 * block
    n_slice = 2 * n_shard
    rows_in, rows_down = wq_ref.shape[0], wd_ref.shape[0]
    width = x_ref.shape[1]
    n_group = n_slice * block

    def piece(ref, at, size):
        return ref.at[pl.ds(pl.multiple_of(at * size, size), size)]

    chain_x = Chain(spot, x_all, block, x_sent, x_here, x_pair_sent, x_pair_here)
    chain_dy = Chain(spot, dy_all, block, dy_sent, dy_here, dy_pair_sent, dy_pair_here)

    raw = [
        pltpu.make_async_copy(source, held, loads.at[place])
        for place, (source, held) in enumerate(
            [
                (wq_ref, wu_raw.at[:, pl.ds(0, wq_ref.shape[1])]),
                (wu_ref, wu_raw),
                (wd_ref, wd_raw),
                (wo_ref, wo_raw),
                (x_ref, chain_x.rows(shard, core)),
                (dy_ref, chain_dy.rows(shard, core)),
                (pos_ref, pos_all.at[shard]),
                (vec_ref, vec_all.at[plane, slot]),
            ]
        )
    ]
    for place, copy in enumerate(raw):
        if place != 1:
            copy.start()
    spot.greet(spot.owner())

    index = plane * n_slice + slot
    wq_own = piece(wq_all, index, rows_in)
    wu_own = piece(wu_all, index, rows_in)

    def to_group(place, source, target):
        return [
            push(
                source(device["core"] * n_shard + device["shard"]),
                target,
                cols_sent.at[place, turn_at],
                cols_here.at[place, turn_at],
                **device,
            )
            for turn_at, device in spot.group()
        ]

    cols_q = to_group(0, lambda to: wq_cut.at[to], wq_own)
    cols_u = to_group(1, lambda to: wu_cut.at[to], wu_own)
    cols_v = to_group(2, lambda to: vec_all.at[plane, slot], vec_all.at[plane, slot])

    def to_planes(place, ref):
        return [
            push(ref, ref, flat_sent.at[place, turn_at], flat_here.at[place, turn_at], plane=to)
            for turn_at, to in spot.planes()
        ]

    group_rows = n_slice * rows_in
    spread_d = Spread(spot, wd_all, rows_down, spread_sent.at[0], spread_here.at[0])
    spread_q = Spread(spot, wq_all, group_rows, spread_sent.at[1], spread_here.at[1])
    spread_u = Spread(spot, wu_all, group_rows, spread_sent.at[2], spread_here.at[2])
    flat_v = to_planes(0, vec_all.at[plane])
    flat_o = to_planes(1, piece(wo_all, plane, rows_in))
    pos_push = [
        push(
            pos_all.at[shard],
            pos_all.at[shard],
            pos_sent.at[turn_at],
            pos_here.at[turn_at],
            shard=to,
        )
        for turn_at, to in spot.along()
    ]

    raw[6].wait()
    raw[7].wait()
    for copy in cols_v + pos_push:
        copy.start()

    raw[4].wait()
    chain_x.start()
    raw[0].wait()
    for to in range(n_slice):
        for part in range(3):
            wq_cut[to, :, part * HD : (part + 1) * HD] = wu_raw[
                :, part * width + to * HD : part * width + (to + 1) * HD
            ].astype(bf16)
    raw[1].start()
    for copy in cols_q:
        copy.start()
    keep_q = pltpu.make_async_copy(wq_cut.at[slot], wq_own, local.at[0])
    keep_q.start()
    for copy in cols_v:
        copy.wait_recv()
    for copy in flat_v:
        copy.start()
    raw[2].wait()

    down_at = plane * rows_down

    @pl.loop(0, rows_down // 32)
    def _(step):
        at = pl.multiple_of(step * 32, 32)
        wd_all[pl.ds(pl.multiple_of(down_at + at, 32), 32), :] = wd_raw[pl.ds(at, 32), :].astype(bf16)

    spread_d.start()
    raw[1].wait()
    for to in range(n_slice):
        for part in range(n_plane):
            wu_cut[to, :, part * rows_down : (part + 1) * rows_down] = wu_raw[
                :, part * width + to * rows_down : part * width + (to + 1) * rows_down
            ].astype(bf16)
    keep_u = pltpu.make_async_copy(wu_cut.at[slot], wu_own, local.at[1])
    keep_u.start()
    raw[3].wait()
    wo_cut[...] = wo_raw[...].astype(bf16)
    head_rows = piece(wo_all, shard, rows_in)
    to_head = push(wo_cut, head_rows, head_sent, head_here, **spot.keeper())
    own_head = pltpu.make_async_copy(wo_cut, head_rows, head_sent)

    @pl.when(spot.head_here)
    def _():
        own_head.start()

    @pl.when(jnp.logical_not(spot.head_here))
    def _():
        to_head.start()

    raw[5].wait()
    chain_x.step(1)
    for copy in cols_u:
        copy.start()
    spread_d.relay()
    chain_dy.start()
    keep_q.wait()
    for copy in cols_q:
        copy.wait_recv()
    spread_q.start()
    chain_x.step(2)

    for copy in pos_push:
        copy.wait_recv()
    freq = freq_ref[...]
    own_blocks = 2 * plane

    @pl.loop(0, n_shard)
    def _(seq):
        for half in range(2):
            at = pl.ds(pl.multiple_of(seq * pair + half * block, block), block)
            cosine, sine, _ = turn_tables(pos_all[seq, pl.ds(own_blocks + half, 1), :], freq)
            cos_row[at, :] = cosine
            sin_row[at, :] = sine

    spread_q.relay()
    keep_u.wait()
    for copy in cols_u:
        copy.wait_recv()
    spread_u.start()
    chain_dy.step(1)
    for dist in range(3, n_shard):
        chain_x.step(dist)

    @pl.when(spot.head_here)
    def _():
        own_head.wait()

    @pl.when(jnp.logical_not(spot.head_here))
    def _():
        to_head.wait_recv()

    for copy in flat_o:
        copy.start()

    @pl.loop(0, n_plane)
    def _(part):
        for half in range(2):
            at = pl.ds(pl.multiple_of(part * pair + half * block, block), block)
            cosine, sine, places = turn_tables(pos_all[plane, pl.ds(2 * part + half, 1), :], freq)
            cos_head[at, :] = cosine
            sin_head[at, :] = sine
            place_head[at, :] = places

    for at in range(pos_all.shape[1]):
        key_row[:, at * block : (at + 1) * block] = pos_all[plane, pl.ds(at, 1), :].astype(f32)

    for copy in flat_v:
        copy.wait_recv()
    n_vec, lanes = vec_all.shape[2:]
    lane = lax.broadcasted_iota(jnp.int32, (n_vec, lanes), 1)
    for p in range(n_plane):
        for t in range(0, n_slice, 2):
            at = (p * n_slice + t) * (lanes // 2)
            full_vec[:, at : at + lanes] = jnp.where(
                lane < lanes // 2, vec_all[p, t], pltpu.roll(vec_all[p, t + 1], lanes // 2, 1)
            )
    save_vec = pltpu.make_async_copy(full_vec, vec_out, stores.at[0])
    save_vec.start()

    chain_x.finish_pairs()
    save_x = pltpu.make_async_copy(x_all, x_out, stores.at[1])
    save_x.start()

    def norm_rows(seq):
        @pl.loop(0, pair // 32)
        def _(step):
            at = pl.ds(pl.multiple_of(seq * pair + step * 32, 32), 32)
            tokens = x_all[at, :].astype(f32)
            mean = jnp.mean(tokens, axis=-1, keepdims=True)
            center = tokens - mean
            scale = lax.rsqrt(jnp.mean(center * center, axis=-1, keepdims=True) + 1e-05)
            lane = lax.broadcasted_iota(jnp.int32, (32, moments.shape[1]), 1)
            moments[at, :] = jnp.where(lane < 1, mean, scale)
            hat = center * scale
            one[at, :] = (hat * full_vec[0:1, :] + full_vec[1:2, :]).astype(bf16)
            two[at, :] = (hat * full_vec[2:3, :] + full_vec[3:4, :]).astype(bf16)

    for seq in range(n_shard):
        norm_rows(seq)
        if seq == 1:
            chain_dy.step(2)
            spread_u.relay()
    save_moments = pltpu.make_async_copy(moments, moments_out, stores.at[12])
    save_moments.start()
    save_one = pltpu.make_async_copy(one, one_out, stores.at[2])
    save_one.start()
    save_two = pltpu.make_async_copy(two, two_out, stores.at[3])
    save_two.start()

    spread_q.finish()
    save_wq = pltpu.make_async_copy(wq_all, wq_out, stores.at[4])
    save_wq.start()
    head_lanes = pl.ds(pl.multiple_of(slot * HD, HD), HD)

    def swap(place, source, target, cols, to, turn_at):
        def piece_of(ref, at):
            return ref.at[pl.ds(pl.multiple_of(at * pair, pair), pair), cols]

        return push(
            piece_of(source, to),
            piece_of(target, plane),
            swap_sent.at[place, turn_at - 1],
            swap_here.at[place, turn_at - 1],
            plane=to,
        )

    def keep_own(place, source, target, cols):
        at = pl.ds(pl.multiple_of(plane * pair, pair), pair)
        return pltpu.make_async_copy(source.at[at, cols], target.at[at, cols], local.at[place])

    def swaps(place, source, target, cols):
        return [
            swap(place, source, target, cols, lax.rem(plane + turn_at, n_plane), turn_at)
            for turn_at in range(1, n_plane)
        ]

    qkv_cols = pl.ds(0, 3 * HD)
    q_cols, kv_cols, o_cols = pl.ds(0, HD), pl.ds(HD, 2 * HD), pl.ds(3 * HD, HD)

    for step in range(2):
        at = slice(step * 2 * pair, (step + 1) * 2 * pair)
        heads_now = dot(one[at, :], wq_all[...])
        for part in range(3):
            cols = slice(part * HD, (part + 1) * HD)
            value = heads_now[:, cols] + full_vec[4 + part : 5 + part, head_lanes]
            if part < 2:
                value = turn(value, cos_row[at, :], sin_row[at, :])
            to_heads[at, cols] = value.astype(bf16)

    for copy in swaps(0, to_heads, heads, qkv_cols):
        copy.start()
    keep_qkv = keep_own(2, to_heads, heads, qkv_cols)
    keep_qkv.start()

    spread_u.finish()
    save_wu = pltpu.make_async_copy(wu_all, wu_out, stores.at[8])
    save_wu.start()
    save_one.wait()
    up_lanes = pl.ds(pl.multiple_of(slot * rows_down, rows_down), rows_down)
    n_hid = n_plane * rows_down

    def hidden_rows(step):
        at = pl.ds(pl.multiple_of(step * pair, pair), pair)
        hidden = dot(two[at, :], wu_all[...])
        for part in range(n_plane):
            cols = slice(part * rows_down, (part + 1) * rows_down)
            value = hidden[:, cols] + full_vec[8 + part : 9 + part, up_lanes]
            half = 0.5 + 0.5 * lax.erf(value * 0.7071067811865476)
            slope[at, cols] = half + value * (0.3989422804014327 * jnp.exp(-0.5 * value * value))
            one[at, cols] = (value * half).astype(bf16)

    @pl.loop(0, n_shard)
    def _(step):
        hidden_rows(step)

    for dist in range(3, n_shard):
        chain_dy.step(dist)

    save_hid = pltpu.make_async_copy(one.at[:, 0:n_hid], hid_out, stores.at[9])
    save_hid.start()

    chain_dy.finish_pairs()
    save_dy = pltpu.make_async_copy(dy_all, dy_out, stores.at[5])
    save_dy.start()
    for copy in flat_o:
        copy.wait_recv()
    save_wo = pltpu.make_async_copy(wo_all, wo_out, stores.at[6])
    save_wo.start()

    @pl.loop(0, 2)
    def _(step):
        at = pl.ds(pl.multiple_of(step * 2 * pair, 2 * pair), 2 * pair)
        to_heads[at, 3 * HD : 4 * HD] = dot(dy_all[at, :], wo_all[...], 1, 1).astype(bf16)

    for copy in swaps(1, to_heads, heads, o_cols):
        copy.start()
    keep_o = keep_own(3, to_heads, heads, o_cols)
    keep_o.start()

    grad_k[...] = jnp.zeros_like(grad_k)
    grad_v[...] = jnp.zeros_like(grad_v)
    scale = HD ** (-0.5)
    keep_qkv.wait()
    for copy in swaps(0, to_heads, heads, qkv_cols):
        copy.wait_recv()

    @pl.loop(0, n_plane)
    def _(part):
        at = pl.ds(pl.multiple_of(part * pair, pair), pair)
        places = place_head[at, 0:1]
        scores = dot(heads[at, 0:HD], heads[:, HD : 2 * HD], 1, 1) * scale
        scores = jnp.where(key_row[...] <= places, scores, -1e30)
        weights = jnp.exp(scores - jnp.max(scores, axis=-1, keepdims=True))
        share = weights / jnp.sum(weights, axis=-1, keepdims=True)
        probs[at, :] = share
        value = dot(share.astype(bf16), heads[:, 2 * HD : 3 * HD])
        attention[at, :] = value
        from_heads[at, 3 * HD : 4 * HD] = value.astype(bf16)

    for copy in swaps(2, from_heads, back, o_cols):
        copy.start()

    keep_o.wait()
    for copy in swaps(1, to_heads, heads, o_cols):
        copy.wait_recv()

    @pl.loop(0, n_plane)
    def _(step):
        turn_at = lax.rem(step + 1, n_plane)
        part = lax.rem(plane + turn_at, n_plane)
        at = pl.ds(pl.multiple_of(part * pair, pair), pair)
        grad_out = heads[at, 3 * HD : 4 * HD]
        delta = jnp.sum(grad_out.astype(f32) * attention[at, :], axis=-1, keepdims=True)
        grad_prob = dot(grad_out, heads[:, 2 * HD : 3 * HD], 1, 1)
        share = probs[at, :]
        dscore = (share * (grad_prob - delta)).astype(bf16)
        grad_q = dot(dscore, heads[:, HD : 2 * HD]) * scale
        from_heads[at, 0:HD] = turn(grad_q, cos_head[at, :], -sin_head[at, :]).astype(bf16)

        @pl.when(turn_at > 0)
        def _():
            swap(3, from_heads, back, q_cols, part, turn_at).start()

        grad_k[...] += dot(dscore, heads[at, 0:HD], 0, 0)
        grad_v[...] += dot(share.astype(bf16), grad_out, 0, 0)

    @pl.loop(0, n_plane)
    def _(step):
        turn_at = lax.rem(step + 1, n_plane)
        part = lax.rem(plane + turn_at, n_plane)
        at = pl.ds(pl.multiple_of(part * pair, pair), pair)
        turned = turn(grad_k[at, :] * scale, cos_head[at, :], -sin_head[at, :])
        from_heads[at, HD : 2 * HD] = turned.astype(bf16)
        from_heads[at, 2 * HD : 3 * HD] = grad_v[at, :].astype(bf16)

        @pl.when(turn_at > 0)
        def _():
            swap(4, from_heads, back, kv_cols, part, turn_at).start()

    keep_back = keep_own(2, from_heads, back, pl.ds(0, 4 * HD))
    keep_back.start()

    spread_d.finish()
    save_wd = pltpu.make_async_copy(wd_all, wd_out, stores.at[7])
    save_wd.start()

    @pl.loop(0, n_shard)
    def _(step):
        at = pl.ds(pl.multiple_of(step * pair, pair), pair)
        one[at, n_hid : 2 * n_hid] = (dot(dy_all[at, :], wd_all[...], 1, 1) * slope[at, :]).astype(
            bf16
        )

    save_gup = pltpu.make_async_copy(one.at[:, n_hid : 2 * n_hid], gup_out, stores.at[10])
    save_gup.start()
    keep_back.wait()
    again = (
        swaps(2, from_heads, back, o_cols)
        + swaps(3, from_heads, back, q_cols)
        + swaps(4, from_heads, back, kv_cols)
    )
    for copy in again:
        copy.wait_recv()
    save_back = pltpu.make_async_copy(back, back_out, stores.at[11])
    save_back.start()

    @pl.when(jnp.logical_not(spot.head_here))
    def _():
        to_head.wait_send()

    chain_x.finish_sends()
    chain_dy.finish_sends()
    for copy in cols_q + cols_u + cols_v + pos_push:
        copy.wait_send()
    for spread in [spread_d, spread_q, spread_u]:
        spread.finish_sends()
    again += swaps(0, to_heads, heads, qkv_cols) + swaps(1, to_heads, heads, o_cols)
    for copy in flat_v + flat_o + again:
        copy.wait_send()
    for copy in [
        save_vec,
        save_moments,
        save_x,
        save_two,
        save_wq,
        save_dy,
        save_wo,
        save_wd,
        save_wu,
        save_hid,
        save_gup,
        save_back,
    ]:
        copy.wait()


def forward_all(n_plane, n_shard, x, dy, pos, vec, freq, wq, wu, wd, wo):
    f32, bf16 = jnp.float32, jnp.bfloat16
    n_slice = 2 * n_shard
    block, width = x.shape
    rows_in, rows_down = wq.shape[0], wd.shape[0]
    group = n_slice * block
    n_hid = n_plane * rows_down
    cols_q = 3 * HD
    n_vec, lanes = vec.shape
    dma = pltpu.SemaphoreType.DMA
    vmem = pltpu.VMEM
    shape = jax.ShapeDtypeStruct
    anywhere = pl.BlockSpec(memory_space=pl.ANY)
    far, near = n_shard - 1, n_plane - 1
    return pl.pallas_call(
        partial(forward_kernel, n_plane, n_shard),
        out_shape=[
            shape((group, width), bf16),
            shape((group, width), bf16),
            shape((group, width), bf16),
            shape((group, width), bf16),
            shape((group, n_hid), bf16),
            shape((group, n_hid), bf16),
            shape((group, 4 * HD), bf16),
            shape((width, cols_q), bf16),
            shape((width, n_hid), bf16),
            shape((n_hid, width), bf16),
            shape((HD, width), bf16),
            shape((n_vec, width), f32),
            shape((group, block), f32),
        ],
        in_specs=[anywhere] * 4 + [pl.BlockSpec(memory_space=vmem)] + [anywhere] * 4,
        out_specs=[anywhere] * 13,
        scratch_shapes=[
            vmem((group, width), bf16),
            vmem((group, width), bf16),
            vmem((group, width), bf16),
            vmem((group, width), bf16),
            vmem((width, cols_q), bf16),
            vmem((width, n_hid), bf16),
            vmem((n_hid, width), bf16),
            vmem((HD, width), bf16),
            vmem((n_plane, n_slice, n_vec, lanes), f32),
            vmem((n_shard, *pos.shape), jnp.int32),
            vmem((n_vec, width), f32),
            vmem(wu.shape, f32),
            vmem(wd.shape, f32),
            vmem(wo.shape, f32),
            vmem((n_slice, rows_in, cols_q), bf16),
            vmem((n_slice, rows_in, n_hid), bf16),
            vmem(wo.shape, bf16),
            vmem((group, 4 * HD), bf16),
            vmem((group, 4 * HD), bf16),
            vmem((group, 4 * HD), bf16),
            vmem((group, 4 * HD), bf16),
            vmem((group, HD), f32),
            vmem((group, HD), f32),
            *([vmem((group, block), f32)] * 5),
            vmem((1, group), f32),
            vmem((group, group), f32),
            vmem((group, n_hid), f32),
            vmem((group, HD), f32),
            vmem((group, block), f32),
            dma((8,)),
            dma((13,)),
            dma((4,)),
            *([dma((2, n_shard))] * 8),
            dma((far,)),
            dma((far,)),
            dma((3, n_slice - 1)),
            dma((3, n_slice - 1)),
            dma((2, near)),
            dma((2, near)),
            dma((3, 4)),
            dma((3, 4)),
            dma((5, near)),
            dma((5, near)),
            dma,
            dma,
        ],
        compiler_params=pltpu.CompilerParams(
            collective_id=0, has_side_effects=True, vmem_limit_bytes=VMEM_BYTES
        ),
        name="forward_all",
    )(x, dy, pos, vec, freq, wq, wu, wd, wo)


def add_rows(target, terms, rows):
    columns = target.shape[1]
    chunk = min(rows, 64 if columns <= 1024 else 32)

    @pl.loop(0, rows // chunk)
    def _(step):
        at = pl.ds(pl.multiple_of(step * chunk, chunk), chunk)
        for start in range(0, columns, 256):
            cols = slice(start, start + 256)
            total = terms[0][at, cols].astype(jnp.float32)
            for term in terms[1:]:
                total = total + term[at, cols].astype(jnp.float32)
            target[at, cols] = total.astype(target.dtype)


def backward_kernel(
    n_plane,
    n_shard,
    x_ref,
    dy_ref,
    one_ref,
    two_ref,
    hid_ref,
    gup_ref,
    back_ref,
    wq_ref,
    wu_ref,
    wd_ref,
    wo_ref,
    vec_ref,
    moments_ref,
    out_sum,
    hat_sum,
    dq_sum,
    du_sum,
    dd_sum,
    do_sum,
    vec_sum,
    big_one,
    big_two,
    big_three,
    x_rows,
    hid,
    gup,
    back,
    wq,
    wo,
    vec,
    moments,
    rows_part,
    other_half,
    theirs,
    parts,
    q_part,
    u_part,
    o_part,
    v_part,
    q_in,
    u_in,
    d_in,
    o_in,
    v_in,
    o_mid,
    v_mid,
    v_end,
    loads,
    local,
    pair_sent,
    pair_here,
    rows_sent,
    rows_here,
    flat_sent,
    flat_here,
    sum_sent,
    sum_here,
    cols_sent,
    cols_here,
    head_sent,
    head_here,
    x_sem,
    free,
):
    spot = Spot(n_plane, n_shard)
    plane, core, shard, slot = spot.plane, spot.core, spot.shard, spot.slot
    f32, bf16 = jnp.float32, jnp.bfloat16
    n_slice = 2 * n_shard
    n_group, width = dy_ref.shape
    block = n_group // n_slice
    pair = 2 * block
    rows_down = width // n_slice
    cols_q = 3 * HD
    n_hid = hid_ref.shape[1]
    rows_plane = width // n_plane
    rows_in = rows_plane // n_slice

    def load(source, target, place):
        copy = pltpu.make_async_copy(source, target, loads.at[place])
        copy.start()
        return copy

    def plane_rows(ref, at):
        return ref.at[pl.ds(pl.multiple_of(at * pair, pair), pair)]

    load_two = load(two_ref, big_three, 0)
    load_hid = load(hid_ref, hid, 1)
    load_dy = load(dy_ref, big_one, 2)
    load_back = load(back_ref, back, 3)
    load_wo = load(wo_ref, wo, 4)
    load_wd = load(wd_ref, big_two, 5)
    load_gup = load(gup_ref, gup, 7)
    load_wq = load(wq_ref, wq, 8)
    load_vec = load(vec_ref, vec, 9)
    load_moments = load(moments_ref, moments, 10)
    spot.greet(spot.keeper())

    def flat(place, source, target):
        return [
            push(
                source(to),
                target.at[turn_at],
                flat_sent.at[place, turn_at],
                flat_here.at[place, turn_at],
                plane=to,
            )
            for turn_at, to in spot.planes()
        ]

    def at_plane(ref, size):
        return lambda to: ref.at[pl.ds(pl.multiple_of(to * size, size), size)]

    sum_u = Gather(spot, u_part, rows_plane, u_in, sum_sent.at[0], sum_here.at[0])
    sum_q = Gather(spot, q_part, rows_plane, q_in, sum_sent.at[1], sum_here.at[1])
    sum_d = Gather(spot, big_two, rows_down, d_in, sum_sent.at[2], sum_here.at[2])
    flat_o = flat(0, at_plane(o_part, rows_in), o_in)
    flat_v = flat(
        1,
        lambda to: v_part.at[:, pl.ds(pl.multiple_of(to * rows_plane, rows_plane), rows_plane)],
        v_in,
    )

    def weight_grad(left, right, target, columns):
        @pl.loop(0, left.shape[1] // 512)
        def _(step):
            at = pl.ds(pl.multiple_of(step * 512, 512), 512)
            turned = left[:, at].T
            for start in range(0, columns, n_group):
                cols = slice(start, min(start + n_group, columns))
                target[at, cols] = dot(turned, right[:, cols]).astype(bf16)

    sums = [
        RowSum(spot, rows_part.at[place], parts.at[place], rows_sent.at[place], rows_here.at[place])
        for place in range(2)
    ]

    def pair_push(place, seq):
        return push(
            other_half.at[seq],
            theirs.at[seq],
            pair_sent.at[place, seq],
            pair_here.at[place, seq],
            core=1 - core,
        )

    def put(place, seq, cols, total):
        first, second = total[:block], total[block:]
        rows_part[place, seq, :, cols] = jnp.where(core == 0, first, second).astype(bf16)
        other_half[seq, :, cols] = jnp.where(core == 0, second, first).astype(bf16)

    def add_pairs(place):
        @pl.loop(0, n_shard)
        def _(seq):
            pair_push(place, seq).wait_recv()
            held = rows_part.at[place, seq]
            add_rows(held, [held, theirs.at[seq]], block)

        sums[place].start()

    def add_shards(place, target):
        sums[place].finish(sums[place].rows(shard))
        copy = pltpu.make_async_copy(sums[place].rows(shard), target, local.at[2, 1 + place])
        copy.start()
        return copy

    def regroup(place, held, target, wide):
        base = pl.multiple_of(plane * rows_plane, rows_plane)
        parts_here = held.shape[1] // wide

        def rows(to, part):
            start = pl.multiple_of(base + to * rows_in, rows_in)
            return held.at[pl.ds(start, rows_in), pl.ds(part * wide, wide)]

        def lands(part):
            start = pl.multiple_of(part * width + slot * wide, wide)
            return target.at[:, pl.ds(start, wide)]

        copies = []
        for turn_at, device in spot.group():
            to = device["core"] * n_shard + device["shard"]
            for part in range(parts_here):
                copies.append(
                    push(
                        rows(to, part),
                        lands(part),
                        cols_sent.at[place, turn_at, part],
                        cols_here.at[place, turn_at, part],
                        **device,
                    )
                )
        keeps = [
            pltpu.make_async_copy(rows(slot, part), lands(part), local.at[place, part])
            for part in range(parts_here)
        ]
        for copy in copies + keeps:
            copy.start()
        return copies, keeps

    load_two.wait()
    load_gup.wait()
    weight_grad(big_three, gup, u_part, n_hid)
    sum_u.start()

    load_wu = [
        load(
            wu_ref.at[pl.ds(part * n_group, n_group)],
            big_three.at[:, pl.ds(part * n_hid, n_hid)],
            11 + part,
        )
        for part in range(width // n_group)
    ]

    load_hid.wait()
    load_back.wait()
    load_wo.wait()
    load_wd.wait()

    @pl.loop(0, n_shard)
    def _(seq):
        at = pl.ds(pl.multiple_of(seq * pair, pair), pair)
        for start in range(0, width, n_group):
            cols = slice(start, start + n_group)
            total = dot(back[at, cols_q : cols_q + HD], wo[:, cols])
            put(0, seq, cols, total + dot(hid[at, :], big_two[:, cols]))
        pair_push(0, seq).start()

    add_pairs(0)
    pl.semaphore_signal(free, inc=1, device_id=dict(core=1 - core), device_id_type=MESH)

    def x_load(seq):
        return pltpu.make_async_copy(plane_rows(x_ref, seq), x_rows, x_sem)

    x_load(0).start()
    v_part[...] = jnp.zeros_like(v_part)
    load_wq.wait()
    load_vec.wait()
    for copy in load_wu:
        copy.wait()
    load_moments.wait()
    for seq in range(n_shard):
        pair_push(0, seq).wait_send()
    pl.semaphore_wait(free, 1)

    def norm_rows(seq):
        at = pl.ds(pl.multiple_of(seq * pair, pair), pair)
        mean, scale = moments[at, 0:1], moments[at, 1:2]
        for start in range(0, width, 512):
            cols = slice(start, start + 512)
            up_rows = slice(start % n_group, start % n_group + 512)
            up_cols = slice(start // n_group * n_hid, (start // n_group + 1) * n_hid)
            grad_one = dot(back[at, 0:cols_q], wq[cols, :], 1, 1)
            grad_two = dot(gup[at, :], big_three[up_rows, up_cols], 1, 1)
            if start == 0:
                x_load(seq).wait()
            hat = (x_rows[:, cols].astype(f32) - mean) * scale
            v_part[0:1, cols] += jnp.sum(grad_one * hat, axis=0, keepdims=True)
            v_part[1:2, cols] += jnp.sum(grad_one, axis=0, keepdims=True)
            v_part[2:3, cols] += jnp.sum(grad_two * hat, axis=0, keepdims=True)
            v_part[3:4, cols] += jnp.sum(grad_two, axis=0, keepdims=True)
            put(1, seq, cols, grad_one * vec[0:1, cols] + grad_two * vec[2:3, cols])
        pair_push(1, seq).start()

        @pl.when(seq + 1 < n_shard)
        def _():
            x_load(seq + 1).start()


    @pl.loop(0, n_shard // 2)
    def _(seq):
        norm_rows(seq)

    sum_u.relay()
    sums[0].relay(1)

    @pl.loop(n_shard // 2, n_shard)
    def _(seq):
        norm_rows(seq)

    load_one = load(one_ref, big_three, 6)
    add_pairs(1)
    sum_u.finish()
    cols_u, keep_u = regroup(0, u_part, du_sum, rows_down)

    load_one.wait()
    weight_grad(big_three, back, q_part, cols_q)
    sum_q.start()
    sums[0].relay(2)
    sums[1].relay(1)

    load_dy.wait()
    weight_grad(hid, big_one, big_two, width)
    sum_q.relay()
    sum_d.start()
    attn = back[:, cols_q : cols_q + HD]
    half = width // 2
    for part in range(2):
        cols = slice(part * half, (part + 1) * half)
        o_part[:, cols] = dot(attn, big_one[:, cols], 0, 0).astype(bf16)
    for copy in flat_o:
        copy.start()

    own = pl.ds(pl.multiple_of((shard * 2 + core) * block, block), block)
    column_out = jnp.sum(big_one[own, :].astype(f32), axis=0, keepdims=True)
    v_part[7:8, :] = column_out
    v_part[12:13, :] = column_out
    lanes = pl.ds(pl.multiple_of(slot * HD, HD), HD)
    for part in range(3):
        cols = slice(part * HD, (part + 1) * HD)
        v_part[4 + part : 5 + part, lanes] = jnp.sum(
            back[:, cols].astype(f32), axis=0, keepdims=True
        )
    lanes = pl.ds(pl.multiple_of(slot * rows_down, rows_down), rows_down)
    for part in range(n_plane):
        cols = slice(part * rows_down, (part + 1) * rows_down)
        v_part[8 + part : 9 + part, lanes] = jnp.sum(
            gup[:, cols].astype(f32), axis=0, keepdims=True
        )
    for copy in flat_v:
        copy.start()
    sums[1].relay(2)
    save_out = add_shards(0, out_sum)
    sum_q.finish()
    cols_q_copies, keep_q = regroup(1, q_part, dq_sum, HD)
    save_hat = add_shards(1, hat_sum)
    sum_d.relay()

    for copy in flat_o:
        copy.wait_recv()
    mine = o_part.at[pl.ds(pl.multiple_of(plane * rows_in, rows_in), rows_in)]
    add_rows(o_mid, [mine] + [o_in.at[turn_at] for turn_at in range(n_plane - 1)], rows_in)
    to_owner = push(
        o_mid,
        do_sum,
        head_sent,
        head_here,
        plane=spot.owner_plane,
        core=spot.owner_core,
        shard=plane,
    )
    own_rows = pltpu.make_async_copy(o_mid, do_sum, head_sent)

    @pl.when(spot.head_here)
    def _():
        own_rows.start()

    @pl.when(jnp.logical_not(spot.head_here))
    def _():
        to_owner.start()

    for copy in flat_v:
        copy.wait_recv()
    total = v_part[:, pl.ds(pl.multiple_of(plane * rows_plane, rows_plane), rows_plane)]
    for turn_at in range(n_plane - 1):
        total = total + v_in[turn_at]
    v_mid[...] = total
    wide = 2 * rows_in

    def lanes_of(device):
        half_slot = device["core"] * n_shard + device["shard"]
        return pl.ds(pl.multiple_of(lax.div(half_slot, 2) * wide, wide), wide)

    v_end[slot] = v_mid[:, lanes_of(spot.turned(0))]
    cols_v = []
    for turn_at, device in spot.group():
        cols_v.append(
            push(
                v_mid.at[:, lanes_of(device)],
                v_end.at[slot],
                cols_sent.at[2, turn_at, 0],
                cols_here.at[2, turn_at, 0],
                **device,
            )
        )
    for copy in cols_v:
        copy.start()

    save_sums = [save_out, save_hat]
    sum_d.finish()
    save_d = pltpu.make_async_copy(sum_d.own(), dd_sum, local.at[2, 0])
    save_d.start()
    for copy in cols_v:
        copy.wait_recv()
    total = v_end[0]
    for other in range(1, n_slice):
        total = total + v_end[other]
    odd = lax.rem(slot, 2) == 1
    vec_sum[...] = jnp.where(odd, pltpu.roll(total, rows_in, 1), total)

    for copy in keep_u + keep_q:
        copy.wait()
    for copy in cols_u + cols_q_copies:
        copy.wait_recv()

    @pl.when(spot.head_here)
    def _():
        own_rows.wait()

    @pl.when(jnp.logical_not(spot.head_here))
    def _():
        to_owner.wait_recv()
        to_owner.wait_send()

    for seq in range(n_shard):
        pair_push(1, seq).wait_send()
    for place in range(2):
        sums[place].finish_sends()
    for copy in save_sums + [save_d]:
        copy.wait()
    for total in [sum_u, sum_q, sum_d]:
        total.finish_sends()
    for copy in flat_o + flat_v + cols_u + cols_q_copies + cols_v:
        copy.wait_send()


def backward_all(n_plane, n_shard, *arrays):
    x, dy, _, _, hid, _, back, wq, _, _, wo, vec, moments = arrays
    f32, bf16 = jnp.float32, jnp.bfloat16
    n_slice = 2 * n_shard
    group, width = dy.shape
    block = group // n_slice
    rows_down = width // n_slice
    rows_plane = width // n_plane
    rows_in = rows_plane // n_slice
    cols_q, n_hid = 3 * HD, hid.shape[1]
    n_vec = 16
    dma = pltpu.SemaphoreType.DMA
    vmem = pltpu.VMEM
    shape = jax.ShapeDtypeStruct
    near = n_plane - 1
    inside = pl.BlockSpec(memory_space=vmem)
    anywhere = pl.BlockSpec(memory_space=pl.ANY)
    return pl.pallas_call(
        partial(backward_kernel, n_plane, n_shard),
        out_shape=[
            shape((block, width), bf16),
            shape((block, width), bf16),
            shape((rows_in, n_slice * cols_q), bf16),
            shape((rows_in, n_slice * n_hid), bf16),
            shape((rows_down, width), bf16),
            shape((rows_in, width), bf16),
            shape((n_vec, 2 * rows_in), f32),
        ],
        in_specs=[anywhere] * 13,
        out_specs=[anywhere] * 6 + [inside],
        scratch_shapes=[
            vmem((group, width), bf16),
            vmem((group, width), bf16),
            vmem((group, width), bf16),
            vmem((2 * block, width), bf16),
            vmem(hid.shape, bf16),
            vmem(hid.shape, bf16),
            vmem(back.shape, bf16),
            vmem(wq.shape, bf16),
            vmem(wo.shape, bf16),
            vmem(vec.shape, f32),
            vmem(moments.shape, f32),
            vmem((2, n_shard, block, width), bf16),
            vmem((n_shard, block, width), bf16),
            vmem((n_shard, block, width), bf16),
            vmem((2, n_shard + 1, block, width), bf16),
            vmem((width, cols_q), bf16),
            vmem((width, n_hid), bf16),
            vmem(wo.shape, bf16),
            vmem((n_vec, width), f32),
            vmem((6, rows_plane // 2, cols_q), bf16),
            vmem((6, rows_plane // 2, n_hid), bf16),
            vmem((6, rows_down // 2, width), bf16),
            vmem((near, rows_in, width), bf16),
            vmem((near, n_vec, rows_plane), f32),
            vmem((rows_in, width), bf16),
            vmem((n_vec, rows_plane), f32),
            vmem((n_slice, n_vec, 2 * rows_in), f32),
            dma((13,)),
            dma((3, n_plane)),
            dma((2, n_shard)),
            dma((2, n_shard)),
            dma((2, 2, n_shard)),
            dma((2, 2, n_shard)),
            dma((2, near)),
            dma((2, near)),
            dma((3, 6)),
            dma((3, 6)),
            dma((3, n_slice - 1, n_plane)),
            dma((3, n_slice - 1, n_plane)),
            dma,
            dma,
            dma,
            pltpu.SemaphoreType.REGULAR,
        ],
        compiler_params=pltpu.CompilerParams(
            collective_id=1, has_side_effects=True, vmem_limit_bytes=VMEM_BYTES
        ),
        name="backward_all",
    )(*arrays)


def fast_device(
    layer_input,
    out_grad,
    positions,
    w_qkv,
    w_dense,
    w_up,
    w_down,
    vectors,
    m_qkv,
    m_dense,
    m_up,
    m_down,
    m_vectors,
    v_qkv,
    v_dense,
    v_up,
    v_down,
    v_vectors,
):
    bf16 = jnp.bfloat16
    f32 = jnp.float32
    n_plane = lax.axis_size("plane")
    n_shard = lax.axis_size("shard")
    block_rows = layer_input.shape[1]
    n_vec, vec_cols = vectors.shape

    half_rot = ROT // 2
    inverse = 10000.0 ** (-jnp.arange(0, ROT, 2).astype(f32) / ROT)
    freq = jnp.pad(jnp.concatenate([inverse, inverse]), (0, 128 - 2 * half_rot))[None]
    kept = forward_all(
        n_plane,
        n_shard,
        layer_input[0],
        out_grad[0],
        positions.reshape(-1, block_rows),
        jnp.pad(vectors, ((0, 16 - n_vec), (0, 128 - vec_cols))),
        freq,
        w_qkv,
        w_up,
        w_down,
        w_dense,
    )
    branches, grad_hat, part_qkv, part_up, part_down, part_dense, part_vec = backward_all(
        n_plane, n_shard, *kept
    )
    full_vec = kept[-2]
    branches = branches.astype(f32)
    grad_hat = grad_hat.astype(f32)
    own_tokens = layer_input[0].astype(f32)
    grad_rows = out_grad[0].astype(f32)
    layer_output = (own_tokens + branches + full_vec[7] + full_vec[12]).astype(bf16)[None]
    own_center = own_tokens - jnp.mean(own_tokens, axis=-1, keepdims=True)
    own_inv = lax.rsqrt(jnp.mean(own_center * own_center, axis=-1, keepdims=True) + 1e-05)
    own_hat = own_center * own_inv
    grad_input = (
        grad_rows
        + own_inv
        * (
            grad_hat
            - jnp.mean(grad_hat, axis=-1, keepdims=True)
            - own_hat * jnp.mean(grad_hat * own_hat, axis=-1, keepdims=True)
        )
    )[None]
    grad_vectors = part_vec[:n_vec, :vec_cols]
    grad_dense = part_dense.astype(f32)
    grad_down = part_down.astype(f32)
    grad_qkv = part_qkv.astype(f32)
    grad_up = part_up.astype(f32)
    new_qkv, second_qkv = adam_step(w_qkv, grad_qkv, m_qkv, v_qkv, 4.0 * (D // 2) ** (-0.5), 0.1)
    new_dense, second_dense = adam_step(
        w_dense, grad_dense, m_dense, v_dense, 4.0 * (D // 32) ** (-0.5), 0.1
    )
    new_up, second_up = adam_step(w_up, grad_up, m_up, v_up, 4.0 * D ** (-0.5), 0.1)
    new_down, second_down = adam_step(w_down, grad_down, m_down, v_down, 4.0 * FF ** (-0.5), 0.1)
    new_vectors, second_vectors = adam_step(vectors, grad_vectors, m_vectors, v_vectors, 1.0, 0.0)
    return (
        layer_output,
        grad_input,
        grad_qkv,
        grad_dense,
        grad_up,
        grad_down,
        grad_vectors,
        second_qkv,
        second_dense,
        second_up,
        second_down,
        second_vectors,
        new_qkv,
        new_dense,
        new_up,
        new_down,
        new_vectors,
    )


def solution(mesh):
    n_ctx, n_shard = mesh.devices.shape
    if n_ctx == 2 * n_shard and n_ctx == H:
        device_mesh = Mesh(
            mesh.devices.reshape(n_shard, 2, n_shard), ("plane", "core", "shard")
        )
        ctx, body = ("plane", "core"), fast_device
    else:
        device_mesh, ctx, body = mesh, ("ctx",), general_device
    rows = P("shard", ctx, None)
    weight = P((*ctx, "shard"), None)
    vector = P(None, (*ctx, "shard"))
    matrices = (weight,) * 4 + (vector,)
    in_specs = (rows, rows, P("shard", None)) + matrices * 3
    out_specs = (rows, rows) + matrices * 3
    return jax.shard_map(
        body, mesh=device_mesh, in_specs=in_specs, out_specs=out_specs, check_vma=False
    )
```

```python
from functools import partial

import jax
import jax.numpy as jnp
from jax import lax
from jax.experimental import pallas as pl
from jax.experimental.pallas import tpu as pltpu
from jax.sharding import Mesh, PartitionSpec as P

D = 2048
H = 8
HD = 256
ROT = 64
FF = 8192
STEP = 10


def from_behind(value, axis, steps):
    count = lax.axis_size(axis)
    pairs = [(source, (source + steps) % count) for source in range(count)]
    return lax.ppermute(value, axis, pairs)


def layer_norm(values, gain, shift):
    center = values - jnp.mean(values, axis=-1, keepdims=True)
    spread = jnp.mean(center * center, axis=-1, keepdims=True)
    return center * lax.rsqrt(spread + 1e-05) * gain + shift


def angles(places):
    inverse = 10000.0 ** (-jnp.arange(0, ROT, 2).astype(jnp.float32) / ROT)
    phases = places.astype(jnp.float32)[:, None] * inverse[None, :]
    return (jnp.cos(phases), jnp.sin(phases))


def rotate(values, cosine, sine):
    half_rot = cosine.shape[-1]
    front = values[..., :half_rot]
    second = values[..., half_rot : 2 * half_rot]
    others = values[..., 2 * half_rot :]
    cos_b = cosine[:, None, :]
    sin_b = sine[:, None, :]
    return jnp.concatenate(
        [front * cos_b - second * sin_b, second * cos_b + front * sin_b, others], axis=-1
    )


def adam_step(weight, gradient, moment, second, rate, decay):
    moment = 0.9 * moment + 0.1 * gradient
    second = 0.95 * second + 0.05 * gradient * gradient
    unbiased = moment / (1.0 - 0.9**STEP)
    scaled = second / (1.0 - 0.95**STEP)
    return (weight - rate * (unbiased / (jnp.sqrt(scaled) + 1e-08) + decay * weight), second)


def general_device(
    layer_input,
    out_grad,
    positions,
    w_qkv,
    w_dense,
    w_up,
    w_down,
    vectors,
    m_qkv,
    m_dense,
    m_up,
    m_down,
    m_vectors,
    v_qkv,
    v_dense,
    v_up,
    v_down,
    v_vectors,
):
    block_rows = layer_input.shape[1]
    model_width = layer_input.shape[2]
    hidden = w_up.shape[1]
    rows_in = w_qkv.shape[0]
    rows_down = w_down.shape[0]
    n_ctx = lax.axis_size("ctx")
    score_scale = HD ** (-0.5)
    ctx_index = lax.axis_index("ctx")
    all_pos = positions[0]
    own_pos = lax.dynamic_slice_in_dim(all_pos, ctx_index * block_rows, block_rows)
    last_own = jnp.max(own_pos)
    cosine, sine = angles(own_pos)
    full_vec = lax.all_gather(vectors, ("ctx", "shard"), axis=1, tiled=True)
    tokens = layer_input[0].astype(jnp.float32)
    normed_one = layer_norm(tokens, full_vec[0], full_vec[1]).astype(jnp.bfloat16)
    normed_two = layer_norm(tokens, full_vec[2], full_vec[3]).astype(jnp.bfloat16)
    qkv_low = w_qkv.astype(jnp.bfloat16)
    dense_low = w_dense.astype(jnp.bfloat16)
    up_low = w_up.astype(jnp.bfloat16)
    down_low = w_down.astype(jnp.bfloat16)
    grad_low = out_grad[0]
    grad_rows = grad_low.astype(jnp.float32)
    pieces = (
        lax.all_gather(qkv_low, ("ctx", "shard"), axis=0, tiled=True),
        lax.all_gather(up_low, ("ctx", "shard"), axis=0, tiled=True),
    )
    left_one = normed_one
    left_two = normed_two
    proj_sum = jnp.dot(left_one, pieces[0], preferred_element_type=jnp.float32)
    up_sum = jnp.dot(left_two, pieces[1], preferred_element_type=jnp.float32)
    projection = proj_sum + full_vec[4:7].reshape(-1)
    up_value = up_sum + full_vec[8:12].reshape(-1)
    queries = projection[:, :model_width].reshape(block_rows, H, HD)
    keys_raw = projection[:, model_width : 2 * model_width].reshape(block_rows, H, HD)
    values_raw = projection[:, 2 * model_width :].reshape(block_rows, H, HD)
    q_rot = rotate(queries, cosine, sine).astype(jnp.bfloat16)
    k_rot = rotate(keys_raw, cosine, sine).astype(jnp.bfloat16)
    v_low = values_raw.astype(jnp.bfloat16)
    start_state = (
        jnp.full((block_rows, H), -1e30, jnp.float32),
        jnp.zeros((block_rows, H), jnp.float32),
        jnp.zeros((block_rows, H, HD), jnp.float32),
    )
    pieces = (
        lax.all_gather(k_rot, "ctx", axis=0, tiled=True),
        lax.all_gather(v_low, "ctx", axis=0, tiled=True),
    )
    key_pos = all_pos
    allowed = (key_pos[None, :] <= own_pos[:, None])[:, None, :]

    def attend_compute(states):
        running_top, totals, accum = states
        scores = (
            jnp.einsum("qhd,khd->qhk", q_rot, pieces[0], preferred_element_type=jnp.float32)
            * score_scale
        )
        scores = jnp.where(allowed, scores, -1e30)
        new_top = jnp.maximum(running_top, jnp.max(scores, axis=-1))
        weights = jnp.where(allowed, jnp.exp(scores - new_top[..., None]), 0.0)
        totals = jnp.sum(weights, axis=-1)
        accum = jnp.einsum(
            "qhk,khd->qhd",
            weights.astype(jnp.bfloat16),
            pieces[1],
            preferred_element_type=jnp.float32,
        )
        return (new_top, totals, accum)

    skipped = jnp.min(key_pos) > last_own
    running_top, totals, accum = lax.cond(
        skipped, lambda states: states, attend_compute, start_state
    )
    attention = accum / totals[..., None]
    log_sum = running_top + jnp.log(totals)
    attn_low = attention.reshape(block_rows, model_width).astype(jnp.bfloat16)
    gelu_exact = partial(jax.nn.gelu, approximate=False)
    hid_low = gelu_exact(up_value).astype(jnp.bfloat16)
    add_pieces = (
        lax.all_gather(dense_low, ("ctx", "shard"), axis=0, tiled=True),
        lax.all_gather(down_low, ("ctx", "shard"), axis=0, tiled=True),
    )
    second_count = add_pieces[1].shape[0]
    second_begin = jnp.int32(0) // rows_in * rows_down
    left_attn = attn_low
    left_hid = lax.dynamic_slice_in_dim(hid_low, second_begin, second_count, 1)
    branches = jnp.dot(left_attn, add_pieces[0], preferred_element_type=jnp.float32) + jnp.dot(
        left_hid, add_pieces[1], preferred_element_type=jnp.float32
    )
    back_pieces = lax.all_gather((dense_low, down_low), ("ctx", "shard"), axis=0, tiled=True)
    shard_count = back_pieces[0].shape[0] // rows_in
    first_part = jnp.einsum(
        "td,rd->tr", grad_low, back_pieces[0], preferred_element_type=jnp.float32
    ).reshape(block_rows, shard_count, rows_in)
    second_part = jnp.einsum(
        "td,rd->tr", grad_low, back_pieces[1], preferred_element_type=jnp.float32
    ).reshape(block_rows, shard_count, rows_down)
    merged_out = jnp.concatenate([first_part, second_part], axis=2).reshape(
        block_rows, shard_count * (rows_in + rows_down)
    )
    merged_out = merged_out.reshape(block_rows, -1, rows_in + rows_down)
    grad_attn = merged_out[:, :, :rows_in].reshape(block_rows, model_width)
    grad_hid = merged_out[:, :, rows_in:].reshape(block_rows, hidden)
    layer_output = (tokens + branches + full_vec[7] + full_vec[12]).astype(jnp.bfloat16)[None]
    gelu_pull = jax.vjp(gelu_exact, up_value)[1]
    grad_upval = gelu_pull(grad_hid)[0].astype(jnp.bfloat16)
    grad_heads = grad_attn.astype(jnp.bfloat16).reshape(block_rows, H, HD)
    delta_rows = jnp.sum(grad_heads.astype(jnp.float32) * attention, axis=-1)

    def key_turn(turn_index, states):
        pair_now, pair_grad, query_grad = states
        owner_index = (ctx_index - turn_index) % n_ctx
        key_pos = lax.dynamic_slice_in_dim(all_pos, owner_index * block_rows, block_rows)
        allowed = (key_pos[None, :] <= own_pos[:, None])[:, None, :]

        def key_compute(partials):
            grads_held, query_held = partials
            scores = (
                jnp.einsum("qhd,khd->qhk", q_rot, pair_now[0], preferred_element_type=jnp.float32)
                * score_scale
            )
            weights_now = jnp.where(allowed, jnp.exp(scores - log_sum[..., None]), 0.0)
            grad_prob = jnp.einsum(
                "qhd,khd->qhk", grad_heads, pair_now[1], preferred_element_type=jnp.float32
            )
            dscore = (weights_now * (grad_prob - delta_rows[..., None])).astype(jnp.bfloat16)
            query_held = (
                query_held
                + jnp.einsum(
                    "qhk,khd->qhd", dscore, pair_now[0], preferred_element_type=jnp.float32
                )
                * score_scale
            )
            key_term = (
                jnp.einsum("qhk,qhd->khd", dscore, q_rot, preferred_element_type=jnp.float32)
                * score_scale
            )
            value_term = jnp.einsum(
                "qhk,qhd->khd",
                weights_now.astype(jnp.bfloat16),
                grad_heads,
                preferred_element_type=jnp.float32,
            )
            return (grads_held + jnp.stack([key_term, value_term]), query_held)

        skipped = jnp.min(key_pos) > last_own
        pair_grad, query_grad = lax.cond(
            skipped, lambda partials: partials, key_compute, (pair_grad, query_grad)
        )
        pair_now = from_behind(pair_now, "ctx", 1)
        pair_grad = from_behind(pair_grad.astype(jnp.bfloat16), "ctx", 1).astype(pair_grad.dtype)
        return (pair_now, pair_grad, query_grad)

    loop_start = (
        jnp.stack([k_rot, v_low]),
        jnp.zeros((2, block_rows, H, HD), jnp.float32),
        jnp.zeros((block_rows, H, HD), jnp.float32),
    )
    loop_end = lax.fori_loop(0, n_ctx, key_turn, loop_start)
    pair_grad = loop_end[1]
    query_grad = loop_end[2]

    def turn_values(values):
        return rotate(values, cosine, sine)

    rot_pull = jax.vjp(turn_values, queries)[1]
    grad_proj = jnp.concatenate(
        [
            rot_pull(query_grad)[0].reshape(block_rows, model_width),
            rot_pull(pair_grad[0])[0].reshape(block_rows, model_width),
            pair_grad[1].reshape(block_rows, model_width),
        ],
        axis=1,
    ).astype(jnp.bfloat16)

    def back_inputs(pieces):
        shard_count = pieces[0].shape[0] // rows_in
        first_part = jnp.einsum(
            "tc,rc->tr", grad_proj, pieces[0], preferred_element_type=jnp.float32
        ).reshape(block_rows, shard_count, 1, rows_in)
        second_part = jnp.einsum(
            "tc,rc->tr", grad_upval, pieces[1], preferred_element_type=jnp.float32
        ).reshape(block_rows, shard_count, 1, rows_in)
        return jnp.concatenate([first_part, second_part], axis=2).reshape(
            block_rows, shard_count * 2 * rows_in
        )

    merged_in = back_inputs(lax.all_gather((qkv_low, up_low), ("ctx", "shard"), axis=0, tiled=True))
    merged_in = merged_in.reshape(block_rows, -1, 2, rows_in)
    grad_norm_one = merged_in[:, :, 0].reshape(block_rows, model_width)
    grad_norm_two = merged_in[:, :, 1].reshape(block_rows, model_width)
    norm_pull_one = jax.vjp(layer_norm, tokens, full_vec[0], full_vec[1])[1]
    norm_pull_two = jax.vjp(layer_norm, tokens, full_vec[2], full_vec[3])[1]
    back_one, gain_one, shift_one = norm_pull_one(grad_norm_one)
    back_two, gain_two, shift_two = norm_pull_two(grad_norm_two)
    grad_input = (grad_rows + back_one + back_two)[None]
    column_out = jnp.sum(grad_rows, axis=0)
    vector_terms = jnp.concatenate(
        [
            jnp.stack([gain_one, shift_one, gain_two, shift_two]),
            jnp.sum(grad_proj.astype(jnp.float32), axis=0).reshape(3, model_width),
            column_out[None],
            jnp.sum(grad_upval.astype(jnp.float32), axis=0).reshape(4, model_width),
            column_out[None],
        ],
        axis=0,
    )
    grad_vectors = lax.psum_scatter(vector_terms, ("ctx", "shard"), scatter_dimension=1, tiled=True)
    block_count = (rows_in + rows_down) * lax.axis_size(("ctx", "shard")) // (rows_in + rows_down)
    first_block = jnp.int32(0) // (rows_in + rows_down)
    left_attn = attn_low
    left_hid = lax.dynamic_slice_in_dim(
        hid_low, first_block * rows_down, block_count * rows_down, 1
    )
    dense_part = jnp.einsum(
        "tr,td->rd", left_attn, grad_low, preferred_element_type=jnp.float32
    ).reshape(block_count, rows_in, model_width)
    down_part = jnp.einsum(
        "tr,td->rd", left_hid, grad_low, preferred_element_type=jnp.float32
    ).reshape(block_count, rows_down, model_width)
    out_grads = lax.psum_scatter(
        jnp.concatenate([dense_part, down_part], axis=1).reshape(
            (rows_in + rows_down) * lax.axis_size(("ctx", "shard")), model_width
        ),
        ("ctx", "shard"),
        scatter_dimension=0,
        tiled=True,
    )
    left_one = normed_one
    left_two = normed_two
    in_grads = lax.psum_scatter(
        jnp.concatenate(
            [
                jnp.einsum("tr,tc->rc", left_one, grad_proj, preferred_element_type=jnp.float32),
                jnp.einsum("tr,tc->rc", left_two, grad_upval, preferred_element_type=jnp.float32),
            ],
            axis=1,
        ),
        ("ctx", "shard"),
        scatter_dimension=0,
        tiled=True,
    )
    grad_qkv = in_grads[:, : 3 * model_width]
    grad_up = in_grads[:, 3 * model_width :]
    grad_dense = out_grads[:rows_in]
    grad_down = out_grads[rows_in:]
    new_qkv, second_qkv = adam_step(w_qkv, grad_qkv, m_qkv, v_qkv, 4.0 * (D // 2) ** (-0.5), 0.1)
    new_dense, second_dense = adam_step(
        w_dense, grad_dense, m_dense, v_dense, 4.0 * (D // 32) ** (-0.5), 0.1
    )
    new_up, second_up = adam_step(w_up, grad_up, m_up, v_up, 4.0 * D ** (-0.5), 0.1)
    new_down, second_down = adam_step(w_down, grad_down, m_down, v_down, 4.0 * FF ** (-0.5), 0.1)
    new_vectors, second_vectors = adam_step(vectors, grad_vectors, m_vectors, v_vectors, 1.0, 0.0)
    return (
        layer_output,
        grad_input,
        grad_qkv,
        grad_dense,
        grad_up,
        grad_down,
        grad_vectors,
        second_qkv,
        second_dense,
        second_up,
        second_down,
        second_vectors,
        new_qkv,
        new_dense,
        new_up,
        new_down,
        new_vectors,
    )


MESH = pl.DeviceIdType.MESH
VMEM_BYTES = 62 * 1024 * 1024


def push(source, target, sent, arrived, **device):
    return pltpu.make_async_remote_copy(
        src_ref=source,
        dst_ref=target,
        send_sem=sent,
        recv_sem=arrived,
        device_id=device,
        device_id_type=MESH,
    )


class Spot:
    def __init__(self, n_plane, n_shard):
        self.n_plane, self.n_shard = n_plane, n_shard
        self.plane = lax.axis_index("plane")
        self.core = lax.axis_index("core")
        self.shard = lax.axis_index("shard")
        self.slot = self.core * n_shard + self.shard
        head = 2 * self.plane + self.core
        self.head_core = lax.div(head, n_shard)
        self.head_shard = lax.rem(head, n_shard)
        self.owner_plane = lax.div(self.slot, 2)
        self.owner_core = lax.rem(self.slot, 2)
        self.head_here = jnp.logical_and(self.slot == head, self.plane == self.shard)

    def group(self):
        for turn in range(1, 2 * self.n_shard):
            yield turn - 1, self.turned(turn)

    def turned(self, turn):
        core = lax.rem(self.core + turn // self.n_shard, 2)
        shard = lax.rem(self.shard + turn % self.n_shard, self.n_shard)
        return dict(core=core, shard=shard)

    def beside(self):
        across = self.plane + 1 - 2 * lax.rem(self.plane, 2)
        return across, lax.rem(self.plane + 2, 4), 3 - self.plane

    def along(self):
        for step in range(1, self.n_shard):
            yield step - 1, lax.rem(self.shard + step, self.n_shard)

    def planes(self):
        for step in range(1, self.n_plane):
            yield step - 1, lax.rem(self.plane + step, self.n_plane)

    def keeper(self):
        return dict(plane=self.shard, core=self.head_core, shard=self.head_shard)

    def owner(self):
        return dict(plane=self.owner_plane, core=self.owner_core, shard=self.plane)

    def greet(self, sender):
        barrier = pltpu.get_barrier_semaphore()
        count = 0
        for _, device in self.group():
            pl.semaphore_signal(barrier, inc=1, device_id=device, device_id_type=MESH)
            count += 1
        for _, plane in self.planes():
            pl.semaphore_signal(barrier, inc=1, device_id=dict(plane=plane), device_id_type=MESH)
            count += 1

        @pl.when(jnp.logical_not(self.head_here))
        def _():
            pl.semaphore_signal(barrier, inc=1, device_id=sender, device_id_type=MESH)
            pl.semaphore_wait(barrier, count + 1)

        @pl.when(self.head_here)
        def _():
            pl.semaphore_wait(barrier, count)


def turn_tables(pos_row, freq):
    n_pos = pos_row.shape[1]
    places = jnp.broadcast_to(pos_row.astype(jnp.float32), (n_pos, n_pos)).T
    phase = places * freq
    return jnp.cos(phase), jnp.sin(phase), places


def turn(head, cosine, sine):
    half = ROT // 2
    lanes = cosine.shape[1]
    front = head[:, :lanes]
    lane = lax.broadcasted_iota(jnp.int32, front.shape, 1)
    first = jnp.where(lane < half, -sine, 0.0)
    second = jnp.where((lane >= half) & (lane < ROT), sine, 0.0)
    turned = (
        front * cosine
        + pltpu.roll(front, lanes - half, 1) * first
        + pltpu.roll(front, half, 1) * second
    )
    return jnp.concatenate([turned, head[:, lanes:]], axis=1)


def dot(left, right, left_dim=1, right_dim=0):
    return lax.dot_general(
        left, right, (((left_dim,), (right_dim,)), ((), ())), preferred_element_type=jnp.float32
    )


class Spread:
    def __init__(self, spot, ref, size, sent, here):
        self.spot, self.ref, self.size, self.sent, self.here = spot, ref, size, sent, here
        self.across, self.along, self.diagonal = spot.beside()

    def rows(self, plane, part=None):
        size = self.size
        if part is None:
            return self.ref.at[pl.ds(pl.multiple_of(plane * size, size), size)]
        half = size // 2
        return self.ref.at[pl.ds(pl.multiple_of(plane * size + part * half, half), half)]

    def send(self, rows, place, plane):
        return push(rows, rows, self.sent.at[place], self.here.at[place], plane=plane)

    def first(self):
        own = self.rows(self.spot.plane)
        return [self.send(own, 0, self.across), self.send(own, 1, self.along)]

    def second(self):
        return [
            self.send(self.rows(self.along, 0), 2, self.across),
            self.send(self.rows(self.across, 1), 3, self.along),
        ]

    def start(self):
        for copy in self.first():
            copy.start()

    def relay(self):
        first, second = self.first(), self.second()
        first[1].wait_recv()
        second[0].start()
        first[0].wait_recv()
        second[1].start()

    def finish(self):
        for copy in self.second():
            copy.wait_recv()

    def finish_sends(self):
        for copy in self.first() + self.second():
            copy.wait_send()


class Gather:
    def __init__(self, spot, part, size, landed, sent, here):
        self.spot, self.part, self.size, self.landed = spot, part, size, landed
        self.sent, self.here = sent, here
        self.across, self.along, self.diagonal = spot.beside()

    def rows(self, plane, side):
        half = self.size // 2
        return self.part.at[pl.ds(pl.multiple_of(plane * self.size + side * half, half), half)]

    def send(self, rows, place, plane):
        return push(
            rows, self.landed.at[place], self.sent.at[place], self.here.at[place], plane=plane
        )

    def first(self):
        return [
            self.send(self.rows(self.diagonal, 0), 0, self.across),
            self.send(self.rows(self.diagonal, 1), 1, self.along),
            self.send(self.rows(self.across, 0), 2, self.across),
            self.send(self.rows(self.along, 1), 3, self.along),
        ]

    def second(self):
        return [
            self.send(self.rows(self.along, 0), 4, self.along),
            self.send(self.rows(self.across, 1), 5, self.across),
        ]

    def start(self):
        for copy in self.first():
            copy.start()

    def relay(self):
        first, second = self.first(), self.second()
        for side in range(2):
            first[side].wait_recv()
            held = self.rows(self.along if side == 0 else self.across, side)
            add_rows(held, [held, self.landed.at[side]], self.size // 2)
            second[side].start()

    def own(self):
        size = self.size
        return self.part.at[pl.ds(pl.multiple_of(self.spot.plane * size, size), size)]

    def finish(self):
        first, second = self.first(), self.second()
        half = self.size // 2
        for side in range(2):
            first[2 + side].wait_recv()
            second[side].wait_recv()
            held = self.rows(self.spot.plane, side)
            add_rows(held, [held, self.landed.at[2 + side], self.landed.at[4 + side]], half)

    def finish_sends(self):
        for copy in self.first() + self.second():
            copy.wait_send()


class RowSum:
    def __init__(self, spot, part, landed, sent, here):
        self.spot, self.part, self.landed = spot, part, landed
        self.sent, self.here = sent, here

    def rows(self, shard):
        return self.part.at[shard]

    def place(self, side, at, shard):
        if side == 0:
            return shard
        return jnp.where(shard == at, self.spot.n_shard, shard)

    def hop(self, side, shard):
        spot = self.spot
        to = spot.shard + (1 if side == 0 else -1)
        return push(
            self.rows(shard),
            self.landed.at[self.place(side, to, shard)],
            self.sent.at[side, shard],
            self.here.at[side, shard],
            shard=to,
        )

    def wait(self, side, shard):
        spot = self.spot
        push(
            self.rows(shard),
            self.landed.at[self.place(side, spot.shard, shard)],
            self.sent.at[side, shard],
            self.here.at[side, shard],
            shard=spot.shard,
        ).wait_recv()

    def start(self):
        spot, last = self.spot, self.spot.n_shard - 1
        for side in range(2):

            @pl.when(spot.shard == (0 if side == 0 else last))
            def _():
                for step in range(last):
                    self.hop(side, last - step if side == 0 else step).start()

    def relay(self, turn):
        spot, last = self.spot, self.spot.n_shard - 1
        for side in range(2):
            depth = spot.shard if side == 0 else last - spot.shard
            shard = last - turn + spot.shard if side == 0 else turn - last + spot.shard

            @pl.when(jnp.logical_and(depth >= 1, depth <= turn))
            def _():
                self.wait(side, shard)
                held = self.rows(shard)
                came = self.landed.at[self.place(side, spot.shard, shard)]
                add_rows(held, [held, came], held.shape[0])
                self.hop(side, shard).start()

    def finish(self, target):
        spot, last = self.spot, self.spot.n_shard - 1
        held = self.rows(spot.shard)
        first = self.landed.at[self.place(0, spot.shard, spot.shard)]
        second = self.landed.at[self.place(1, spot.shard, spot.shard)]

        @pl.when(spot.shard >= 1)
        def _():
            self.wait(0, spot.shard)

        @pl.when(spot.shard < last)
        def _():
            self.wait(1, spot.shard)

        @pl.when(spot.shard == 0)
        def _():
            add_rows(target, [held, second], held.shape[0])

        @pl.when(spot.shard == last)
        def _():
            add_rows(target, [held, first], held.shape[0])

        @pl.when(jnp.logical_and(spot.shard >= 1, spot.shard < last))
        def _():
            add_rows(target, [held, first, second], held.shape[0])

    def finish_sends(self):
        spot = self.spot
        for shard in range(spot.n_shard):
            for side in range(2):

                @pl.when(spot.shard < shard if side == 0 else spot.shard > shard)
                def _():
                    self.hop(side, shard).wait_send()


class Chain:
    def __init__(self, spot, ref, block, sent, here, pair_sent, pair_here):
        self.spot, self.ref, self.block = spot, ref, block
        self.sent, self.here = sent, here
        self.pair_sent, self.pair_here = pair_sent, pair_here

    def rows(self, shard, core):
        start = pl.multiple_of((shard * 2 + core) * self.block, self.block)
        return self.ref.at[pl.ds(start, self.block)]

    def hop(self, side, dist):
        spot = self.spot
        sign = 1 if side == 0 else -1
        rows = self.rows(spot.shard - sign * dist, spot.core)
        return push(
            rows, rows, self.sent.at[side, dist], self.here.at[side, dist], shard=spot.shard + sign
        )

    def pair(self, side, dist):
        spot = self.spot
        sign = 1 if side == 0 else -1
        rows = self.rows(spot.shard - sign * dist, spot.core)
        return push(
            rows,
            rows,
            self.pair_sent.at[side, dist],
            self.pair_here.at[side, dist],
            core=1 - spot.core,
        )

    def holds(self, side, dist):
        spot = self.spot
        return spot.shard >= dist if side == 0 else spot.shard + dist < spot.n_shard

    def goes(self, side, dist):
        spot = self.spot
        more = spot.shard + 1 < spot.n_shard if side == 0 else spot.shard >= 1
        return jnp.logical_and(self.holds(side, dist), more)

    def start(self):
        for side in range(2):

            @pl.when(self.goes(side, 0))
            def _():
                self.hop(side, 0).start()

        self.pair(0, 0).start()

    def step(self, dist):
        for side in range(2):

            @pl.when(self.holds(side, dist))
            def _():
                self.hop(side, dist - 1).wait_recv()
                if dist + 1 < self.spot.n_shard:

                    @pl.when(self.goes(side, dist))
                    def _():
                        self.hop(side, dist).start()

                self.pair(side, dist).start()

    def finish_pairs(self):
        self.pair(0, 0).wait_recv()
        for dist in range(1, self.spot.n_shard):
            for side in range(2):

                @pl.when(self.holds(side, dist))
                def _():
                    self.pair(side, dist).wait_recv()

    def finish_sends(self):
        self.pair(0, 0).wait_send()
        for side in range(2):
            for dist in range(self.spot.n_shard - 1):

                @pl.when(self.goes(side, dist))
                def _():
                    self.hop(side, dist).wait_send()

            for dist in range(1, self.spot.n_shard):

                @pl.when(self.holds(side, dist))
                def _():
                    self.pair(side, dist).wait_send()


def forward_kernel(
    n_plane,
    n_shard,
    x_ref,
    dy_ref,
    pos_ref,
    vec_ref,
    freq_ref,
    wq_ref,
    wu_ref,
    wd_ref,
    wo_ref,
    x_out,
    dy_out,
    one_out,
    two_out,
    hid_out,
    gup_out,
    back_out,
    wq_out,
    wu_out,
    wd_out,
    wo_out,
    vec_out,
    moments_out,
    x_all,
    dy_all,
    one,
    two,
    wq_all,
    wu_all,
    wd_all,
    wo_all,
    vec_all,
    pos_all,
    full_vec,
    wu_raw,
    wd_raw,
    wo_raw,
    wq_cut,
    wu_cut,
    wo_cut,
    to_heads,
    heads,
    from_heads,
    back,
    grad_k,
    grad_v,
    cos_head,
    sin_head,
    place_head,
    cos_row,
    sin_row,
    key_row,
    probs,
    slope,
    attention,
    moments,
    loads,
    stores,
    local,
    x_sent,
    x_here,
    x_pair_sent,
    x_pair_here,
    dy_sent,
    dy_here,
    dy_pair_sent,
    dy_pair_here,
    pos_sent,
    pos_here,
    cols_sent,
    cols_here,
    flat_sent,
    flat_here,
    spread_sent,
    spread_here,
    swap_sent,
    swap_here,
    head_sent,
    head_here,
):
    spot = Spot(n_plane, n_shard)
    plane, core, shard, slot = spot.plane, spot.core, spot.shard, spot.slot
    f32, bf16 = jnp.float32, jnp.bfloat16
    block = x_ref.shape[0]
    pair = 2 * block
    n_slice = 2 * n_shard
    rows_in, rows_down = wq_ref.shape[0], wd_ref.shape[0]
    width = x_ref.shape[1]
    n_group = n_slice * block

    def piece(ref, at, size):
        return ref.at[pl.ds(pl.multiple_of(at * size, size), size)]

    chain_x = Chain(spot, x_all, block, x_sent, x_here, x_pair_sent, x_pair_here)
    chain_dy = Chain(spot, dy_all, block, dy_sent, dy_here, dy_pair_sent, dy_pair_here)

    raw = [
        pltpu.make_async_copy(source, held, loads.at[place])
        for place, (source, held) in enumerate(
            [
                (wq_ref, wu_raw.at[:, pl.ds(0, wq_ref.shape[1])]),
                (wu_ref, wu_raw),
                (wd_ref, wd_raw),
                (wo_ref, wo_raw),
                (x_ref, chain_x.rows(shard, core)),
                (dy_ref, chain_dy.rows(shard, core)),
                (pos_ref, pos_all.at[shard]),
                (vec_ref, vec_all.at[plane, slot]),
            ]
        )
    ]
    for place, copy in enumerate(raw):
        if place != 1:
            copy.start()
    spot.greet(spot.owner())

    index = plane * n_slice + slot
    wq_own = piece(wq_all, index, rows_in)
    wu_own = piece(wu_all, index, rows_in)

    def to_group(place, source, target):
        return [
            push(
                source(device["core"] * n_shard + device["shard"]),
                target,
                cols_sent.at[place, turn_at],
                cols_here.at[place, turn_at],
                **device,
            )
            for turn_at, device in spot.group()
        ]

    cols_q = to_group(0, lambda to: wq_cut.at[to], wq_own)
    cols_u = to_group(1, lambda to: wu_cut.at[to], wu_own)
    cols_v = to_group(2, lambda to: vec_all.at[plane, slot], vec_all.at[plane, slot])

    def to_planes(place, ref):
        return [
            push(ref, ref, flat_sent.at[place, turn_at], flat_here.at[place, turn_at], plane=to)
            for turn_at, to in spot.planes()
        ]

    group_rows = n_slice * rows_in
    spread_d = Spread(spot, wd_all, rows_down, spread_sent.at[0], spread_here.at[0])
    spread_q = Spread(spot, wq_all, group_rows, spread_sent.at[1], spread_here.at[1])
    spread_u = Spread(spot, wu_all, group_rows, spread_sent.at[2], spread_here.at[2])
    flat_v = to_planes(0, vec_all.at[plane])
    flat_o = to_planes(1, piece(wo_all, plane, rows_in))
    pos_push = [
        push(
            pos_all.at[shard],
            pos_all.at[shard],
            pos_sent.at[turn_at],
            pos_here.at[turn_at],
            shard=to,
        )
        for turn_at, to in spot.along()
    ]

    raw[6].wait()
    raw[7].wait()
    for copy in cols_v + pos_push:
        copy.start()

    raw[4].wait()
    chain_x.start()
    raw[0].wait()
    for to in range(n_slice):
        for part in range(3):
            wq_cut[to, :, part * HD : (part + 1) * HD] = wu_raw[
                :, part * width + to * HD : part * width + (to + 1) * HD
            ].astype(bf16)
    raw[1].start()
    for copy in cols_q:
        copy.start()
    keep_q = pltpu.make_async_copy(wq_cut.at[slot], wq_own, local.at[0])
    keep_q.start()
    for copy in cols_v:
        copy.wait_recv()
    for copy in flat_v:
        copy.start()
    raw[2].wait()

    down_at = plane * rows_down

    @pl.loop(0, rows_down // 32)
    def _(step):
        at = pl.multiple_of(step * 32, 32)
        wd_all[pl.ds(pl.multiple_of(down_at + at, 32), 32), :] = wd_raw[pl.ds(at, 32), :].astype(bf16)

    spread_d.start()
    raw[1].wait()
    for to in range(n_slice):
        for part in range(n_plane):
            wu_cut[to, :, part * rows_down : (part + 1) * rows_down] = wu_raw[
                :, part * width + to * rows_down : part * width + (to + 1) * rows_down
            ].astype(bf16)
    keep_u = pltpu.make_async_copy(wu_cut.at[slot], wu_own, local.at[1])
    keep_u.start()
    raw[3].wait()
    wo_cut[...] = wo_raw[...].astype(bf16)
    head_rows = piece(wo_all, shard, rows_in)
    to_head = push(wo_cut, head_rows, head_sent, head_here, **spot.keeper())
    own_head = pltpu.make_async_copy(wo_cut, head_rows, head_sent)

    @pl.when(spot.head_here)
    def _():
        own_head.start()

    @pl.when(jnp.logical_not(spot.head_here))
    def _():
        to_head.start()

    for copy in pos_push:
        copy.wait_recv()
    freq = freq_ref[...]
    own_blocks = 2 * plane

    @pl.loop(0, n_shard)
    def _(seq):
        for half in range(2):
            at = pl.ds(pl.multiple_of(seq * pair + half * block, block), block)
            cosine, sine, _ = turn_tables(pos_all[seq, pl.ds(own_blocks + half, 1), :], freq)
            cos_row[at, :] = cosine
            sin_row[at, :] = sine

    raw[5].wait()
    for copy in flat_v:
        copy.wait_recv()
    n_vec, lanes = vec_all.shape[2:]
    lane = lax.broadcasted_iota(jnp.int32, (n_vec, lanes), 1)
    for p in range(n_plane):
        for t in range(0, n_slice, 2):
            at = (p * n_slice + t) * (lanes // 2)
            full_vec[:, at : at + lanes] = jnp.where(
                lane < lanes // 2, vec_all[p, t], pltpu.roll(vec_all[p, t + 1], lanes // 2, 1)
            )
    save_vec = pltpu.make_async_copy(full_vec, vec_out, stores.at[0])
    save_vec.start()

    def norm_rows(seq):
        @pl.loop(0, pair // 32)
        def _(step):
            at = pl.ds(pl.multiple_of(seq * pair + step * 32, 32), 32)
            tokens = x_all[at, :].astype(f32)
            mean = jnp.mean(tokens, axis=-1, keepdims=True)
            center = tokens - mean
            scale = lax.rsqrt(jnp.mean(center * center, axis=-1, keepdims=True) + 1e-05)
            lane = lax.broadcasted_iota(jnp.int32, (32, moments.shape[1]), 1)
            moments[at, :] = jnp.where(lane < 1, mean, scale)
            hat = center * scale
            one[at, :] = (hat * full_vec[0:1, :] + full_vec[1:2, :]).astype(bf16)
            two[at, :] = (hat * full_vec[2:3, :] + full_vec[3:4, :]).astype(bf16)

    def norm_came(dist):
        for side in range(2):

            @pl.when(chain_x.holds(side, dist))
            def _():
                chain_x.pair(side, dist).wait_recv()
                norm_rows(shard - dist if side == 0 else shard + dist)

    chain_x.step(1)
    for copy in cols_u:
        copy.start()
    chain_x.pair(0, 0).wait_recv()
    norm_rows(shard)
    spread_d.relay()
    keep_q.wait()
    for copy in cols_q:
        copy.wait_recv()
    spread_q.start()
    norm_came(1)
    chain_x.step(2)
    chain_dy.start()
    spread_q.relay()
    norm_came(2)
    keep_u.wait()
    for copy in cols_u:
        copy.wait_recv()
    spread_u.start()

    @pl.loop(0, n_plane)
    def _(part):
        for half in range(2):
            at = pl.ds(pl.multiple_of(part * pair + half * block, block), block)
            cosine, sine, places = turn_tables(pos_all[plane, pl.ds(2 * part + half, 1), :], freq)
            cos_head[at, :] = cosine
            sin_head[at, :] = sine
            place_head[at, :] = places

    for at in range(pos_all.shape[1]):
        key_row[:, at * block : (at + 1) * block] = pos_all[plane, pl.ds(at, 1), :].astype(f32)

    for dist in range(3, n_shard):
        chain_x.step(dist)

    @pl.when(spot.head_here)
    def _():
        own_head.wait()

    @pl.when(jnp.logical_not(spot.head_here))
    def _():
        to_head.wait_recv()

    for copy in flat_o:
        copy.start()


    chain_dy.step(1)
    for dist in range(3, n_shard):
        norm_came(dist)
    save_x = pltpu.make_async_copy(x_all, x_out, stores.at[1])
    save_x.start()
    spread_u.relay()
    chain_dy.step(2)
    save_moments = pltpu.make_async_copy(moments, moments_out, stores.at[12])
    save_moments.start()
    save_one = pltpu.make_async_copy(one, one_out, stores.at[2])
    save_one.start()
    save_two = pltpu.make_async_copy(two, two_out, stores.at[3])
    save_two.start()

    spread_q.finish()
    save_wq = pltpu.make_async_copy(wq_all, wq_out, stores.at[4])
    save_wq.start()
    head_lanes = pl.ds(pl.multiple_of(slot * HD, HD), HD)

    def swap(place, source, target, cols, to, turn_at):
        def piece_of(ref, at):
            return ref.at[pl.ds(pl.multiple_of(at * pair, pair), pair), cols]

        return push(
            piece_of(source, to),
            piece_of(target, plane),
            swap_sent.at[place, turn_at - 1],
            swap_here.at[place, turn_at - 1],
            plane=to,
        )

    def keep_own(place, source, target, cols):
        at = pl.ds(pl.multiple_of(plane * pair, pair), pair)
        return pltpu.make_async_copy(source.at[at, cols], target.at[at, cols], local.at[place])

    def swaps(place, source, target, cols):
        return [
            swap(place, source, target, cols, lax.rem(plane + turn_at, n_plane), turn_at)
            for turn_at in range(1, n_plane)
        ]

    qkv_cols = pl.ds(0, 3 * HD)
    q_cols, kv_cols, o_cols = pl.ds(0, HD), pl.ds(HD, 2 * HD), pl.ds(3 * HD, HD)

    for step in range(2):
        at = slice(step * 2 * pair, (step + 1) * 2 * pair)
        heads_now = dot(one[at, :], wq_all[...])
        for part in range(3):
            cols = slice(part * HD, (part + 1) * HD)
            value = heads_now[:, cols] + full_vec[4 + part : 5 + part, head_lanes]
            if part < 2:
                value = turn(value, cos_row[at, :], sin_row[at, :])
            to_heads[at, cols] = value.astype(bf16)

    for copy in swaps(0, to_heads, heads, qkv_cols):
        copy.start()
    keep_qkv = keep_own(2, to_heads, heads, qkv_cols)
    keep_qkv.start()

    spread_u.finish()
    save_wu = pltpu.make_async_copy(wu_all, wu_out, stores.at[8])
    save_wu.start()
    save_one.wait()
    up_lanes = pl.ds(pl.multiple_of(slot * rows_down, rows_down), rows_down)
    n_hid = n_plane * rows_down

    def hidden_rows(step):
        at = pl.ds(pl.multiple_of(step * pair, pair), pair)
        hidden = dot(two[at, :], wu_all[...])
        for part in range(n_plane):
            cols = slice(part * rows_down, (part + 1) * rows_down)
            value = hidden[:, cols] + full_vec[8 + part : 9 + part, up_lanes]
            half = 0.5 + 0.5 * lax.erf(value * 0.7071067811865476)
            slope[at, cols] = half + value * (0.3989422804014327 * jnp.exp(-0.5 * value * value))
            one[at, cols] = (value * half).astype(bf16)

    @pl.loop(0, n_shard // 2)
    def _(step):
        hidden_rows(step)

    for dist in range(3, n_shard):
        chain_dy.step(dist)

    @pl.loop(n_shard // 2, n_shard)
    def _(step):
        hidden_rows(step)

    save_hid = pltpu.make_async_copy(one.at[:, 0:n_hid], hid_out, stores.at[9])
    save_hid.start()

    chain_dy.finish_pairs()
    save_dy = pltpu.make_async_copy(dy_all, dy_out, stores.at[5])
    save_dy.start()
    for copy in flat_o:
        copy.wait_recv()
    save_wo = pltpu.make_async_copy(wo_all, wo_out, stores.at[6])
    save_wo.start()

    @pl.loop(0, 2)
    def _(step):
        at = pl.ds(pl.multiple_of(step * 2 * pair, 2 * pair), 2 * pair)
        to_heads[at, 3 * HD : 4 * HD] = dot(dy_all[at, :], wo_all[...], 1, 1).astype(bf16)

    for copy in swaps(1, to_heads, heads, o_cols):
        copy.start()
    keep_o = keep_own(3, to_heads, heads, o_cols)
    keep_o.start()

    grad_k[...] = jnp.zeros_like(grad_k)
    grad_v[...] = jnp.zeros_like(grad_v)
    scale = HD ** (-0.5)
    keep_qkv.wait()
    for copy in swaps(0, to_heads, heads, qkv_cols):
        copy.wait_recv()

    @pl.loop(0, n_plane)
    def _(part):
        at = pl.ds(pl.multiple_of(part * pair, pair), pair)
        places = place_head[at, 0:1]
        scores = dot(heads[at, 0:HD], heads[:, HD : 2 * HD], 1, 1) * scale
        scores = jnp.where(key_row[...] <= places, scores, -1e30)
        weights = jnp.exp(scores - jnp.max(scores, axis=-1, keepdims=True))
        share = weights / jnp.sum(weights, axis=-1, keepdims=True)
        probs[at, :] = share
        value = dot(share.astype(bf16), heads[:, 2 * HD : 3 * HD])
        attention[at, :] = value
        from_heads[at, 3 * HD : 4 * HD] = value.astype(bf16)

    for copy in swaps(2, from_heads, back, o_cols):
        copy.start()

    keep_o.wait()
    for copy in swaps(1, to_heads, heads, o_cols):
        copy.wait_recv()

    @pl.loop(0, n_plane)
    def _(step):
        turn_at = lax.rem(step + 1, n_plane)
        part = lax.rem(plane + turn_at, n_plane)
        at = pl.ds(pl.multiple_of(part * pair, pair), pair)
        grad_out = heads[at, 3 * HD : 4 * HD]
        delta = jnp.sum(grad_out.astype(f32) * attention[at, :], axis=-1, keepdims=True)
        grad_prob = dot(grad_out, heads[:, 2 * HD : 3 * HD], 1, 1)
        share = probs[at, :]
        dscore = (share * (grad_prob - delta)).astype(bf16)
        grad_q = dot(dscore, heads[:, HD : 2 * HD]) * scale
        from_heads[at, 0:HD] = turn(grad_q, cos_head[at, :], -sin_head[at, :]).astype(bf16)

        @pl.when(turn_at > 0)
        def _():
            swap(3, from_heads, back, q_cols, part, turn_at).start()

        grad_k[...] += dot(dscore, heads[at, 0:HD], 0, 0)
        grad_v[...] += dot(share.astype(bf16), grad_out, 0, 0)

    @pl.loop(0, n_plane)
    def _(step):
        turn_at = lax.rem(step + 1, n_plane)
        part = lax.rem(plane + turn_at, n_plane)
        at = pl.ds(pl.multiple_of(part * pair, pair), pair)
        turned = turn(grad_k[at, :] * scale, cos_head[at, :], -sin_head[at, :])
        from_heads[at, HD : 2 * HD] = turned.astype(bf16)
        from_heads[at, 2 * HD : 3 * HD] = grad_v[at, :].astype(bf16)

        @pl.when(turn_at > 0)
        def _():
            swap(4, from_heads, back, kv_cols, part, turn_at).start()

    keep_back = keep_own(2, from_heads, back, pl.ds(0, 4 * HD))
    keep_back.start()

    spread_d.finish()
    save_wd = pltpu.make_async_copy(wd_all, wd_out, stores.at[7])
    save_wd.start()

    @pl.loop(0, n_shard)
    def _(step):
        at = pl.ds(pl.multiple_of(step * pair, pair), pair)
        one[at, n_hid : 2 * n_hid] = (dot(dy_all[at, :], wd_all[...], 1, 1) * slope[at, :]).astype(
            bf16
        )

    save_gup = pltpu.make_async_copy(one.at[:, n_hid : 2 * n_hid], gup_out, stores.at[10])
    save_gup.start()
    keep_back.wait()
    again = (
        swaps(2, from_heads, back, o_cols)
        + swaps(3, from_heads, back, q_cols)
        + swaps(4, from_heads, back, kv_cols)
    )
    for copy in again:
        copy.wait_recv()
    save_back = pltpu.make_async_copy(back, back_out, stores.at[11])
    save_back.start()

    @pl.when(jnp.logical_not(spot.head_here))
    def _():
        to_head.wait_send()

    chain_x.finish_sends()
    chain_dy.finish_sends()
    for copy in cols_q + cols_u + cols_v + pos_push:
        copy.wait_send()
    for spread in [spread_d, spread_q, spread_u]:
        spread.finish_sends()
    again += swaps(0, to_heads, heads, qkv_cols) + swaps(1, to_heads, heads, o_cols)
    for copy in flat_v + flat_o + again:
        copy.wait_send()
    for copy in [
        save_vec,
        save_moments,
        save_x,
        save_two,
        save_wq,
        save_dy,
        save_wo,
        save_wd,
        save_wu,
        save_hid,
        save_gup,
        save_back,
    ]:
        copy.wait()


def forward_all(n_plane, n_shard, x, dy, pos, vec, freq, wq, wu, wd, wo):
    f32, bf16 = jnp.float32, jnp.bfloat16
    n_slice = 2 * n_shard
    block, width = x.shape
    rows_in, rows_down = wq.shape[0], wd.shape[0]
    group = n_slice * block
    n_hid = n_plane * rows_down
    cols_q = 3 * HD
    n_vec, lanes = vec.shape
    dma = pltpu.SemaphoreType.DMA
    vmem = pltpu.VMEM
    shape = jax.ShapeDtypeStruct
    anywhere = pl.BlockSpec(memory_space=pl.ANY)
    far, near = n_shard - 1, n_plane - 1
    return pl.pallas_call(
        partial(forward_kernel, n_plane, n_shard),
        out_shape=[
            shape((group, width), bf16),
            shape((group, width), bf16),
            shape((group, width), bf16),
            shape((group, width), bf16),
            shape((group, n_hid), bf16),
            shape((group, n_hid), bf16),
            shape((group, 4 * HD), bf16),
            shape((width, cols_q), bf16),
            shape((width, n_hid), bf16),
            shape((n_hid, width), bf16),
            shape((HD, width), bf16),
            shape((n_vec, width), f32),
            shape((group, block), f32),
        ],
        in_specs=[anywhere] * 4 + [pl.BlockSpec(memory_space=vmem)] + [anywhere] * 4,
        out_specs=[anywhere] * 13,
        scratch_shapes=[
            vmem((group, width), bf16),
            vmem((group, width), bf16),
            vmem((group, width), bf16),
            vmem((group, width), bf16),
            vmem((width, cols_q), bf16),
            vmem((width, n_hid), bf16),
            vmem((n_hid, width), bf16),
            vmem((HD, width), bf16),
            vmem((n_plane, n_slice, n_vec, lanes), f32),
            vmem((n_shard, *pos.shape), jnp.int32),
            vmem((n_vec, width), f32),
            vmem(wu.shape, f32),
            vmem(wd.shape, f32),
            vmem(wo.shape, f32),
            vmem((n_slice, rows_in, cols_q), bf16),
            vmem((n_slice, rows_in, n_hid), bf16),
            vmem(wo.shape, bf16),
            vmem((group, 4 * HD), bf16),
            vmem((group, 4 * HD), bf16),
            vmem((group, 4 * HD), bf16),
            vmem((group, 4 * HD), bf16),
            vmem((group, HD), f32),
            vmem((group, HD), f32),
            *([vmem((group, block), f32)] * 5),
            vmem((1, group), f32),
            vmem((group, group), f32),
            vmem((group, n_hid), f32),
            vmem((group, HD), f32),
            vmem((group, block), f32),
            dma((8,)),
            dma((13,)),
            dma((4,)),
            *([dma((2, n_shard))] * 8),
            dma((far,)),
            dma((far,)),
            dma((3, n_slice - 1)),
            dma((3, n_slice - 1)),
            dma((2, near)),
            dma((2, near)),
            dma((3, 4)),
            dma((3, 4)),
            dma((5, near)),
            dma((5, near)),
            dma,
            dma,
        ],
        compiler_params=pltpu.CompilerParams(
            collective_id=0, has_side_effects=True, vmem_limit_bytes=VMEM_BYTES
        ),
        name="forward_all",
    )(x, dy, pos, vec, freq, wq, wu, wd, wo)


def add_rows(target, terms, rows):
    columns = target.shape[1]
    chunk = min(rows, 64 if columns <= 1024 else 32)

    @pl.loop(0, rows // chunk)
    def _(step):
        at = pl.ds(pl.multiple_of(step * chunk, chunk), chunk)
        for start in range(0, columns, 256):
            cols = slice(start, start + 256)
            total = terms[0][at, cols].astype(jnp.float32)
            for term in terms[1:]:
                total = total + term[at, cols].astype(jnp.float32)
            target[at, cols] = total.astype(target.dtype)


def backward_kernel(
    n_plane,
    n_shard,
    x_ref,
    dy_ref,
    one_ref,
    two_ref,
    hid_ref,
    gup_ref,
    back_ref,
    wq_ref,
    wu_ref,
    wd_ref,
    wo_ref,
    vec_ref,
    moments_ref,
    out_sum,
    hat_sum,
    dq_sum,
    du_sum,
    dd_sum,
    do_sum,
    vec_sum,
    big_one,
    big_two,
    big_three,
    x_rows,
    hid,
    gup,
    back,
    wq,
    wo,
    vec,
    moments,
    rows_part,
    other_half,
    theirs,
    parts,
    q_part,
    u_part,
    o_part,
    v_part,
    q_in,
    u_in,
    d_in,
    o_in,
    v_in,
    o_mid,
    v_mid,
    v_end,
    loads,
    local,
    pair_sent,
    pair_here,
    rows_sent,
    rows_here,
    flat_sent,
    flat_here,
    sum_sent,
    sum_here,
    cols_sent,
    cols_here,
    head_sent,
    head_here,
    x_sem,
    free,
):
    spot = Spot(n_plane, n_shard)
    plane, core, shard, slot = spot.plane, spot.core, spot.shard, spot.slot
    f32, bf16 = jnp.float32, jnp.bfloat16
    n_slice = 2 * n_shard
    n_group, width = dy_ref.shape
    block = n_group // n_slice
    pair = 2 * block
    rows_down = width // n_slice
    cols_q = 3 * HD
    n_hid = hid_ref.shape[1]
    rows_plane = width // n_plane
    rows_in = rows_plane // n_slice

    def load(source, target, place):
        copy = pltpu.make_async_copy(source, target, loads.at[place])
        copy.start()
        return copy

    def plane_rows(ref, at):
        return ref.at[pl.ds(pl.multiple_of(at * pair, pair), pair)]

    load_two = load(two_ref, big_three, 0)
    load_hid = load(hid_ref, hid, 1)
    load_dy = load(dy_ref, big_one, 2)
    load_back = load(back_ref, back, 3)
    load_wo = load(wo_ref, wo, 4)
    load_wd = load(wd_ref, big_two, 5)
    load_gup = load(gup_ref, gup, 7)
    load_wq = load(wq_ref, wq, 8)
    load_vec = load(vec_ref, vec, 9)
    load_moments = load(moments_ref, moments, 10)
    spot.greet(spot.keeper())

    def flat(place, source, target):
        return [
            push(
                source(to),
                target.at[turn_at],
                flat_sent.at[place, turn_at],
                flat_here.at[place, turn_at],
                plane=to,
            )
            for turn_at, to in spot.planes()
        ]

    def at_plane(ref, size):
        return lambda to: ref.at[pl.ds(pl.multiple_of(to * size, size), size)]

    sum_u = Gather(spot, u_part, rows_plane, u_in, sum_sent.at[0], sum_here.at[0])
    sum_q = Gather(spot, q_part, rows_plane, q_in, sum_sent.at[1], sum_here.at[1])
    sum_d = Gather(spot, big_two, rows_down, d_in, sum_sent.at[2], sum_here.at[2])
    flat_o = flat(0, at_plane(o_part, rows_in), o_in)
    flat_v = flat(
        1,
        lambda to: v_part.at[:, pl.ds(pl.multiple_of(to * rows_plane, rows_plane), rows_plane)],
        v_in,
    )

    def weight_grad(left, right, target, columns):
        @pl.loop(0, left.shape[1] // 512)
        def _(step):
            at = pl.ds(pl.multiple_of(step * 512, 512), 512)
            turned = left[:, at].T
            for start in range(0, columns, n_group):
                cols = slice(start, min(start + n_group, columns))
                target[at, cols] = dot(turned, right[:, cols]).astype(bf16)

    sums = [
        RowSum(spot, rows_part.at[place], parts.at[place], rows_sent.at[place], rows_here.at[place])
        for place in range(2)
    ]

    def pair_push(place, seq):
        return push(
            other_half.at[seq],
            theirs.at[seq],
            pair_sent.at[place, seq],
            pair_here.at[place, seq],
            core=1 - core,
        )

    def put(place, seq, cols, total):
        first, second = total[:block], total[block:]
        rows_part[place, seq, :, cols] = jnp.where(core == 0, first, second).astype(bf16)
        other_half[seq, :, cols] = jnp.where(core == 0, second, first).astype(bf16)

    def add_pairs(place):
        @pl.loop(0, n_shard)
        def _(seq):
            pair_push(place, seq).wait_recv()
            held = rows_part.at[place, seq]
            add_rows(held, [held, theirs.at[seq]], block)

        sums[place].start()

    def add_shards(place, target):
        sums[place].finish(sums[place].rows(shard))
        copy = pltpu.make_async_copy(sums[place].rows(shard), target, local.at[2, 1 + place])
        copy.start()
        return copy

    def regroup(place, held, target, wide):
        base = pl.multiple_of(plane * rows_plane, rows_plane)
        parts_here = held.shape[1] // wide

        def rows(to, part):
            start = pl.multiple_of(base + to * rows_in, rows_in)
            return held.at[pl.ds(start, rows_in), pl.ds(part * wide, wide)]

        def lands(part):
            start = pl.multiple_of(part * width + slot * wide, wide)
            return target.at[:, pl.ds(start, wide)]

        copies = []
        for turn_at, device in spot.group():
            to = device["core"] * n_shard + device["shard"]
            for part in range(parts_here):
                copies.append(
                    push(
                        rows(to, part),
                        lands(part),
                        cols_sent.at[place, turn_at, part],
                        cols_here.at[place, turn_at, part],
                        **device,
                    )
                )
        keeps = [
            pltpu.make_async_copy(rows(slot, part), lands(part), local.at[place, part])
            for part in range(parts_here)
        ]
        for copy in copies + keeps:
            copy.start()
        return copies, keeps

    load_two.wait()
    load_gup.wait()
    weight_grad(big_three, gup, u_part, n_hid)
    sum_u.start()

    load_wu = [
        load(
            wu_ref.at[pl.ds(part * n_group, n_group)],
            big_three.at[:, pl.ds(part * n_hid, n_hid)],
            11 + part,
        )
        for part in range(width // n_group)
    ]

    load_hid.wait()
    load_back.wait()
    load_wo.wait()
    load_wd.wait()

    @pl.loop(0, n_shard)
    def _(seq):
        at = pl.ds(pl.multiple_of(seq * pair, pair), pair)
        for start in range(0, width, n_group):
            cols = slice(start, start + n_group)
            total = dot(back[at, cols_q : cols_q + HD], wo[:, cols])
            put(0, seq, cols, total + dot(hid[at, :], big_two[:, cols]))
        pair_push(0, seq).start()

    add_pairs(0)
    pl.semaphore_signal(free, inc=1, device_id=dict(core=1 - core), device_id_type=MESH)

    def x_load(seq):
        return pltpu.make_async_copy(plane_rows(x_ref, seq), x_rows, x_sem)

    x_load(0).start()
    v_part[...] = jnp.zeros_like(v_part)
    load_wq.wait()
    load_vec.wait()
    for copy in load_wu:
        copy.wait()
    load_moments.wait()
    for seq in range(n_shard):
        pair_push(0, seq).wait_send()
    pl.semaphore_wait(free, 1)

    def norm_rows(seq):
        at = pl.ds(pl.multiple_of(seq * pair, pair), pair)
        mean, scale = moments[at, 0:1], moments[at, 1:2]
        for start in range(0, width, 512):
            cols = slice(start, start + 512)
            up_rows = slice(start % n_group, start % n_group + 512)
            up_cols = slice(start // n_group * n_hid, (start // n_group + 1) * n_hid)
            grad_one = dot(back[at, 0:cols_q], wq[cols, :], 1, 1)
            grad_two = dot(gup[at, :], big_three[up_rows, up_cols], 1, 1)
            if start == 0:
                x_load(seq).wait()
            hat = (x_rows[:, cols].astype(f32) - mean) * scale
            v_part[0:1, cols] += jnp.sum(grad_one * hat, axis=0, keepdims=True)
            v_part[1:2, cols] += jnp.sum(grad_one, axis=0, keepdims=True)
            v_part[2:3, cols] += jnp.sum(grad_two * hat, axis=0, keepdims=True)
            v_part[3:4, cols] += jnp.sum(grad_two, axis=0, keepdims=True)
            put(1, seq, cols, grad_one * vec[0:1, cols] + grad_two * vec[2:3, cols])
        pair_push(1, seq).start()

        @pl.when(seq + 1 < n_shard)
        def _():
            x_load(seq + 1).start()


    @pl.loop(0, n_shard // 2)
    def _(seq):
        norm_rows(seq)

    sum_u.relay()
    sums[0].relay(1)

    @pl.loop(n_shard // 2, n_shard)
    def _(seq):
        norm_rows(seq)

    load_one = load(one_ref, big_three, 6)
    add_pairs(1)
    sum_u.finish()
    cols_u, keep_u = regroup(0, u_part, du_sum, rows_down)

    load_one.wait()
    weight_grad(big_three, back, q_part, cols_q)
    sum_q.start()
    sums[0].relay(2)
    sums[1].relay(1)

    load_dy.wait()
    weight_grad(hid, big_one, big_two, width)
    sum_q.relay()
    sum_d.start()
    attn = back[:, cols_q : cols_q + HD]
    half = width // 2
    for part in range(2):
        cols = slice(part * half, (part + 1) * half)
        o_part[:, cols] = dot(attn, big_one[:, cols], 0, 0).astype(bf16)
    for copy in flat_o:
        copy.start()

    own = pl.ds(pl.multiple_of((shard * 2 + core) * block, block), block)
    column_out = jnp.sum(big_one[own, :].astype(f32), axis=0, keepdims=True)
    v_part[7:8, :] = column_out
    v_part[12:13, :] = column_out
    lanes = pl.ds(pl.multiple_of(slot * HD, HD), HD)
    for part in range(3):
        cols = slice(part * HD, (part + 1) * HD)
        v_part[4 + part : 5 + part, lanes] = jnp.sum(
            back[:, cols].astype(f32), axis=0, keepdims=True
        )
    lanes = pl.ds(pl.multiple_of(slot * rows_down, rows_down), rows_down)
    for part in range(n_plane):
        cols = slice(part * rows_down, (part + 1) * rows_down)
        v_part[8 + part : 9 + part, lanes] = jnp.sum(
            gup[:, cols].astype(f32), axis=0, keepdims=True
        )
    for copy in flat_v:
        copy.start()
    sums[1].relay(2)
    save_out = add_shards(0, out_sum)
    sum_q.finish()
    cols_q_copies, keep_q = regroup(1, q_part, dq_sum, HD)
    save_hat = add_shards(1, hat_sum)
    sum_d.relay()

    for copy in flat_o:
        copy.wait_recv()
    mine = o_part.at[pl.ds(pl.multiple_of(plane * rows_in, rows_in), rows_in)]
    add_rows(o_mid, [mine] + [o_in.at[turn_at] for turn_at in range(n_plane - 1)], rows_in)
    to_owner = push(
        o_mid,
        do_sum,
        head_sent,
        head_here,
        plane=spot.owner_plane,
        core=spot.owner_core,
        shard=plane,
    )
    own_rows = pltpu.make_async_copy(o_mid, do_sum, head_sent)

    @pl.when(spot.head_here)
    def _():
        own_rows.start()

    @pl.when(jnp.logical_not(spot.head_here))
    def _():
        to_owner.start()

    for copy in flat_v:
        copy.wait_recv()
    total = v_part[:, pl.ds(pl.multiple_of(plane * rows_plane, rows_plane), rows_plane)]
    for turn_at in range(n_plane - 1):
        total = total + v_in[turn_at]
    v_mid[...] = total
    wide = 2 * rows_in

    def lanes_of(device):
        half_slot = device["core"] * n_shard + device["shard"]
        return pl.ds(pl.multiple_of(lax.div(half_slot, 2) * wide, wide), wide)

    v_end[slot] = v_mid[:, lanes_of(spot.turned(0))]
    cols_v = []
    for turn_at, device in spot.group():
        cols_v.append(
            push(
                v_mid.at[:, lanes_of(device)],
                v_end.at[slot],
                cols_sent.at[2, turn_at, 0],
                cols_here.at[2, turn_at, 0],
                **device,
            )
        )
    for copy in cols_v:
        copy.start()

    save_sums = [save_out, save_hat]
    sum_d.finish()
    save_d = pltpu.make_async_copy(sum_d.own(), dd_sum, local.at[2, 0])
    save_d.start()
    for copy in cols_v:
        copy.wait_recv()
    total = v_end[0]
    for other in range(1, n_slice):
        total = total + v_end[other]
    odd = lax.rem(slot, 2) == 1
    vec_sum[...] = jnp.where(odd, pltpu.roll(total, rows_in, 1), total)

    for copy in keep_u + keep_q:
        copy.wait()
    for copy in cols_u + cols_q_copies:
        copy.wait_recv()

    @pl.when(spot.head_here)
    def _():
        own_rows.wait()

    @pl.when(jnp.logical_not(spot.head_here))
    def _():
        to_owner.wait_recv()
        to_owner.wait_send()

    for seq in range(n_shard):
        pair_push(1, seq).wait_send()
    for place in range(2):
        sums[place].finish_sends()
    for copy in save_sums + [save_d]:
        copy.wait()
    for total in [sum_u, sum_q, sum_d]:
        total.finish_sends()
    for copy in flat_o + flat_v + cols_u + cols_q_copies + cols_v:
        copy.wait_send()


def backward_all(n_plane, n_shard, *arrays):
    x, dy, _, _, hid, _, back, wq, _, _, wo, vec, moments = arrays
    f32, bf16 = jnp.float32, jnp.bfloat16
    n_slice = 2 * n_shard
    group, width = dy.shape
    block = group // n_slice
    rows_down = width // n_slice
    rows_plane = width // n_plane
    rows_in = rows_plane // n_slice
    cols_q, n_hid = 3 * HD, hid.shape[1]
    n_vec = 16
    dma = pltpu.SemaphoreType.DMA
    vmem = pltpu.VMEM
    shape = jax.ShapeDtypeStruct
    near = n_plane - 1
    inside = pl.BlockSpec(memory_space=vmem)
    anywhere = pl.BlockSpec(memory_space=pl.ANY)
    return pl.pallas_call(
        partial(backward_kernel, n_plane, n_shard),
        out_shape=[
            shape((block, width), bf16),
            shape((block, width), bf16),
            shape((rows_in, n_slice * cols_q), bf16),
            shape((rows_in, n_slice * n_hid), bf16),
            shape((rows_down, width), bf16),
            shape((rows_in, width), bf16),
            shape((n_vec, 2 * rows_in), f32),
        ],
        in_specs=[anywhere] * 13,
        out_specs=[anywhere] * 6 + [inside],
        scratch_shapes=[
            vmem((group, width), bf16),
            vmem((group, width), bf16),
            vmem((group, width), bf16),
            vmem((2 * block, width), bf16),
            vmem(hid.shape, bf16),
            vmem(hid.shape, bf16),
            vmem(back.shape, bf16),
            vmem(wq.shape, bf16),
            vmem(wo.shape, bf16),
            vmem(vec.shape, f32),
            vmem(moments.shape, f32),
            vmem((2, n_shard, block, width), bf16),
            vmem((n_shard, block, width), bf16),
            vmem((n_shard, block, width), bf16),
            vmem((2, n_shard + 1, block, width), bf16),
            vmem((width, cols_q), bf16),
            vmem((width, n_hid), bf16),
            vmem(wo.shape, bf16),
            vmem((n_vec, width), f32),
            vmem((6, rows_plane // 2, cols_q), bf16),
            vmem((6, rows_plane // 2, n_hid), bf16),
            vmem((6, rows_down // 2, width), bf16),
            vmem((near, rows_in, width), bf16),
            vmem((near, n_vec, rows_plane), f32),
            vmem((rows_in, width), bf16),
            vmem((n_vec, rows_plane), f32),
            vmem((n_slice, n_vec, 2 * rows_in), f32),
            dma((13,)),
            dma((3, n_plane)),
            dma((2, n_shard)),
            dma((2, n_shard)),
            dma((2, 2, n_shard)),
            dma((2, 2, n_shard)),
            dma((2, near)),
            dma((2, near)),
            dma((3, 6)),
            dma((3, 6)),
            dma((3, n_slice - 1, n_plane)),
            dma((3, n_slice - 1, n_plane)),
            dma,
            dma,
            dma,
            pltpu.SemaphoreType.REGULAR,
        ],
        compiler_params=pltpu.CompilerParams(
            collective_id=1, has_side_effects=True, vmem_limit_bytes=59 * 1024 * 1024
        ),
        name="backward_all",
    )(*arrays)


def fast_device(
    layer_input,
    out_grad,
    positions,
    w_qkv,
    w_dense,
    w_up,
    w_down,
    vectors,
    m_qkv,
    m_dense,
    m_up,
    m_down,
    m_vectors,
    v_qkv,
    v_dense,
    v_up,
    v_down,
    v_vectors,
):
    bf16 = jnp.bfloat16
    f32 = jnp.float32
    n_plane = lax.axis_size("plane")
    n_shard = lax.axis_size("shard")
    block_rows = layer_input.shape[1]
    n_vec, vec_cols = vectors.shape

    half_rot = ROT // 2
    inverse = 10000.0 ** (-jnp.arange(0, ROT, 2).astype(f32) / ROT)
    freq = jnp.pad(jnp.concatenate([inverse, inverse]), (0, 128 - 2 * half_rot))[None]
    kept = forward_all(
        n_plane,
        n_shard,
        layer_input[0],
        out_grad[0],
        positions.reshape(-1, block_rows),
        jnp.pad(vectors, ((0, 16 - n_vec), (0, 128 - vec_cols))),
        freq,
        w_qkv,
        w_up,
        w_down,
        w_dense,
    )
    branches, grad_hat, part_qkv, part_up, part_down, part_dense, part_vec = backward_all(
        n_plane, n_shard, *kept
    )
    full_vec = kept[-2]
    branches = branches.astype(f32)
    grad_hat = grad_hat.astype(f32)
    own_tokens = layer_input[0].astype(f32)
    grad_rows = out_grad[0].astype(f32)
    layer_output = (own_tokens + branches + full_vec[7] + full_vec[12]).astype(bf16)[None]
    own_center = own_tokens - jnp.mean(own_tokens, axis=-1, keepdims=True)
    own_inv = lax.rsqrt(jnp.mean(own_center * own_center, axis=-1, keepdims=True) + 1e-05)
    own_hat = own_center * own_inv
    grad_input = (
        grad_rows
        + own_inv
        * (
            grad_hat
            - jnp.mean(grad_hat, axis=-1, keepdims=True)
            - own_hat * jnp.mean(grad_hat * own_hat, axis=-1, keepdims=True)
        )
    )[None]
    grad_vectors = part_vec[:n_vec, :vec_cols]
    grad_dense = part_dense.astype(f32)
    grad_down = part_down.astype(f32)
    grad_qkv = part_qkv.astype(f32)
    grad_up = part_up.astype(f32)
    new_qkv, second_qkv = adam_step(w_qkv, grad_qkv, m_qkv, v_qkv, 4.0 * (D // 2) ** (-0.5), 0.1)
    new_dense, second_dense = adam_step(
        w_dense, grad_dense, m_dense, v_dense, 4.0 * (D // 32) ** (-0.5), 0.1
    )
    new_up, second_up = adam_step(w_up, grad_up, m_up, v_up, 4.0 * D ** (-0.5), 0.1)
    new_down, second_down = adam_step(w_down, grad_down, m_down, v_down, 4.0 * FF ** (-0.5), 0.1)
    new_vectors, second_vectors = adam_step(vectors, grad_vectors, m_vectors, v_vectors, 1.0, 0.0)
    return (
        layer_output,
        grad_input,
        grad_qkv,
        grad_dense,
        grad_up,
        grad_down,
        grad_vectors,
        second_qkv,
        second_dense,
        second_up,
        second_down,
        second_vectors,
        new_qkv,
        new_dense,
        new_up,
        new_down,
        new_vectors,
    )


def solution(mesh):
    n_ctx, n_shard = mesh.devices.shape
    if n_ctx == 2 * n_shard and n_ctx == H:
        device_mesh = Mesh(
            mesh.devices.reshape(n_shard, 2, n_shard), ("plane", "core", "shard")
        )
        ctx, body = ("plane", "core"), fast_device
    else:
        device_mesh, ctx, body = mesh, ("ctx",), general_device
    rows = P("shard", ctx, None)
    weight = P((*ctx, "shard"), None)
    vector = P(None, (*ctx, "shard"))
    matrices = (weight,) * 4 + (vector,)
    in_specs = (rows, rows, P("shard", None)) + matrices * 3
    out_specs = (rows, rows) + matrices * 3
    return jax.shard_map(
        body, mesh=device_mesh, in_specs=in_specs, out_specs=out_specs, check_vma=False
    )
```

```python
from functools import partial

import jax
import jax.numpy as jnp
from jax import lax
from jax.experimental import pallas as pl
from jax.experimental.pallas import tpu as pltpu
from jax.sharding import Mesh, PartitionSpec as P

D = 2048
H = 8
HD = 256
ROT = 64
FF = 8192
STEP = 10


def from_behind(value, axis, steps):
    count = lax.axis_size(axis)
    pairs = [(source, (source + steps) % count) for source in range(count)]
    return lax.ppermute(value, axis, pairs)


def layer_norm(values, gain, shift):
    center = values - jnp.mean(values, axis=-1, keepdims=True)
    spread = jnp.mean(center * center, axis=-1, keepdims=True)
    return center * lax.rsqrt(spread + 1e-05) * gain + shift


def angles(places):
    inverse = 10000.0 ** (-jnp.arange(0, ROT, 2).astype(jnp.float32) / ROT)
    phases = places.astype(jnp.float32)[:, None] * inverse[None, :]
    return (jnp.cos(phases), jnp.sin(phases))


def rotate(values, cosine, sine):
    half_rot = cosine.shape[-1]
    front = values[..., :half_rot]
    second = values[..., half_rot : 2 * half_rot]
    others = values[..., 2 * half_rot :]
    cos_b = cosine[:, None, :]
    sin_b = sine[:, None, :]
    return jnp.concatenate(
        [front * cos_b - second * sin_b, second * cos_b + front * sin_b, others], axis=-1
    )


def adam_step(weight, gradient, moment, second, rate, decay):
    moment = 0.9 * moment + 0.1 * gradient
    second = 0.95 * second + 0.05 * gradient * gradient
    unbiased = moment / (1.0 - 0.9**STEP)
    scaled = second / (1.0 - 0.95**STEP)
    return (weight - rate * (unbiased / (jnp.sqrt(scaled) + 1e-08) + decay * weight), second)


def general_device(
    layer_input,
    out_grad,
    positions,
    w_qkv,
    w_dense,
    w_up,
    w_down,
    vectors,
    m_qkv,
    m_dense,
    m_up,
    m_down,
    m_vectors,
    v_qkv,
    v_dense,
    v_up,
    v_down,
    v_vectors,
):
    block_rows = layer_input.shape[1]
    model_width = layer_input.shape[2]
    hidden = w_up.shape[1]
    rows_in = w_qkv.shape[0]
    rows_down = w_down.shape[0]
    n_ctx = lax.axis_size("ctx")
    score_scale = HD ** (-0.5)
    ctx_index = lax.axis_index("ctx")
    all_pos = positions[0]
    own_pos = lax.dynamic_slice_in_dim(all_pos, ctx_index * block_rows, block_rows)
    last_own = jnp.max(own_pos)
    cosine, sine = angles(own_pos)
    full_vec = lax.all_gather(vectors, ("ctx", "shard"), axis=1, tiled=True)
    tokens = layer_input[0].astype(jnp.float32)
    normed_one = layer_norm(tokens, full_vec[0], full_vec[1]).astype(jnp.bfloat16)
    normed_two = layer_norm(tokens, full_vec[2], full_vec[3]).astype(jnp.bfloat16)
    qkv_low = w_qkv.astype(jnp.bfloat16)
    dense_low = w_dense.astype(jnp.bfloat16)
    up_low = w_up.astype(jnp.bfloat16)
    down_low = w_down.astype(jnp.bfloat16)
    grad_low = out_grad[0]
    grad_rows = grad_low.astype(jnp.float32)
    pieces = (
        lax.all_gather(qkv_low, ("ctx", "shard"), axis=0, tiled=True),
        lax.all_gather(up_low, ("ctx", "shard"), axis=0, tiled=True),
    )
    left_one = normed_one
    left_two = normed_two
    proj_sum = jnp.dot(left_one, pieces[0], preferred_element_type=jnp.float32)
    up_sum = jnp.dot(left_two, pieces[1], preferred_element_type=jnp.float32)
    projection = proj_sum + full_vec[4:7].reshape(-1)
    up_value = up_sum + full_vec[8:12].reshape(-1)
    queries = projection[:, :model_width].reshape(block_rows, H, HD)
    keys_raw = projection[:, model_width : 2 * model_width].reshape(block_rows, H, HD)
    values_raw = projection[:, 2 * model_width :].reshape(block_rows, H, HD)
    q_rot = rotate(queries, cosine, sine).astype(jnp.bfloat16)
    k_rot = rotate(keys_raw, cosine, sine).astype(jnp.bfloat16)
    v_low = values_raw.astype(jnp.bfloat16)
    start_state = (
        jnp.full((block_rows, H), -1e30, jnp.float32),
        jnp.zeros((block_rows, H), jnp.float32),
        jnp.zeros((block_rows, H, HD), jnp.float32),
    )
    pieces = (
        lax.all_gather(k_rot, "ctx", axis=0, tiled=True),
        lax.all_gather(v_low, "ctx", axis=0, tiled=True),
    )
    key_pos = all_pos
    allowed = (key_pos[None, :] <= own_pos[:, None])[:, None, :]

    def attend_compute(states):
        running_top, totals, accum = states
        scores = (
            jnp.einsum("qhd,khd->qhk", q_rot, pieces[0], preferred_element_type=jnp.float32)
            * score_scale
        )
        scores = jnp.where(allowed, scores, -1e30)
        new_top = jnp.maximum(running_top, jnp.max(scores, axis=-1))
        weights = jnp.where(allowed, jnp.exp(scores - new_top[..., None]), 0.0)
        totals = jnp.sum(weights, axis=-1)
        accum = jnp.einsum(
            "qhk,khd->qhd",
            weights.astype(jnp.bfloat16),
            pieces[1],
            preferred_element_type=jnp.float32,
        )
        return (new_top, totals, accum)

    skipped = jnp.min(key_pos) > last_own
    running_top, totals, accum = lax.cond(
        skipped, lambda states: states, attend_compute, start_state
    )
    attention = accum / totals[..., None]
    log_sum = running_top + jnp.log(totals)
    attn_low = attention.reshape(block_rows, model_width).astype(jnp.bfloat16)
    gelu_exact = partial(jax.nn.gelu, approximate=False)
    hid_low = gelu_exact(up_value).astype(jnp.bfloat16)
    add_pieces = (
        lax.all_gather(dense_low, ("ctx", "shard"), axis=0, tiled=True),
        lax.all_gather(down_low, ("ctx", "shard"), axis=0, tiled=True),
    )
    second_count = add_pieces[1].shape[0]
    second_begin = jnp.int32(0) // rows_in * rows_down
    left_attn = attn_low
    left_hid = lax.dynamic_slice_in_dim(hid_low, second_begin, second_count, 1)
    branches = jnp.dot(left_attn, add_pieces[0], preferred_element_type=jnp.float32) + jnp.dot(
        left_hid, add_pieces[1], preferred_element_type=jnp.float32
    )
    back_pieces = lax.all_gather((dense_low, down_low), ("ctx", "shard"), axis=0, tiled=True)
    shard_count = back_pieces[0].shape[0] // rows_in
    first_part = jnp.einsum(
        "td,rd->tr", grad_low, back_pieces[0], preferred_element_type=jnp.float32
    ).reshape(block_rows, shard_count, rows_in)
    second_part = jnp.einsum(
        "td,rd->tr", grad_low, back_pieces[1], preferred_element_type=jnp.float32
    ).reshape(block_rows, shard_count, rows_down)
    merged_out = jnp.concatenate([first_part, second_part], axis=2).reshape(
        block_rows, shard_count * (rows_in + rows_down)
    )
    merged_out = merged_out.reshape(block_rows, -1, rows_in + rows_down)
    grad_attn = merged_out[:, :, :rows_in].reshape(block_rows, model_width)
    grad_hid = merged_out[:, :, rows_in:].reshape(block_rows, hidden)
    layer_output = (tokens + branches + full_vec[7] + full_vec[12]).astype(jnp.bfloat16)[None]
    gelu_pull = jax.vjp(gelu_exact, up_value)[1]
    grad_upval = gelu_pull(grad_hid)[0].astype(jnp.bfloat16)
    grad_heads = grad_attn.astype(jnp.bfloat16).reshape(block_rows, H, HD)
    delta_rows = jnp.sum(grad_heads.astype(jnp.float32) * attention, axis=-1)

    def key_turn(turn_index, states):
        pair_now, pair_grad, query_grad = states
        owner_index = (ctx_index - turn_index) % n_ctx
        key_pos = lax.dynamic_slice_in_dim(all_pos, owner_index * block_rows, block_rows)
        allowed = (key_pos[None, :] <= own_pos[:, None])[:, None, :]

        def key_compute(partials):
            grads_held, query_held = partials
            scores = (
                jnp.einsum("qhd,khd->qhk", q_rot, pair_now[0], preferred_element_type=jnp.float32)
                * score_scale
            )
            weights_now = jnp.where(allowed, jnp.exp(scores - log_sum[..., None]), 0.0)
            grad_prob = jnp.einsum(
                "qhd,khd->qhk", grad_heads, pair_now[1], preferred_element_type=jnp.float32
            )
            dscore = (weights_now * (grad_prob - delta_rows[..., None])).astype(jnp.bfloat16)
            query_held = (
                query_held
                + jnp.einsum(
                    "qhk,khd->qhd", dscore, pair_now[0], preferred_element_type=jnp.float32
                )
                * score_scale
            )
            key_term = (
                jnp.einsum("qhk,qhd->khd", dscore, q_rot, preferred_element_type=jnp.float32)
                * score_scale
            )
            value_term = jnp.einsum(
                "qhk,qhd->khd",
                weights_now.astype(jnp.bfloat16),
                grad_heads,
                preferred_element_type=jnp.float32,
            )
            return (grads_held + jnp.stack([key_term, value_term]), query_held)

        skipped = jnp.min(key_pos) > last_own
        pair_grad, query_grad = lax.cond(
            skipped, lambda partials: partials, key_compute, (pair_grad, query_grad)
        )
        pair_now = from_behind(pair_now, "ctx", 1)
        pair_grad = from_behind(pair_grad.astype(jnp.bfloat16), "ctx", 1).astype(pair_grad.dtype)
        return (pair_now, pair_grad, query_grad)

    loop_start = (
        jnp.stack([k_rot, v_low]),
        jnp.zeros((2, block_rows, H, HD), jnp.float32),
        jnp.zeros((block_rows, H, HD), jnp.float32),
    )
    loop_end = lax.fori_loop(0, n_ctx, key_turn, loop_start)
    pair_grad = loop_end[1]
    query_grad = loop_end[2]

    def turn_values(values):
        return rotate(values, cosine, sine)

    rot_pull = jax.vjp(turn_values, queries)[1]
    grad_proj = jnp.concatenate(
        [
            rot_pull(query_grad)[0].reshape(block_rows, model_width),
            rot_pull(pair_grad[0])[0].reshape(block_rows, model_width),
            pair_grad[1].reshape(block_rows, model_width),
        ],
        axis=1,
    ).astype(jnp.bfloat16)

    def back_inputs(pieces):
        shard_count = pieces[0].shape[0] // rows_in
        first_part = jnp.einsum(
            "tc,rc->tr", grad_proj, pieces[0], preferred_element_type=jnp.float32
        ).reshape(block_rows, shard_count, 1, rows_in)
        second_part = jnp.einsum(
            "tc,rc->tr", grad_upval, pieces[1], preferred_element_type=jnp.float32
        ).reshape(block_rows, shard_count, 1, rows_in)
        return jnp.concatenate([first_part, second_part], axis=2).reshape(
            block_rows, shard_count * 2 * rows_in
        )

    merged_in = back_inputs(lax.all_gather((qkv_low, up_low), ("ctx", "shard"), axis=0, tiled=True))
    merged_in = merged_in.reshape(block_rows, -1, 2, rows_in)
    grad_norm_one = merged_in[:, :, 0].reshape(block_rows, model_width)
    grad_norm_two = merged_in[:, :, 1].reshape(block_rows, model_width)
    norm_pull_one = jax.vjp(layer_norm, tokens, full_vec[0], full_vec[1])[1]
    norm_pull_two = jax.vjp(layer_norm, tokens, full_vec[2], full_vec[3])[1]
    back_one, gain_one, shift_one = norm_pull_one(grad_norm_one)
    back_two, gain_two, shift_two = norm_pull_two(grad_norm_two)
    grad_input = (grad_rows + back_one + back_two)[None]
    column_out = jnp.sum(grad_rows, axis=0)
    vector_terms = jnp.concatenate(
        [
            jnp.stack([gain_one, shift_one, gain_two, shift_two]),
            jnp.sum(grad_proj.astype(jnp.float32), axis=0).reshape(3, model_width),
            column_out[None],
            jnp.sum(grad_upval.astype(jnp.float32), axis=0).reshape(4, model_width),
            column_out[None],
        ],
        axis=0,
    )
    grad_vectors = lax.psum_scatter(vector_terms, ("ctx", "shard"), scatter_dimension=1, tiled=True)
    block_count = (rows_in + rows_down) * lax.axis_size(("ctx", "shard")) // (rows_in + rows_down)
    first_block = jnp.int32(0) // (rows_in + rows_down)
    left_attn = attn_low
    left_hid = lax.dynamic_slice_in_dim(
        hid_low, first_block * rows_down, block_count * rows_down, 1
    )
    dense_part = jnp.einsum(
        "tr,td->rd", left_attn, grad_low, preferred_element_type=jnp.float32
    ).reshape(block_count, rows_in, model_width)
    down_part = jnp.einsum(
        "tr,td->rd", left_hid, grad_low, preferred_element_type=jnp.float32
    ).reshape(block_count, rows_down, model_width)
    out_grads = lax.psum_scatter(
        jnp.concatenate([dense_part, down_part], axis=1).reshape(
            (rows_in + rows_down) * lax.axis_size(("ctx", "shard")), model_width
        ),
        ("ctx", "shard"),
        scatter_dimension=0,
        tiled=True,
    )
    left_one = normed_one
    left_two = normed_two
    in_grads = lax.psum_scatter(
        jnp.concatenate(
            [
                jnp.einsum("tr,tc->rc", left_one, grad_proj, preferred_element_type=jnp.float32),
                jnp.einsum("tr,tc->rc", left_two, grad_upval, preferred_element_type=jnp.float32),
            ],
            axis=1,
        ),
        ("ctx", "shard"),
        scatter_dimension=0,
        tiled=True,
    )
    grad_qkv = in_grads[:, : 3 * model_width]
    grad_up = in_grads[:, 3 * model_width :]
    grad_dense = out_grads[:rows_in]
    grad_down = out_grads[rows_in:]
    new_qkv, second_qkv = adam_step(w_qkv, grad_qkv, m_qkv, v_qkv, 4.0 * (D // 2) ** (-0.5), 0.1)
    new_dense, second_dense = adam_step(
        w_dense, grad_dense, m_dense, v_dense, 4.0 * (D // 32) ** (-0.5), 0.1
    )
    new_up, second_up = adam_step(w_up, grad_up, m_up, v_up, 4.0 * D ** (-0.5), 0.1)
    new_down, second_down = adam_step(w_down, grad_down, m_down, v_down, 4.0 * FF ** (-0.5), 0.1)
    new_vectors, second_vectors = adam_step(vectors, grad_vectors, m_vectors, v_vectors, 1.0, 0.0)
    return (
        layer_output,
        grad_input,
        grad_qkv,
        grad_dense,
        grad_up,
        grad_down,
        grad_vectors,
        second_qkv,
        second_dense,
        second_up,
        second_down,
        second_vectors,
        new_qkv,
        new_dense,
        new_up,
        new_down,
        new_vectors,
    )


MESH = pl.DeviceIdType.MESH
VMEM_BYTES = 62 * 1024 * 1024


def push(source, target, sent, arrived, **device):
    return pltpu.make_async_remote_copy(
        src_ref=source,
        dst_ref=target,
        send_sem=sent,
        recv_sem=arrived,
        device_id=device,
        device_id_type=MESH,
    )


class Spot:
    def __init__(self, n_plane, n_shard):
        self.n_plane, self.n_shard = n_plane, n_shard
        self.plane = lax.axis_index("plane")
        self.core = lax.axis_index("core")
        self.shard = lax.axis_index("shard")
        self.slot = self.core * n_shard + self.shard
        head = 2 * self.plane + self.core
        self.head_core = lax.div(head, n_shard)
        self.head_shard = lax.rem(head, n_shard)
        self.owner_plane = lax.div(self.slot, 2)
        self.owner_core = lax.rem(self.slot, 2)
        self.head_here = jnp.logical_and(self.slot == head, self.plane == self.shard)

    def group(self):
        for turn in range(1, 2 * self.n_shard):
            yield turn - 1, self.turned(turn)

    def turned(self, turn):
        core = lax.rem(self.core + turn // self.n_shard, 2)
        shard = lax.rem(self.shard + turn % self.n_shard, self.n_shard)
        return dict(core=core, shard=shard)

    def beside(self):
        across = self.plane + 1 - 2 * lax.rem(self.plane, 2)
        return across, lax.rem(self.plane + 2, 4), 3 - self.plane

    def along(self):
        for step in range(1, self.n_shard):
            yield step - 1, lax.rem(self.shard + step, self.n_shard)

    def planes(self):
        for step in range(1, self.n_plane):
            yield step - 1, lax.rem(self.plane + step, self.n_plane)

    def keeper(self):
        return dict(plane=self.shard, core=self.head_core, shard=self.head_shard)

    def owner(self):
        return dict(plane=self.owner_plane, core=self.owner_core, shard=self.plane)

    def greet(self, sender):
        barrier = pltpu.get_barrier_semaphore()
        count = 0
        for _, device in self.group():
            pl.semaphore_signal(barrier, inc=1, device_id=device, device_id_type=MESH)
            count += 1
        for _, plane in self.planes():
            pl.semaphore_signal(barrier, inc=1, device_id=dict(plane=plane), device_id_type=MESH)
            count += 1

        @pl.when(jnp.logical_not(self.head_here))
        def _():
            pl.semaphore_signal(barrier, inc=1, device_id=sender, device_id_type=MESH)
            pl.semaphore_wait(barrier, count + 1)

        @pl.when(self.head_here)
        def _():
            pl.semaphore_wait(barrier, count)


def turn_tables(pos_row, freq):
    n_pos = pos_row.shape[1]
    places = jnp.broadcast_to(pos_row.astype(jnp.float32), (n_pos, n_pos)).T
    phase = places * freq
    return jnp.cos(phase), jnp.sin(phase), places


def turn(head, cosine, sine):
    half = ROT // 2
    lanes = cosine.shape[1]
    front = head[:, :lanes]
    lane = lax.broadcasted_iota(jnp.int32, front.shape, 1)
    first = jnp.where(lane < half, -sine, 0.0)
    second = jnp.where((lane >= half) & (lane < ROT), sine, 0.0)
    turned = (
        front * cosine
        + pltpu.roll(front, lanes - half, 1) * first
        + pltpu.roll(front, half, 1) * second
    )
    return jnp.concatenate([turned, head[:, lanes:]], axis=1)


def dot(left, right, left_dim=1, right_dim=0):
    return lax.dot_general(
        left, right, (((left_dim,), (right_dim,)), ((), ())), preferred_element_type=jnp.float32
    )


class Spread:
    def __init__(self, spot, ref, size, sent, here):
        self.spot, self.ref, self.size, self.sent, self.here = spot, ref, size, sent, here
        self.across, self.along, self.diagonal = spot.beside()

    def rows(self, plane, part=None):
        size = self.size
        if part is None:
            return self.ref.at[pl.ds(pl.multiple_of(plane * size, size), size)]
        half = size // 2
        return self.ref.at[pl.ds(pl.multiple_of(plane * size + part * half, half), half)]

    def send(self, rows, place, plane):
        return push(rows, rows, self.sent.at[place], self.here.at[place], plane=plane)

    def first(self):
        own = self.rows(self.spot.plane)
        return [self.send(own, 0, self.across), self.send(own, 1, self.along)]

    def second(self):
        return [
            self.send(self.rows(self.along, 0), 2, self.across),
            self.send(self.rows(self.across, 1), 3, self.along),
        ]

    def start(self):
        for copy in self.first():
            copy.start()

    def relay(self):
        first, second = self.first(), self.second()
        first[1].wait_recv()
        second[0].start()
        first[0].wait_recv()
        second[1].start()

    def finish(self):
        for copy in self.second():
            copy.wait_recv()

    def finish_sends(self):
        for copy in self.first() + self.second():
            copy.wait_send()


class Gather:
    def __init__(self, spot, part, size, landed, sent, here):
        self.spot, self.part, self.size, self.landed = spot, part, size, landed
        self.sent, self.here = sent, here
        self.across, self.along, self.diagonal = spot.beside()

    def rows(self, plane, side):
        half = self.size // 2
        return self.part.at[pl.ds(pl.multiple_of(plane * self.size + side * half, half), half)]

    def send(self, rows, place, plane):
        return push(
            rows, self.landed.at[place], self.sent.at[place], self.here.at[place], plane=plane
        )

    def first(self):
        return [
            self.send(self.rows(self.diagonal, 0), 0, self.across),
            self.send(self.rows(self.diagonal, 1), 1, self.along),
            self.send(self.rows(self.across, 0), 2, self.across),
            self.send(self.rows(self.along, 1), 3, self.along),
        ]

    def second(self):
        return [
            self.send(self.rows(self.along, 0), 4, self.along),
            self.send(self.rows(self.across, 1), 5, self.across),
        ]

    def start(self):
        for copy in self.first():
            copy.start()

    def relay(self):
        first, second = self.first(), self.second()
        for side in range(2):
            first[side].wait_recv()
            held = self.rows(self.along if side == 0 else self.across, side)
            add_rows(held, [held, self.landed.at[side]], self.size // 2)
            second[side].start()

    def own(self):
        size = self.size
        return self.part.at[pl.ds(pl.multiple_of(self.spot.plane * size, size), size)]

    def finish(self):
        first, second = self.first(), self.second()
        half = self.size // 2
        for side in range(2):
            first[2 + side].wait_recv()
            second[side].wait_recv()
            held = self.rows(self.spot.plane, side)
            add_rows(held, [held, self.landed.at[2 + side], self.landed.at[4 + side]], half)

    def finish_sends(self):
        for copy in self.first() + self.second():
            copy.wait_send()


class RowSum:
    def __init__(self, spot, part, landed, sent, here):
        self.spot, self.part, self.landed = spot, part, landed
        self.sent, self.here = sent, here

    def rows(self, shard):
        return self.part.at[shard]

    def place(self, side, at, shard):
        if side == 0:
            return shard
        return jnp.where(shard == at, self.spot.n_shard, shard)

    def hop(self, side, shard):
        spot = self.spot
        to = spot.shard + (1 if side == 0 else -1)
        return push(
            self.rows(shard),
            self.landed.at[self.place(side, to, shard)],
            self.sent.at[side, shard],
            self.here.at[side, shard],
            shard=to,
        )

    def wait(self, side, shard):
        spot = self.spot
        push(
            self.rows(shard),
            self.landed.at[self.place(side, spot.shard, shard)],
            self.sent.at[side, shard],
            self.here.at[side, shard],
            shard=spot.shard,
        ).wait_recv()

    def start(self):
        spot, last = self.spot, self.spot.n_shard - 1
        for side in range(2):

            @pl.when(spot.shard == (0 if side == 0 else last))
            def _():
                for step in range(last):
                    self.hop(side, last - step if side == 0 else step).start()

    def relay(self, turn):
        spot, last = self.spot, self.spot.n_shard - 1
        for side in range(2):
            depth = spot.shard if side == 0 else last - spot.shard
            shard = last - turn + spot.shard if side == 0 else turn - last + spot.shard

            @pl.when(jnp.logical_and(depth >= 1, depth <= turn))
            def _():
                self.wait(side, shard)
                held = self.rows(shard)
                came = self.landed.at[self.place(side, spot.shard, shard)]
                add_rows(held, [held, came], held.shape[0])
                self.hop(side, shard).start()

    def finish(self, target):
        spot, last = self.spot, self.spot.n_shard - 1
        held = self.rows(spot.shard)
        first = self.landed.at[self.place(0, spot.shard, spot.shard)]
        second = self.landed.at[self.place(1, spot.shard, spot.shard)]

        @pl.when(spot.shard >= 1)
        def _():
            self.wait(0, spot.shard)

        @pl.when(spot.shard < last)
        def _():
            self.wait(1, spot.shard)

        @pl.when(spot.shard == 0)
        def _():
            add_rows(target, [held, second], held.shape[0])

        @pl.when(spot.shard == last)
        def _():
            add_rows(target, [held, first], held.shape[0])

        @pl.when(jnp.logical_and(spot.shard >= 1, spot.shard < last))
        def _():
            add_rows(target, [held, first, second], held.shape[0])

    def finish_sends(self):
        spot = self.spot
        for shard in range(spot.n_shard):
            for side in range(2):

                @pl.when(spot.shard < shard if side == 0 else spot.shard > shard)
                def _():
                    self.hop(side, shard).wait_send()


class Chain:
    def __init__(self, spot, ref, block, sent, here, pair_sent, pair_here):
        self.spot, self.ref, self.block = spot, ref, block
        self.sent, self.here = sent, here
        self.pair_sent, self.pair_here = pair_sent, pair_here

    def rows(self, shard, core):
        start = pl.multiple_of((shard * 2 + core) * self.block, self.block)
        return self.ref.at[pl.ds(start, self.block)]

    def hop(self, side, dist):
        spot = self.spot
        sign = 1 if side == 0 else -1
        rows = self.rows(spot.shard - sign * dist, spot.core)
        return push(
            rows, rows, self.sent.at[side, dist], self.here.at[side, dist], shard=spot.shard + sign
        )

    def pair(self, side, dist):
        spot = self.spot
        sign = 1 if side == 0 else -1
        rows = self.rows(spot.shard - sign * dist, spot.core)
        return push(
            rows,
            rows,
            self.pair_sent.at[side, dist],
            self.pair_here.at[side, dist],
            core=1 - spot.core,
        )

    def holds(self, side, dist):
        spot = self.spot
        return spot.shard >= dist if side == 0 else spot.shard + dist < spot.n_shard

    def goes(self, side, dist):
        spot = self.spot
        more = spot.shard + 1 < spot.n_shard if side == 0 else spot.shard >= 1
        return jnp.logical_and(self.holds(side, dist), more)

    def start(self):
        for side in range(2):

            @pl.when(self.goes(side, 0))
            def _():
                self.hop(side, 0).start()

        self.pair(0, 0).start()

    def step(self, dist):
        for side in range(2):

            @pl.when(self.holds(side, dist))
            def _():
                self.hop(side, dist - 1).wait_recv()
                if dist + 1 < self.spot.n_shard:

                    @pl.when(self.goes(side, dist))
                    def _():
                        self.hop(side, dist).start()

                self.pair(side, dist).start()

    def finish_pairs(self):
        self.pair(0, 0).wait_recv()
        for dist in range(1, self.spot.n_shard):
            for side in range(2):

                @pl.when(self.holds(side, dist))
                def _():
                    self.pair(side, dist).wait_recv()

    def finish_sends(self):
        self.pair(0, 0).wait_send()
        for side in range(2):
            for dist in range(self.spot.n_shard - 1):

                @pl.when(self.goes(side, dist))
                def _():
                    self.hop(side, dist).wait_send()

            for dist in range(1, self.spot.n_shard):

                @pl.when(self.holds(side, dist))
                def _():
                    self.pair(side, dist).wait_send()


def forward_kernel(
    n_plane,
    n_shard,
    x_ref,
    dy_ref,
    pos_ref,
    vec_ref,
    freq_ref,
    wq_ref,
    wu_ref,
    wd_ref,
    wo_ref,
    x_out,
    dy_out,
    one_out,
    two_out,
    hid_out,
    gup_out,
    back_out,
    wq_out,
    wu_out,
    wd_out,
    wo_out,
    vec_out,
    moments_out,
    x_all,
    dy_all,
    one,
    two,
    wq_all,
    wu_all,
    wd_all,
    wo_all,
    vec_all,
    pos_all,
    full_vec,
    wu_raw,
    wd_raw,
    wo_raw,
    wq_cut,
    wu_cut,
    wo_cut,
    to_heads,
    heads,
    from_heads,
    back,
    grad_k,
    grad_v,
    cos_head,
    sin_head,
    place_head,
    cos_row,
    sin_row,
    key_row,
    probs,
    attention,
    moments,
    loads,
    stores,
    local,
    x_sent,
    x_here,
    x_pair_sent,
    x_pair_here,
    dy_sent,
    dy_here,
    dy_pair_sent,
    dy_pair_here,
    pos_sent,
    pos_here,
    cols_sent,
    cols_here,
    flat_sent,
    flat_here,
    spread_sent,
    spread_here,
    swap_sent,
    swap_here,
    head_sent,
    head_here,
):
    spot = Spot(n_plane, n_shard)
    plane, core, shard, slot = spot.plane, spot.core, spot.shard, spot.slot
    f32, bf16 = jnp.float32, jnp.bfloat16
    block = x_ref.shape[0]
    pair = 2 * block
    n_slice = 2 * n_shard
    rows_in, rows_down = wq_ref.shape[0], wd_ref.shape[0]
    width = x_ref.shape[1]
    n_group = n_slice * block

    def piece(ref, at, size):
        return ref.at[pl.ds(pl.multiple_of(at * size, size), size)]

    chain_x = Chain(spot, x_all, block, x_sent, x_here, x_pair_sent, x_pair_here)
    chain_dy = Chain(spot, dy_all, block, dy_sent, dy_here, dy_pair_sent, dy_pair_here)

    raw = [
        pltpu.make_async_copy(source, held, loads.at[place])
        for place, (source, held) in enumerate(
            [
                (wq_ref, wu_raw.at[:, pl.ds(0, wq_ref.shape[1])]),
                (wu_ref, wu_raw),
                (wd_ref, wd_raw),
                (wo_ref, wo_raw),
                (x_ref, chain_x.rows(shard, core)),
                (dy_ref, chain_dy.rows(shard, core)),
                (pos_ref, pos_all.at[shard]),
                (vec_ref, vec_all.at[plane, slot]),
            ]
        )
    ]
    for place, copy in enumerate(raw):
        if place != 1:
            copy.start()
    spot.greet(spot.owner())

    index = plane * n_slice + slot
    wq_own = piece(wq_all, index, rows_in)
    wu_own = piece(wu_all, index, rows_in)

    def to_group(place, source, target):
        return [
            push(
                source(device["core"] * n_shard + device["shard"]),
                target,
                cols_sent.at[place, turn_at],
                cols_here.at[place, turn_at],
                **device,
            )
            for turn_at, device in spot.group()
        ]

    cols_q = to_group(0, lambda to: wq_cut.at[to], wq_own)
    cols_u = to_group(1, lambda to: wu_cut.at[to], wu_own)
    cols_v = to_group(2, lambda to: vec_all.at[plane, slot], vec_all.at[plane, slot])

    def to_planes(place, ref):
        return [
            push(ref, ref, flat_sent.at[place, turn_at], flat_here.at[place, turn_at], plane=to)
            for turn_at, to in spot.planes()
        ]

    group_rows = n_slice * rows_in
    spread_d = Spread(spot, wd_all, rows_down, spread_sent.at[0], spread_here.at[0])
    spread_q = Spread(spot, wq_all, group_rows, spread_sent.at[1], spread_here.at[1])
    spread_u = Spread(spot, wu_all, group_rows, spread_sent.at[2], spread_here.at[2])
    flat_v = to_planes(0, vec_all.at[plane])
    flat_o = to_planes(1, piece(wo_all, plane, rows_in))
    pos_push = [
        push(
            pos_all.at[shard],
            pos_all.at[shard],
            pos_sent.at[turn_at],
            pos_here.at[turn_at],
            shard=to,
        )
        for turn_at, to in spot.along()
    ]

    raw[6].wait()
    raw[7].wait()
    for copy in cols_v + pos_push:
        copy.start()

    raw[4].wait()
    chain_x.start()
    raw[0].wait()
    for to in range(n_slice):
        for part in range(3):
            wq_cut[to, :, part * HD : (part + 1) * HD] = wu_raw[
                :, part * width + to * HD : part * width + (to + 1) * HD
            ].astype(bf16)
    raw[1].start()
    for copy in cols_q:
        copy.start()
    keep_q = pltpu.make_async_copy(wq_cut.at[slot], wq_own, local.at[0])
    keep_q.start()
    for copy in cols_v:
        copy.wait_recv()
    for copy in flat_v:
        copy.start()
    raw[2].wait()

    down_at = plane * rows_down

    @pl.loop(0, rows_down // 32)
    def _(step):
        at = pl.multiple_of(step * 32, 32)
        wd_all[pl.ds(pl.multiple_of(down_at + at, 32), 32), :] = wd_raw[pl.ds(at, 32), :].astype(bf16)

    spread_d.start()
    raw[1].wait()
    for to in range(n_slice):
        for part in range(n_plane):
            wu_cut[to, :, part * rows_down : (part + 1) * rows_down] = wu_raw[
                :, part * width + to * rows_down : part * width + (to + 1) * rows_down
            ].astype(bf16)
    keep_u = pltpu.make_async_copy(wu_cut.at[slot], wu_own, local.at[1])
    keep_u.start()
    raw[3].wait()
    wo_cut[...] = wo_raw[...].astype(bf16)
    head_rows = piece(wo_all, shard, rows_in)
    to_head = push(wo_cut, head_rows, head_sent, head_here, **spot.keeper())
    own_head = pltpu.make_async_copy(wo_cut, head_rows, head_sent)

    @pl.when(spot.head_here)
    def _():
        own_head.start()

    @pl.when(jnp.logical_not(spot.head_here))
    def _():
        to_head.start()

    for copy in pos_push:
        copy.wait_recv()
    freq = freq_ref[...]
    own_blocks = 2 * plane

    @pl.loop(0, n_shard)
    def _(seq):
        for half in range(2):
            at = pl.ds(pl.multiple_of(seq * pair + half * block, block), block)
            cosine, sine, _ = turn_tables(pos_all[seq, pl.ds(own_blocks + half, 1), :], freq)
            cos_row[at, :] = cosine
            sin_row[at, :] = sine

    raw[5].wait()
    for copy in flat_v:
        copy.wait_recv()
    n_vec, lanes = vec_all.shape[2:]
    lane = lax.broadcasted_iota(jnp.int32, (n_vec, lanes), 1)
    for p in range(n_plane):
        for t in range(0, n_slice, 2):
            at = (p * n_slice + t) * (lanes // 2)
            full_vec[:, at : at + lanes] = jnp.where(
                lane < lanes // 2, vec_all[p, t], pltpu.roll(vec_all[p, t + 1], lanes // 2, 1)
            )
    save_vec = pltpu.make_async_copy(full_vec, vec_out, stores.at[0])
    save_vec.start()

    def norm_rows(seq):
        @pl.loop(0, pair // 32)
        def _(step):
            at = pl.ds(pl.multiple_of(seq * pair + step * 32, 32), 32)
            tokens = x_all[at, :].astype(f32)
            mean = jnp.mean(tokens, axis=-1, keepdims=True)
            center = tokens - mean
            scale = lax.rsqrt(jnp.mean(center * center, axis=-1, keepdims=True) + 1e-05)
            lane = lax.broadcasted_iota(jnp.int32, (32, moments.shape[1]), 1)
            moments[at, :] = jnp.where(lane < 1, mean, scale)
            hat = center * scale
            one[at, :] = (hat * full_vec[0:1, :] + full_vec[1:2, :]).astype(bf16)
            two[at, :] = (hat * full_vec[2:3, :] + full_vec[3:4, :]).astype(bf16)

    def norm_came(dist):
        for side in range(2):

            @pl.when(chain_x.holds(side, dist))
            def _():
                chain_x.pair(side, dist).wait_recv()
                norm_rows(shard - dist if side == 0 else shard + dist)

    chain_x.step(1)
    for copy in cols_u:
        copy.start()
    chain_x.pair(0, 0).wait_recv()
    norm_rows(shard)
    spread_d.relay()
    chain_dy.start()
    keep_q.wait()
    for copy in cols_q:
        copy.wait_recv()
    spread_q.start()
    norm_came(1)
    chain_x.step(2)
    spread_q.relay()
    norm_came(2)

    @pl.loop(0, n_plane)
    def _(part):
        for half in range(2):
            at = pl.ds(pl.multiple_of(part * pair + half * block, block), block)
            cosine, sine, places = turn_tables(pos_all[plane, pl.ds(2 * part + half, 1), :], freq)
            cos_head[at, :] = cosine
            sin_head[at, :] = sine
            place_head[at, :] = places

    for at in range(pos_all.shape[1]):
        key_row[:, at * block : (at + 1) * block] = pos_all[plane, pl.ds(at, 1), :].astype(f32)

    for dist in range(3, n_shard):
        chain_x.step(dist)

    @pl.when(spot.head_here)
    def _():
        own_head.wait()

    @pl.when(jnp.logical_not(spot.head_here))
    def _():
        to_head.wait_recv()

    for copy in flat_o:
        copy.start()


    chain_dy.step(1)
    for dist in range(3, n_shard):
        norm_came(dist)
    save_x = pltpu.make_async_copy(x_all, x_out, stores.at[1])
    save_x.start()
    keep_u.wait()
    for copy in cols_u:
        copy.wait_recv()
    spread_u.start()
    chain_dy.step(2)
    save_moments = pltpu.make_async_copy(moments, moments_out, stores.at[12])
    save_moments.start()
    save_one = pltpu.make_async_copy(one, one_out, stores.at[2])
    save_one.start()
    save_two = pltpu.make_async_copy(two, two_out, stores.at[3])
    save_two.start()

    spread_q.finish()
    save_wq = pltpu.make_async_copy(wq_all, wq_out, stores.at[4])
    save_wq.start()
    head_lanes = pl.ds(pl.multiple_of(slot * HD, HD), HD)

    def swap(place, source, target, cols, to, turn_at):
        def piece_of(ref, at):
            return ref.at[pl.ds(pl.multiple_of(at * pair, pair), pair), cols]

        return push(
            piece_of(source, to),
            piece_of(target, plane),
            swap_sent.at[place, turn_at - 1],
            swap_here.at[place, turn_at - 1],
            plane=to,
        )

    def keep_own(place, source, target, cols):
        at = pl.ds(pl.multiple_of(plane * pair, pair), pair)
        return pltpu.make_async_copy(source.at[at, cols], target.at[at, cols], local.at[place])

    def swaps(place, source, target, cols):
        return [
            swap(place, source, target, cols, lax.rem(plane + turn_at, n_plane), turn_at)
            for turn_at in range(1, n_plane)
        ]

    qkv_cols = pl.ds(0, 3 * HD)
    q_cols, kv_cols, o_cols = pl.ds(0, HD), pl.ds(HD, 2 * HD), pl.ds(3 * HD, HD)

    for step in range(2):
        at = slice(step * 2 * pair, (step + 1) * 2 * pair)
        heads_now = dot(one[at, :], wq_all[...])
        for part in range(3):
            cols = slice(part * HD, (part + 1) * HD)
            value = heads_now[:, cols] + full_vec[4 + part : 5 + part, head_lanes]
            if part < 2:
                value = turn(value, cos_row[at, :], sin_row[at, :])
            to_heads[at, cols] = value.astype(bf16)

    for copy in swaps(0, to_heads, heads, qkv_cols):
        copy.start()
    keep_qkv = keep_own(2, to_heads, heads, qkv_cols)
    keep_qkv.start()

    for dist in range(3, n_shard):
        chain_dy.step(dist)

    chain_dy.finish_pairs()
    save_dy = pltpu.make_async_copy(dy_all, dy_out, stores.at[5])
    save_dy.start()
    for copy in flat_o:
        copy.wait_recv()
    save_wo = pltpu.make_async_copy(wo_all, wo_out, stores.at[6])
    save_wo.start()

    @pl.loop(0, 2)
    def _(step):
        at = pl.ds(pl.multiple_of(step * 2 * pair, 2 * pair), 2 * pair)
        to_heads[at, 3 * HD : 4 * HD] = dot(dy_all[at, :], wo_all[...], 1, 1).astype(bf16)

    for copy in swaps(1, to_heads, heads, o_cols):
        copy.start()
    keep_o = keep_own(3, to_heads, heads, o_cols)
    keep_o.start()

    grad_k[...] = jnp.zeros_like(grad_k)
    grad_v[...] = jnp.zeros_like(grad_v)
    scale = HD ** (-0.5)
    keep_qkv.wait()
    for copy in swaps(0, to_heads, heads, qkv_cols):
        copy.wait_recv()

    @pl.loop(0, n_plane)
    def _(part):
        at = pl.ds(pl.multiple_of(part * pair, pair), pair)
        places = place_head[at, 0:1]
        scores = dot(heads[at, 0:HD], heads[:, HD : 2 * HD], 1, 1) * scale
        scores = jnp.where(key_row[...] <= places, scores, -1e30)
        weights = jnp.exp(scores - jnp.max(scores, axis=-1, keepdims=True))
        share = weights / jnp.sum(weights, axis=-1, keepdims=True)
        probs[at, :] = share
        value = dot(share.astype(bf16), heads[:, 2 * HD : 3 * HD])
        attention[at, :] = value
        from_heads[at, 3 * HD : 4 * HD] = value.astype(bf16)

    for copy in swaps(2, from_heads, back, o_cols):
        copy.start()

    spread_u.relay()

    keep_o.wait()
    for copy in swaps(1, to_heads, heads, o_cols):
        copy.wait_recv()

    @pl.loop(0, n_plane)
    def _(step):
        turn_at = lax.rem(step + 1, n_plane)
        part = lax.rem(plane + turn_at, n_plane)
        at = pl.ds(pl.multiple_of(part * pair, pair), pair)
        grad_out = heads[at, 3 * HD : 4 * HD]
        delta = jnp.sum(grad_out.astype(f32) * attention[at, :], axis=-1, keepdims=True)
        grad_prob = dot(grad_out, heads[:, 2 * HD : 3 * HD], 1, 1)
        share = probs[at, :]
        dscore = (share * (grad_prob - delta)).astype(bf16)
        grad_q = dot(dscore, heads[:, HD : 2 * HD]) * scale
        from_heads[at, 0:HD] = turn(grad_q, cos_head[at, :], -sin_head[at, :]).astype(bf16)

        @pl.when(turn_at > 0)
        def _():
            swap(3, from_heads, back, q_cols, part, turn_at).start()

        grad_k[...] += dot(dscore, heads[at, 0:HD], 0, 0)
        grad_v[...] += dot(share.astype(bf16), grad_out, 0, 0)

    @pl.loop(0, n_plane)
    def _(step):
        turn_at = lax.rem(step + 1, n_plane)
        part = lax.rem(plane + turn_at, n_plane)
        at = pl.ds(pl.multiple_of(part * pair, pair), pair)
        turned = turn(grad_k[at, :] * scale, cos_head[at, :], -sin_head[at, :])
        from_heads[at, HD : 2 * HD] = turned.astype(bf16)
        from_heads[at, 2 * HD : 3 * HD] = grad_v[at, :].astype(bf16)

        @pl.when(turn_at > 0)
        def _():
            swap(4, from_heads, back, kv_cols, part, turn_at).start()

    keep_back = keep_own(2, from_heads, back, pl.ds(0, 4 * HD))
    keep_back.start()

    spread_u.finish()
    save_wu = pltpu.make_async_copy(wu_all, wu_out, stores.at[8])
    save_wu.start()
    spread_d.finish()
    save_wd = pltpu.make_async_copy(wd_all, wd_out, stores.at[7])
    save_wd.start()
    save_one.wait()
    up_lanes = pl.ds(pl.multiple_of(slot * rows_down, rows_down), rows_down)
    n_hid = n_plane * rows_down

    @pl.loop(0, n_shard)
    def _(step):
        at = pl.ds(pl.multiple_of(step * pair, pair), pair)
        hidden = dot(two[at, :], wu_all[...])
        grad = dot(dy_all[at, :], wd_all[...], 1, 1)
        for part in range(n_plane):
            cols = slice(part * rows_down, (part + 1) * rows_down)
            grad_cols = slice(n_hid + part * rows_down, n_hid + (part + 1) * rows_down)
            value = hidden[:, cols] + full_vec[8 + part : 9 + part, up_lanes]
            half = 0.5 + 0.5 * lax.erf(value * 0.7071067811865476)
            slope = half + value * (0.3989422804014327 * jnp.exp(-0.5 * value * value))
            one[at, cols] = (value * half).astype(bf16)
            one[at, grad_cols] = (grad[:, cols] * slope).astype(bf16)

    save_hid = pltpu.make_async_copy(one.at[:, 0:n_hid], hid_out, stores.at[9])
    save_hid.start()
    save_gup = pltpu.make_async_copy(one.at[:, n_hid : 2 * n_hid], gup_out, stores.at[10])
    save_gup.start()
    keep_back.wait()
    again = (
        swaps(2, from_heads, back, o_cols)
        + swaps(3, from_heads, back, q_cols)
        + swaps(4, from_heads, back, kv_cols)
    )
    for copy in again:
        copy.wait_recv()
    save_back = pltpu.make_async_copy(back, back_out, stores.at[11])
    save_back.start()

    @pl.when(jnp.logical_not(spot.head_here))
    def _():
        to_head.wait_send()

    chain_x.finish_sends()
    chain_dy.finish_sends()
    for copy in cols_q + cols_u + cols_v + pos_push:
        copy.wait_send()
    for spread in [spread_d, spread_q, spread_u]:
        spread.finish_sends()
    again += swaps(0, to_heads, heads, qkv_cols) + swaps(1, to_heads, heads, o_cols)
    for copy in flat_v + flat_o + again:
        copy.wait_send()
    for copy in [
        save_vec,
        save_moments,
        save_x,
        save_two,
        save_wq,
        save_dy,
        save_wo,
        save_wd,
        save_wu,
        save_hid,
        save_gup,
        save_back,
    ]:
        copy.wait()


def forward_all(n_plane, n_shard, x, dy, pos, vec, freq, wq, wu, wd, wo):
    f32, bf16 = jnp.float32, jnp.bfloat16
    n_slice = 2 * n_shard
    block, width = x.shape
    rows_in, rows_down = wq.shape[0], wd.shape[0]
    group = n_slice * block
    n_hid = n_plane * rows_down
    cols_q = 3 * HD
    n_vec, lanes = vec.shape
    dma = pltpu.SemaphoreType.DMA
    vmem = pltpu.VMEM
    shape = jax.ShapeDtypeStruct
    anywhere = pl.BlockSpec(memory_space=pl.ANY)
    far, near = n_shard - 1, n_plane - 1
    return pl.pallas_call(
        partial(forward_kernel, n_plane, n_shard),
        out_shape=[
            shape((group, width), bf16),
            shape((group, width), bf16),
            shape((group, width), bf16),
            shape((group, width), bf16),
            shape((group, n_hid), bf16),
            shape((group, n_hid), bf16),
            shape((group, 4 * HD), bf16),
            shape((width, cols_q), bf16),
            shape((width, n_hid), bf16),
            shape((n_hid, width), bf16),
            shape((HD, width), bf16),
            shape((n_vec, width), f32),
            shape((group, block), f32),
        ],
        in_specs=[anywhere] * 4 + [pl.BlockSpec(memory_space=vmem)] + [anywhere] * 4,
        out_specs=[anywhere] * 13,
        scratch_shapes=[
            vmem((group, width), bf16),
            vmem((group, width), bf16),
            vmem((group, width), bf16),
            vmem((group, width), bf16),
            vmem((width, cols_q), bf16),
            vmem((width, n_hid), bf16),
            vmem((n_hid, width), bf16),
            vmem((HD, width), bf16),
            vmem((n_plane, n_slice, n_vec, lanes), f32),
            vmem((n_shard, *pos.shape), jnp.int32),
            vmem((n_vec, width), f32),
            vmem(wu.shape, f32),
            vmem(wd.shape, f32),
            vmem(wo.shape, f32),
            vmem((n_slice, rows_in, cols_q), bf16),
            vmem((n_slice, rows_in, n_hid), bf16),
            vmem(wo.shape, bf16),
            vmem((group, 4 * HD), bf16),
            vmem((group, 4 * HD), bf16),
            vmem((group, 4 * HD), bf16),
            vmem((group, 4 * HD), bf16),
            vmem((group, HD), f32),
            vmem((group, HD), f32),
            *([vmem((group, block), f32)] * 5),
            vmem((1, group), f32),
            vmem((group, group), f32),
            vmem((group, HD), f32),
            vmem((group, block), f32),
            dma((8,)),
            dma((13,)),
            dma((4,)),
            *([dma((2, n_shard))] * 8),
            dma((far,)),
            dma((far,)),
            dma((3, n_slice - 1)),
            dma((3, n_slice - 1)),
            dma((2, near)),
            dma((2, near)),
            dma((3, 4)),
            dma((3, 4)),
            dma((5, near)),
            dma((5, near)),
            dma,
            dma,
        ],
        compiler_params=pltpu.CompilerParams(
            collective_id=0, has_side_effects=True, vmem_limit_bytes=VMEM_BYTES
        ),
        name="forward_all",
    )(x, dy, pos, vec, freq, wq, wu, wd, wo)


def add_rows(target, terms, rows):
    columns = target.shape[1]
    chunk = min(rows, 64 if columns <= 1024 else 32)

    @pl.loop(0, rows // chunk)
    def _(step):
        at = pl.ds(pl.multiple_of(step * chunk, chunk), chunk)
        for start in range(0, columns, 256):
            cols = slice(start, start + 256)
            total = terms[0][at, cols].astype(jnp.float32)
            for term in terms[1:]:
                total = total + term[at, cols].astype(jnp.float32)
            target[at, cols] = total.astype(target.dtype)


def backward_kernel(
    n_plane,
    n_shard,
    x_ref,
    dy_ref,
    one_ref,
    two_ref,
    hid_ref,
    gup_ref,
    back_ref,
    wq_ref,
    wu_ref,
    wd_ref,
    wo_ref,
    vec_ref,
    moments_ref,
    out_sum,
    hat_sum,
    dq_sum,
    du_sum,
    dd_sum,
    do_sum,
    vec_sum,
    big_one,
    big_two,
    big_three,
    x_rows,
    hid,
    gup,
    back,
    wq,
    wo,
    vec,
    moments,
    rows_part,
    other_half,
    theirs,
    parts,
    q_part,
    u_part,
    o_part,
    v_part,
    q_in,
    u_in,
    d_in,
    o_in,
    v_in,
    o_mid,
    v_mid,
    v_end,
    loads,
    local,
    pair_sent,
    pair_here,
    rows_sent,
    rows_here,
    flat_sent,
    flat_here,
    sum_sent,
    sum_here,
    cols_sent,
    cols_here,
    head_sent,
    head_here,
    x_sem,
    free,
):
    spot = Spot(n_plane, n_shard)
    plane, core, shard, slot = spot.plane, spot.core, spot.shard, spot.slot
    f32, bf16 = jnp.float32, jnp.bfloat16
    n_slice = 2 * n_shard
    n_group, width = dy_ref.shape
    block = n_group // n_slice
    pair = 2 * block
    rows_down = width // n_slice
    cols_q = 3 * HD
    n_hid = hid_ref.shape[1]
    rows_plane = width // n_plane
    rows_in = rows_plane // n_slice

    def load(source, target, place):
        copy = pltpu.make_async_copy(source, target, loads.at[place])
        copy.start()
        return copy

    def plane_rows(ref, at):
        return ref.at[pl.ds(pl.multiple_of(at * pair, pair), pair)]

    load_two = load(two_ref, big_three, 0)
    load_hid = load(hid_ref, hid, 1)
    load_dy = load(dy_ref, big_one, 2)
    load_back = load(back_ref, back, 3)
    load_wo = load(wo_ref, wo, 4)
    load_wd = load(wd_ref, big_two, 5)
    load_gup = load(gup_ref, gup, 7)
    load_wq = load(wq_ref, wq, 8)
    load_vec = load(vec_ref, vec, 9)
    load_moments = load(moments_ref, moments, 10)
    spot.greet(spot.keeper())

    def flat(place, source, target):
        return [
            push(
                source(to),
                target.at[turn_at],
                flat_sent.at[place, turn_at],
                flat_here.at[place, turn_at],
                plane=to,
            )
            for turn_at, to in spot.planes()
        ]

    def at_plane(ref, size):
        return lambda to: ref.at[pl.ds(pl.multiple_of(to * size, size), size)]

    sum_u = Gather(spot, u_part, rows_plane, u_in, sum_sent.at[0], sum_here.at[0])
    sum_q = Gather(spot, q_part, rows_plane, q_in, sum_sent.at[1], sum_here.at[1])
    sum_d = Gather(spot, big_two, rows_down, d_in, sum_sent.at[2], sum_here.at[2])
    flat_o = flat(0, at_plane(o_part, rows_in), o_in)
    flat_v = flat(
        1,
        lambda to: v_part.at[:, pl.ds(pl.multiple_of(to * rows_plane, rows_plane), rows_plane)],
        v_in,
    )

    def weight_grad(left, right, target, columns):
        @pl.loop(0, left.shape[1] // 512)
        def _(step):
            at = pl.ds(pl.multiple_of(step * 512, 512), 512)
            turned = left[:, at].T
            for start in range(0, columns, n_group):
                cols = slice(start, min(start + n_group, columns))
                target[at, cols] = dot(turned, right[:, cols]).astype(bf16)

    sums = [
        RowSum(spot, rows_part.at[place], parts.at[place], rows_sent.at[place], rows_here.at[place])
        for place in range(2)
    ]

    def pair_push(place, seq):
        return push(
            other_half.at[seq],
            theirs.at[seq],
            pair_sent.at[place, seq],
            pair_here.at[place, seq],
            core=1 - core,
        )

    def put(place, seq, cols, total):
        first, second = total[:block], total[block:]
        rows_part[place, seq, :, cols] = jnp.where(core == 0, first, second).astype(bf16)
        other_half[seq, :, cols] = jnp.where(core == 0, second, first).astype(bf16)

    def add_pairs(place):
        @pl.loop(0, n_shard)
        def _(seq):
            pair_push(place, seq).wait_recv()
            held = rows_part.at[place, seq]
            add_rows(held, [held, theirs.at[seq]], block)

        sums[place].start()

    def add_shards(place, target):
        sums[place].finish(sums[place].rows(shard))
        copy = pltpu.make_async_copy(sums[place].rows(shard), target, local.at[2, 1 + place])
        copy.start()
        return copy

    def regroup(place, held, target, wide):
        base = pl.multiple_of(plane * rows_plane, rows_plane)
        parts_here = held.shape[1] // wide

        def rows(to, part):
            start = pl.multiple_of(base + to * rows_in, rows_in)
            return held.at[pl.ds(start, rows_in), pl.ds(part * wide, wide)]

        def lands(part):
            start = pl.multiple_of(part * width + slot * wide, wide)
            return target.at[:, pl.ds(start, wide)]

        copies = []
        for turn_at, device in spot.group():
            to = device["core"] * n_shard + device["shard"]
            for part in range(parts_here):
                copies.append(
                    push(
                        rows(to, part),
                        lands(part),
                        cols_sent.at[place, turn_at, part],
                        cols_here.at[place, turn_at, part],
                        **device,
                    )
                )
        keeps = [
            pltpu.make_async_copy(rows(slot, part), lands(part), local.at[place, part])
            for part in range(parts_here)
        ]
        for copy in copies + keeps:
            copy.start()
        return copies, keeps

    load_two.wait()
    load_gup.wait()
    weight_grad(big_three, gup, u_part, n_hid)
    sum_u.start()

    load_wu = [
        load(
            wu_ref.at[pl.ds(part * n_group, n_group)],
            big_three.at[:, pl.ds(part * n_hid, n_hid)],
            11 + part,
        )
        for part in range(width // n_group)
    ]

    load_hid.wait()
    load_back.wait()
    load_wo.wait()
    load_wd.wait()

    @pl.loop(0, n_shard)
    def _(seq):
        at = pl.ds(pl.multiple_of(seq * pair, pair), pair)
        for start in range(0, width, n_group):
            cols = slice(start, start + n_group)
            total = dot(back[at, cols_q : cols_q + HD], wo[:, cols])
            put(0, seq, cols, total + dot(hid[at, :], big_two[:, cols]))
        pair_push(0, seq).start()

    add_pairs(0)
    pl.semaphore_signal(free, inc=1, device_id=dict(core=1 - core), device_id_type=MESH)

    def x_load(seq):
        return pltpu.make_async_copy(plane_rows(x_ref, seq), x_rows, x_sem)

    x_load(0).start()
    v_part[...] = jnp.zeros_like(v_part)
    load_wq.wait()
    load_vec.wait()
    for copy in load_wu:
        copy.wait()
    load_moments.wait()
    for seq in range(n_shard):
        pair_push(0, seq).wait_send()
    pl.semaphore_wait(free, 1)

    def norm_rows(seq):
        at = pl.ds(pl.multiple_of(seq * pair, pair), pair)
        mean, scale = moments[at, 0:1], moments[at, 1:2]
        for start in range(0, width, 512):
            cols = slice(start, start + 512)
            up_rows = slice(start % n_group, start % n_group + 512)
            up_cols = slice(start // n_group * n_hid, (start // n_group + 1) * n_hid)
            grad_one = dot(back[at, 0:cols_q], wq[cols, :], 1, 1)
            grad_two = dot(gup[at, :], big_three[up_rows, up_cols], 1, 1)
            if start == 0:
                x_load(seq).wait()
            hat = (x_rows[:, cols].astype(f32) - mean) * scale
            v_part[0:1, cols] += jnp.sum(grad_one * hat, axis=0, keepdims=True)
            v_part[1:2, cols] += jnp.sum(grad_one, axis=0, keepdims=True)
            v_part[2:3, cols] += jnp.sum(grad_two * hat, axis=0, keepdims=True)
            v_part[3:4, cols] += jnp.sum(grad_two, axis=0, keepdims=True)
            put(1, seq, cols, grad_one * vec[0:1, cols] + grad_two * vec[2:3, cols])
        pair_push(1, seq).start()

        @pl.when(seq + 1 < n_shard)
        def _():
            x_load(seq + 1).start()


    @pl.loop(0, n_shard // 2)
    def _(seq):
        norm_rows(seq)

    sum_u.relay()
    sums[0].relay(1)

    @pl.loop(n_shard // 2, n_shard)
    def _(seq):
        norm_rows(seq)

    load_one = load(one_ref, big_three, 6)
    add_pairs(1)
    sum_u.finish()
    cols_u, keep_u = regroup(0, u_part, du_sum, rows_down)

    load_one.wait()
    weight_grad(big_three, back, q_part, cols_q)
    sum_q.start()
    sums[0].relay(2)
    sums[1].relay(1)

    load_dy.wait()
    weight_grad(hid, big_one, big_two, width)
    sum_q.relay()
    sum_d.start()
    attn = back[:, cols_q : cols_q + HD]
    half = width // 2
    for part in range(2):
        cols = slice(part * half, (part + 1) * half)
        o_part[:, cols] = dot(attn, big_one[:, cols], 0, 0).astype(bf16)
    for copy in flat_o:
        copy.start()

    own = pl.ds(pl.multiple_of((shard * 2 + core) * block, block), block)
    column_out = jnp.sum(big_one[own, :].astype(f32), axis=0, keepdims=True)
    v_part[7:8, :] = column_out
    v_part[12:13, :] = column_out
    lanes = pl.ds(pl.multiple_of(slot * HD, HD), HD)
    for part in range(3):
        cols = slice(part * HD, (part + 1) * HD)
        v_part[4 + part : 5 + part, lanes] = jnp.sum(
            back[:, cols].astype(f32), axis=0, keepdims=True
        )
    lanes = pl.ds(pl.multiple_of(slot * rows_down, rows_down), rows_down)
    for part in range(n_plane):
        cols = slice(part * rows_down, (part + 1) * rows_down)
        v_part[8 + part : 9 + part, lanes] = jnp.sum(
            gup[:, cols].astype(f32), axis=0, keepdims=True
        )
    for copy in flat_v:
        copy.start()
    sums[1].relay(2)
    save_out = add_shards(0, out_sum)
    sum_q.finish()
    cols_q_copies, keep_q = regroup(1, q_part, dq_sum, HD)
    save_hat = add_shards(1, hat_sum)
    sum_d.relay()

    for copy in flat_o:
        copy.wait_recv()
    mine = o_part.at[pl.ds(pl.multiple_of(plane * rows_in, rows_in), rows_in)]
    add_rows(o_mid, [mine] + [o_in.at[turn_at] for turn_at in range(n_plane - 1)], rows_in)
    to_owner = push(
        o_mid,
        do_sum,
        head_sent,
        head_here,
        plane=spot.owner_plane,
        core=spot.owner_core,
        shard=plane,
    )
    own_rows = pltpu.make_async_copy(o_mid, do_sum, head_sent)

    @pl.when(spot.head_here)
    def _():
        own_rows.start()

    @pl.when(jnp.logical_not(spot.head_here))
    def _():
        to_owner.start()

    for copy in flat_v:
        copy.wait_recv()
    total = v_part[:, pl.ds(pl.multiple_of(plane * rows_plane, rows_plane), rows_plane)]
    for turn_at in range(n_plane - 1):
        total = total + v_in[turn_at]
    v_mid[...] = total
    wide = 2 * rows_in

    def lanes_of(device):
        half_slot = device["core"] * n_shard + device["shard"]
        return pl.ds(pl.multiple_of(lax.div(half_slot, 2) * wide, wide), wide)

    v_end[slot] = v_mid[:, lanes_of(spot.turned(0))]
    cols_v = []
    for turn_at, device in spot.group():
        cols_v.append(
            push(
                v_mid.at[:, lanes_of(device)],
                v_end.at[slot],
                cols_sent.at[2, turn_at, 0],
                cols_here.at[2, turn_at, 0],
                **device,
            )
        )
    for copy in cols_v:
        copy.start()

    save_sums = [save_out, save_hat]
    sum_d.finish()
    save_d = pltpu.make_async_copy(sum_d.own(), dd_sum, local.at[2, 0])
    save_d.start()
    for copy in cols_v:
        copy.wait_recv()
    total = v_end[0]
    for other in range(1, n_slice):
        total = total + v_end[other]
    odd = lax.rem(slot, 2) == 1
    vec_sum[...] = jnp.where(odd, pltpu.roll(total, rows_in, 1), total)

    for copy in keep_u + keep_q:
        copy.wait()
    for copy in cols_u + cols_q_copies:
        copy.wait_recv()

    @pl.when(spot.head_here)
    def _():
        own_rows.wait()

    @pl.when(jnp.logical_not(spot.head_here))
    def _():
        to_owner.wait_recv()
        to_owner.wait_send()

    for seq in range(n_shard):
        pair_push(1, seq).wait_send()
    for place in range(2):
        sums[place].finish_sends()
    for copy in save_sums + [save_d]:
        copy.wait()
    for total in [sum_u, sum_q, sum_d]:
        total.finish_sends()
    for copy in flat_o + flat_v + cols_u + cols_q_copies + cols_v:
        copy.wait_send()


def backward_all(n_plane, n_shard, *arrays):
    x, dy, _, _, hid, _, back, wq, _, _, wo, vec, moments = arrays
    f32, bf16 = jnp.float32, jnp.bfloat16
    n_slice = 2 * n_shard
    group, width = dy.shape
    block = group // n_slice
    rows_down = width // n_slice
    rows_plane = width // n_plane
    rows_in = rows_plane // n_slice
    cols_q, n_hid = 3 * HD, hid.shape[1]
    n_vec = 16
    dma = pltpu.SemaphoreType.DMA
    vmem = pltpu.VMEM
    shape = jax.ShapeDtypeStruct
    near = n_plane - 1
    inside = pl.BlockSpec(memory_space=vmem)
    anywhere = pl.BlockSpec(memory_space=pl.ANY)
    return pl.pallas_call(
        partial(backward_kernel, n_plane, n_shard),
        out_shape=[
            shape((block, width), bf16),
            shape((block, width), bf16),
            shape((rows_in, n_slice * cols_q), bf16),
            shape((rows_in, n_slice * n_hid), bf16),
            shape((rows_down, width), bf16),
            shape((rows_in, width), bf16),
            shape((n_vec, 2 * rows_in), f32),
        ],
        in_specs=[anywhere] * 13,
        out_specs=[anywhere] * 6 + [inside],
        scratch_shapes=[
            vmem((group, width), bf16),
            vmem((group, width), bf16),
            vmem((group, width), bf16),
            vmem((2 * block, width), bf16),
            vmem(hid.shape, bf16),
            vmem(hid.shape, bf16),
            vmem(back.shape, bf16),
            vmem(wq.shape, bf16),
            vmem(wo.shape, bf16),
            vmem(vec.shape, f32),
            vmem(moments.shape, f32),
            vmem((2, n_shard, block, width), bf16),
            vmem((n_shard, block, width), bf16),
            vmem((n_shard, block, width), bf16),
            vmem((2, n_shard + 1, block, width), bf16),
            vmem((width, cols_q), bf16),
            vmem((width, n_hid), bf16),
            vmem(wo.shape, bf16),
            vmem((n_vec, width), f32),
            vmem((6, rows_plane // 2, cols_q), bf16),
            vmem((6, rows_plane // 2, n_hid), bf16),
            vmem((6, rows_down // 2, width), bf16),
            vmem((near, rows_in, width), bf16),
            vmem((near, n_vec, rows_plane), f32),
            vmem((rows_in, width), bf16),
            vmem((n_vec, rows_plane), f32),
            vmem((n_slice, n_vec, 2 * rows_in), f32),
            dma((13,)),
            dma((3, n_plane)),
            dma((2, n_shard)),
            dma((2, n_shard)),
            dma((2, 2, n_shard)),
            dma((2, 2, n_shard)),
            dma((2, near)),
            dma((2, near)),
            dma((3, 6)),
            dma((3, 6)),
            dma((3, n_slice - 1, n_plane)),
            dma((3, n_slice - 1, n_plane)),
            dma,
            dma,
            dma,
            pltpu.SemaphoreType.REGULAR,
        ],
        compiler_params=pltpu.CompilerParams(
            collective_id=1, has_side_effects=True, vmem_limit_bytes=59 * 1024 * 1024
        ),
        name="backward_all",
    )(*arrays)


def fast_device(
    layer_input,
    out_grad,
    positions,
    w_qkv,
    w_dense,
    w_up,
    w_down,
    vectors,
    m_qkv,
    m_dense,
    m_up,
    m_down,
    m_vectors,
    v_qkv,
    v_dense,
    v_up,
    v_down,
    v_vectors,
):
    bf16 = jnp.bfloat16
    f32 = jnp.float32
    n_plane = lax.axis_size("plane")
    n_shard = lax.axis_size("shard")
    block_rows = layer_input.shape[1]
    n_vec, vec_cols = vectors.shape

    half_rot = ROT // 2
    inverse = 10000.0 ** (-jnp.arange(0, ROT, 2).astype(f32) / ROT)
    freq = jnp.pad(jnp.concatenate([inverse, inverse]), (0, 128 - 2 * half_rot))[None]
    kept = forward_all(
        n_plane,
        n_shard,
        layer_input[0],
        out_grad[0],
        positions.reshape(-1, block_rows),
        jnp.pad(vectors, ((0, 16 - n_vec), (0, 128 - vec_cols))),
        freq,
        w_qkv,
        w_up,
        w_down,
        w_dense,
    )
    branches, grad_hat, part_qkv, part_up, part_down, part_dense, part_vec = backward_all(
        n_plane, n_shard, *kept
    )
    full_vec = kept[-2]
    branches = branches.astype(f32)
    grad_hat = grad_hat.astype(f32)
    own_tokens = layer_input[0].astype(f32)
    grad_rows = out_grad[0].astype(f32)
    layer_output = (own_tokens + branches + full_vec[7] + full_vec[12]).astype(bf16)[None]
    own_center = own_tokens - jnp.mean(own_tokens, axis=-1, keepdims=True)
    own_inv = lax.rsqrt(jnp.mean(own_center * own_center, axis=-1, keepdims=True) + 1e-05)
    own_hat = own_center * own_inv
    grad_input = (
        grad_rows
        + own_inv
        * (
            grad_hat
            - jnp.mean(grad_hat, axis=-1, keepdims=True)
            - own_hat * jnp.mean(grad_hat * own_hat, axis=-1, keepdims=True)
        )
    )[None]
    grad_vectors = part_vec[:n_vec, :vec_cols]
    grad_dense = part_dense.astype(f32)
    grad_down = part_down.astype(f32)
    grad_qkv = part_qkv.astype(f32)
    grad_up = part_up.astype(f32)
    new_qkv, second_qkv = adam_step(w_qkv, grad_qkv, m_qkv, v_qkv, 4.0 * (D // 2) ** (-0.5), 0.1)
    new_dense, second_dense = adam_step(
        w_dense, grad_dense, m_dense, v_dense, 4.0 * (D // 32) ** (-0.5), 0.1
    )
    new_up, second_up = adam_step(w_up, grad_up, m_up, v_up, 4.0 * D ** (-0.5), 0.1)
    new_down, second_down = adam_step(w_down, grad_down, m_down, v_down, 4.0 * FF ** (-0.5), 0.1)
    new_vectors, second_vectors = adam_step(vectors, grad_vectors, m_vectors, v_vectors, 1.0, 0.0)
    return (
        layer_output,
        grad_input,
        grad_qkv,
        grad_dense,
        grad_up,
        grad_down,
        grad_vectors,
        second_qkv,
        second_dense,
        second_up,
        second_down,
        second_vectors,
        new_qkv,
        new_dense,
        new_up,
        new_down,
        new_vectors,
    )


def solution(mesh):
    n_ctx, n_shard = mesh.devices.shape
    if n_ctx == 2 * n_shard and n_ctx == H:
        device_mesh = Mesh(
            mesh.devices.reshape(n_shard, 2, n_shard), ("plane", "core", "shard")
        )
        ctx, body = ("plane", "core"), fast_device
    else:
        device_mesh, ctx, body = mesh, ("ctx",), general_device
    rows = P("shard", ctx, None)
    weight = P((*ctx, "shard"), None)
    vector = P(None, (*ctx, "shard"))
    matrices = (weight,) * 4 + (vector,)
    in_specs = (rows, rows, P("shard", None)) + matrices * 3
    out_specs = (rows, rows) + matrices * 3
    return jax.shard_map(
        body, mesh=device_mesh, in_specs=in_specs, out_specs=out_specs, check_vma=False
    )
```

```python
from functools import partial

import jax
import jax.numpy as jnp
from jax import lax
from jax.experimental import pallas as pl
from jax.experimental.pallas import tpu as pltpu
from jax.sharding import Mesh, PartitionSpec as P

D = 2048
H = 8
HD = 256
ROT = 64
FF = 8192
STEP = 10


def from_behind(value, axis, steps):
    count = lax.axis_size(axis)
    pairs = [(source, (source + steps) % count) for source in range(count)]
    return lax.ppermute(value, axis, pairs)


def layer_norm(values, gain, shift):
    center = values - jnp.mean(values, axis=-1, keepdims=True)
    spread = jnp.mean(center * center, axis=-1, keepdims=True)
    return center * lax.rsqrt(spread + 1e-05) * gain + shift


def angles(places):
    inverse = 10000.0 ** (-jnp.arange(0, ROT, 2).astype(jnp.float32) / ROT)
    phases = places.astype(jnp.float32)[:, None] * inverse[None, :]
    return (jnp.cos(phases), jnp.sin(phases))


def rotate(values, cosine, sine):
    half_rot = cosine.shape[-1]
    front = values[..., :half_rot]
    second = values[..., half_rot : 2 * half_rot]
    others = values[..., 2 * half_rot :]
    cos_b = cosine[:, None, :]
    sin_b = sine[:, None, :]
    return jnp.concatenate(
        [front * cos_b - second * sin_b, second * cos_b + front * sin_b, others], axis=-1
    )


def adam_step(weight, gradient, moment, second, rate, decay):
    moment = 0.9 * moment + 0.1 * gradient
    second = 0.95 * second + 0.05 * gradient * gradient
    unbiased = moment / (1.0 - 0.9**STEP)
    scaled = second / (1.0 - 0.95**STEP)
    return (weight - rate * (unbiased / (jnp.sqrt(scaled) + 1e-08) + decay * weight), second)


def general_device(
    layer_input,
    out_grad,
    positions,
    w_qkv,
    w_dense,
    w_up,
    w_down,
    vectors,
    m_qkv,
    m_dense,
    m_up,
    m_down,
    m_vectors,
    v_qkv,
    v_dense,
    v_up,
    v_down,
    v_vectors,
):
    block_rows = layer_input.shape[1]
    model_width = layer_input.shape[2]
    hidden = w_up.shape[1]
    rows_in = w_qkv.shape[0]
    rows_down = w_down.shape[0]
    n_ctx = lax.axis_size("ctx")
    score_scale = HD ** (-0.5)
    ctx_index = lax.axis_index("ctx")
    all_pos = positions[0]
    own_pos = lax.dynamic_slice_in_dim(all_pos, ctx_index * block_rows, block_rows)
    last_own = jnp.max(own_pos)
    cosine, sine = angles(own_pos)
    full_vec = lax.all_gather(vectors, ("ctx", "shard"), axis=1, tiled=True)
    tokens = layer_input[0].astype(jnp.float32)
    normed_one = layer_norm(tokens, full_vec[0], full_vec[1]).astype(jnp.bfloat16)
    normed_two = layer_norm(tokens, full_vec[2], full_vec[3]).astype(jnp.bfloat16)
    qkv_low = w_qkv.astype(jnp.bfloat16)
    dense_low = w_dense.astype(jnp.bfloat16)
    up_low = w_up.astype(jnp.bfloat16)
    down_low = w_down.astype(jnp.bfloat16)
    grad_low = out_grad[0]
    grad_rows = grad_low.astype(jnp.float32)
    pieces = (
        lax.all_gather(qkv_low, ("ctx", "shard"), axis=0, tiled=True),
        lax.all_gather(up_low, ("ctx", "shard"), axis=0, tiled=True),
    )
    left_one = normed_one
    left_two = normed_two
    proj_sum = jnp.dot(left_one, pieces[0], preferred_element_type=jnp.float32)
    up_sum = jnp.dot(left_two, pieces[1], preferred_element_type=jnp.float32)
    projection = proj_sum + full_vec[4:7].reshape(-1)
    up_value = up_sum + full_vec[8:12].reshape(-1)
    queries = projection[:, :model_width].reshape(block_rows, H, HD)
    keys_raw = projection[:, model_width : 2 * model_width].reshape(block_rows, H, HD)
    values_raw = projection[:, 2 * model_width :].reshape(block_rows, H, HD)
    q_rot = rotate(queries, cosine, sine).astype(jnp.bfloat16)
    k_rot = rotate(keys_raw, cosine, sine).astype(jnp.bfloat16)
    v_low = values_raw.astype(jnp.bfloat16)
    start_state = (
        jnp.full((block_rows, H), -1e30, jnp.float32),
        jnp.zeros((block_rows, H), jnp.float32),
        jnp.zeros((block_rows, H, HD), jnp.float32),
    )
    pieces = (
        lax.all_gather(k_rot, "ctx", axis=0, tiled=True),
        lax.all_gather(v_low, "ctx", axis=0, tiled=True),
    )
    key_pos = all_pos
    allowed = (key_pos[None, :] <= own_pos[:, None])[:, None, :]

    def attend_compute(states):
        running_top, totals, accum = states
        scores = (
            jnp.einsum("qhd,khd->qhk", q_rot, pieces[0], preferred_element_type=jnp.float32)
            * score_scale
        )
        scores = jnp.where(allowed, scores, -1e30)
        new_top = jnp.maximum(running_top, jnp.max(scores, axis=-1))
        weights = jnp.where(allowed, jnp.exp(scores - new_top[..., None]), 0.0)
        totals = jnp.sum(weights, axis=-1)
        accum = jnp.einsum(
            "qhk,khd->qhd",
            weights.astype(jnp.bfloat16),
            pieces[1],
            preferred_element_type=jnp.float32,
        )
        return (new_top, totals, accum)

    skipped = jnp.min(key_pos) > last_own
    running_top, totals, accum = lax.cond(
        skipped, lambda states: states, attend_compute, start_state
    )
    attention = accum / totals[..., None]
    log_sum = running_top + jnp.log(totals)
    attn_low = attention.reshape(block_rows, model_width).astype(jnp.bfloat16)
    gelu_exact = partial(jax.nn.gelu, approximate=False)
    hid_low = gelu_exact(up_value).astype(jnp.bfloat16)
    add_pieces = (
        lax.all_gather(dense_low, ("ctx", "shard"), axis=0, tiled=True),
        lax.all_gather(down_low, ("ctx", "shard"), axis=0, tiled=True),
    )
    second_count = add_pieces[1].shape[0]
    second_begin = jnp.int32(0) // rows_in * rows_down
    left_attn = attn_low
    left_hid = lax.dynamic_slice_in_dim(hid_low, second_begin, second_count, 1)
    branches = jnp.dot(left_attn, add_pieces[0], preferred_element_type=jnp.float32) + jnp.dot(
        left_hid, add_pieces[1], preferred_element_type=jnp.float32
    )
    back_pieces = lax.all_gather((dense_low, down_low), ("ctx", "shard"), axis=0, tiled=True)
    shard_count = back_pieces[0].shape[0] // rows_in
    first_part = jnp.einsum(
        "td,rd->tr", grad_low, back_pieces[0], preferred_element_type=jnp.float32
    ).reshape(block_rows, shard_count, rows_in)
    second_part = jnp.einsum(
        "td,rd->tr", grad_low, back_pieces[1], preferred_element_type=jnp.float32
    ).reshape(block_rows, shard_count, rows_down)
    merged_out = jnp.concatenate([first_part, second_part], axis=2).reshape(
        block_rows, shard_count * (rows_in + rows_down)
    )
    merged_out = merged_out.reshape(block_rows, -1, rows_in + rows_down)
    grad_attn = merged_out[:, :, :rows_in].reshape(block_rows, model_width)
    grad_hid = merged_out[:, :, rows_in:].reshape(block_rows, hidden)
    layer_output = (tokens + branches + full_vec[7] + full_vec[12]).astype(jnp.bfloat16)[None]
    gelu_pull = jax.vjp(gelu_exact, up_value)[1]
    grad_upval = gelu_pull(grad_hid)[0].astype(jnp.bfloat16)
    grad_heads = grad_attn.astype(jnp.bfloat16).reshape(block_rows, H, HD)
    delta_rows = jnp.sum(grad_heads.astype(jnp.float32) * attention, axis=-1)

    def key_turn(turn_index, states):
        pair_now, pair_grad, query_grad = states
        owner_index = (ctx_index - turn_index) % n_ctx
        key_pos = lax.dynamic_slice_in_dim(all_pos, owner_index * block_rows, block_rows)
        allowed = (key_pos[None, :] <= own_pos[:, None])[:, None, :]

        def key_compute(partials):
            grads_held, query_held = partials
            scores = (
                jnp.einsum("qhd,khd->qhk", q_rot, pair_now[0], preferred_element_type=jnp.float32)
                * score_scale
            )
            weights_now = jnp.where(allowed, jnp.exp(scores - log_sum[..., None]), 0.0)
            grad_prob = jnp.einsum(
                "qhd,khd->qhk", grad_heads, pair_now[1], preferred_element_type=jnp.float32
            )
            dscore = (weights_now * (grad_prob - delta_rows[..., None])).astype(jnp.bfloat16)
            query_held = (
                query_held
                + jnp.einsum(
                    "qhk,khd->qhd", dscore, pair_now[0], preferred_element_type=jnp.float32
                )
                * score_scale
            )
            key_term = (
                jnp.einsum("qhk,qhd->khd", dscore, q_rot, preferred_element_type=jnp.float32)
                * score_scale
            )
            value_term = jnp.einsum(
                "qhk,qhd->khd",
                weights_now.astype(jnp.bfloat16),
                grad_heads,
                preferred_element_type=jnp.float32,
            )
            return (grads_held + jnp.stack([key_term, value_term]), query_held)

        skipped = jnp.min(key_pos) > last_own
        pair_grad, query_grad = lax.cond(
            skipped, lambda partials: partials, key_compute, (pair_grad, query_grad)
        )
        pair_now = from_behind(pair_now, "ctx", 1)
        pair_grad = from_behind(pair_grad.astype(jnp.bfloat16), "ctx", 1).astype(pair_grad.dtype)
        return (pair_now, pair_grad, query_grad)

    loop_start = (
        jnp.stack([k_rot, v_low]),
        jnp.zeros((2, block_rows, H, HD), jnp.float32),
        jnp.zeros((block_rows, H, HD), jnp.float32),
    )
    loop_end = lax.fori_loop(0, n_ctx, key_turn, loop_start)
    pair_grad = loop_end[1]
    query_grad = loop_end[2]

    def turn_values(values):
        return rotate(values, cosine, sine)

    rot_pull = jax.vjp(turn_values, queries)[1]
    grad_proj = jnp.concatenate(
        [
            rot_pull(query_grad)[0].reshape(block_rows, model_width),
            rot_pull(pair_grad[0])[0].reshape(block_rows, model_width),
            pair_grad[1].reshape(block_rows, model_width),
        ],
        axis=1,
    ).astype(jnp.bfloat16)

    def back_inputs(pieces):
        shard_count = pieces[0].shape[0] // rows_in
        first_part = jnp.einsum(
            "tc,rc->tr", grad_proj, pieces[0], preferred_element_type=jnp.float32
        ).reshape(block_rows, shard_count, 1, rows_in)
        second_part = jnp.einsum(
            "tc,rc->tr", grad_upval, pieces[1], preferred_element_type=jnp.float32
        ).reshape(block_rows, shard_count, 1, rows_in)
        return jnp.concatenate([first_part, second_part], axis=2).reshape(
            block_rows, shard_count * 2 * rows_in
        )

    merged_in = back_inputs(lax.all_gather((qkv_low, up_low), ("ctx", "shard"), axis=0, tiled=True))
    merged_in = merged_in.reshape(block_rows, -1, 2, rows_in)
    grad_norm_one = merged_in[:, :, 0].reshape(block_rows, model_width)
    grad_norm_two = merged_in[:, :, 1].reshape(block_rows, model_width)
    norm_pull_one = jax.vjp(layer_norm, tokens, full_vec[0], full_vec[1])[1]
    norm_pull_two = jax.vjp(layer_norm, tokens, full_vec[2], full_vec[3])[1]
    back_one, gain_one, shift_one = norm_pull_one(grad_norm_one)
    back_two, gain_two, shift_two = norm_pull_two(grad_norm_two)
    grad_input = (grad_rows + back_one + back_two)[None]
    column_out = jnp.sum(grad_rows, axis=0)
    vector_terms = jnp.concatenate(
        [
            jnp.stack([gain_one, shift_one, gain_two, shift_two]),
            jnp.sum(grad_proj.astype(jnp.float32), axis=0).reshape(3, model_width),
            column_out[None],
            jnp.sum(grad_upval.astype(jnp.float32), axis=0).reshape(4, model_width),
            column_out[None],
        ],
        axis=0,
    )
    grad_vectors = lax.psum_scatter(vector_terms, ("ctx", "shard"), scatter_dimension=1, tiled=True)
    block_count = (rows_in + rows_down) * lax.axis_size(("ctx", "shard")) // (rows_in + rows_down)
    first_block = jnp.int32(0) // (rows_in + rows_down)
    left_attn = attn_low
    left_hid = lax.dynamic_slice_in_dim(
        hid_low, first_block * rows_down, block_count * rows_down, 1
    )
    dense_part = jnp.einsum(
        "tr,td->rd", left_attn, grad_low, preferred_element_type=jnp.float32
    ).reshape(block_count, rows_in, model_width)
    down_part = jnp.einsum(
        "tr,td->rd", left_hid, grad_low, preferred_element_type=jnp.float32
    ).reshape(block_count, rows_down, model_width)
    out_grads = lax.psum_scatter(
        jnp.concatenate([dense_part, down_part], axis=1).reshape(
            (rows_in + rows_down) * lax.axis_size(("ctx", "shard")), model_width
        ),
        ("ctx", "shard"),
        scatter_dimension=0,
        tiled=True,
    )
    left_one = normed_one
    left_two = normed_two
    in_grads = lax.psum_scatter(
        jnp.concatenate(
            [
                jnp.einsum("tr,tc->rc", left_one, grad_proj, preferred_element_type=jnp.float32),
                jnp.einsum("tr,tc->rc", left_two, grad_upval, preferred_element_type=jnp.float32),
            ],
            axis=1,
        ),
        ("ctx", "shard"),
        scatter_dimension=0,
        tiled=True,
    )
    grad_qkv = in_grads[:, : 3 * model_width]
    grad_up = in_grads[:, 3 * model_width :]
    grad_dense = out_grads[:rows_in]
    grad_down = out_grads[rows_in:]
    new_qkv, second_qkv = adam_step(w_qkv, grad_qkv, m_qkv, v_qkv, 4.0 * (D // 2) ** (-0.5), 0.1)
    new_dense, second_dense = adam_step(
        w_dense, grad_dense, m_dense, v_dense, 4.0 * (D // 32) ** (-0.5), 0.1
    )
    new_up, second_up = adam_step(w_up, grad_up, m_up, v_up, 4.0 * D ** (-0.5), 0.1)
    new_down, second_down = adam_step(w_down, grad_down, m_down, v_down, 4.0 * FF ** (-0.5), 0.1)
    new_vectors, second_vectors = adam_step(vectors, grad_vectors, m_vectors, v_vectors, 1.0, 0.0)
    return (
        layer_output,
        grad_input,
        grad_qkv,
        grad_dense,
        grad_up,
        grad_down,
        grad_vectors,
        second_qkv,
        second_dense,
        second_up,
        second_down,
        second_vectors,
        new_qkv,
        new_dense,
        new_up,
        new_down,
        new_vectors,
    )


MESH = pl.DeviceIdType.MESH
VMEM_BYTES = 62 * 1024 * 1024


def push(source, target, sent, arrived, **device):
    return pltpu.make_async_remote_copy(
        src_ref=source,
        dst_ref=target,
        send_sem=sent,
        recv_sem=arrived,
        device_id=device,
        device_id_type=MESH,
    )


class Spot:
    def __init__(self, n_plane, n_shard):
        self.n_plane, self.n_shard = n_plane, n_shard
        self.plane = lax.axis_index("plane")
        self.core = lax.axis_index("core")
        self.shard = lax.axis_index("shard")
        self.slot = self.core * n_shard + self.shard
        head = 2 * self.plane + self.core
        self.head_core = lax.div(head, n_shard)
        self.head_shard = lax.rem(head, n_shard)
        self.owner_plane = lax.div(self.slot, 2)
        self.owner_core = lax.rem(self.slot, 2)
        self.head_here = jnp.logical_and(self.slot == head, self.plane == self.shard)

    def group(self):
        for turn in range(1, 2 * self.n_shard):
            yield turn - 1, self.turned(turn)

    def turned(self, turn):
        core = lax.rem(self.core + turn // self.n_shard, 2)
        shard = lax.rem(self.shard + turn % self.n_shard, self.n_shard)
        return dict(core=core, shard=shard)

    def beside(self):
        across = self.plane + 1 - 2 * lax.rem(self.plane, 2)
        return across, lax.rem(self.plane + 2, 4), 3 - self.plane

    def along(self):
        for step in range(1, self.n_shard):
            yield step - 1, lax.rem(self.shard + step, self.n_shard)

    def planes(self):
        for step in range(1, self.n_plane):
            yield step - 1, lax.rem(self.plane + step, self.n_plane)

    def keeper(self):
        return dict(plane=self.shard, core=self.head_core, shard=self.head_shard)

    def owner(self):
        return dict(plane=self.owner_plane, core=self.owner_core, shard=self.plane)

    def greet(self, sender):
        barrier = pltpu.get_barrier_semaphore()
        count = 0
        for _, device in self.group():
            pl.semaphore_signal(barrier, inc=1, device_id=device, device_id_type=MESH)
            count += 1
        for _, plane in self.planes():
            pl.semaphore_signal(barrier, inc=1, device_id=dict(plane=plane), device_id_type=MESH)
            count += 1

        @pl.when(jnp.logical_not(self.head_here))
        def _():
            pl.semaphore_signal(barrier, inc=1, device_id=sender, device_id_type=MESH)
            pl.semaphore_wait(barrier, count + 1)

        @pl.when(self.head_here)
        def _():
            pl.semaphore_wait(barrier, count)


def turn_tables(pos_row, freq):
    n_pos = pos_row.shape[1]
    places = jnp.broadcast_to(pos_row.astype(jnp.float32), (n_pos, n_pos)).T
    phase = places * freq
    return jnp.cos(phase), jnp.sin(phase), places


def turn(head, cosine, sine):
    half = ROT // 2
    lanes = cosine.shape[1]
    front = head[:, :lanes]
    lane = lax.broadcasted_iota(jnp.int32, front.shape, 1)
    first = jnp.where(lane < half, -sine, 0.0)
    second = jnp.where((lane >= half) & (lane < ROT), sine, 0.0)
    turned = (
        front * cosine
        + pltpu.roll(front, lanes - half, 1) * first
        + pltpu.roll(front, half, 1) * second
    )
    return jnp.concatenate([turned, head[:, lanes:]], axis=1)


def dot(left, right, left_dim=1, right_dim=0):
    return lax.dot_general(
        left, right, (((left_dim,), (right_dim,)), ((), ())), preferred_element_type=jnp.float32
    )


class Spread:
    def __init__(self, spot, ref, size, sent, here):
        self.spot, self.ref, self.size, self.sent, self.here = spot, ref, size, sent, here
        self.across, self.along, self.diagonal = spot.beside()

    def rows(self, plane, part=None):
        size = self.size
        if part is None:
            return self.ref.at[pl.ds(pl.multiple_of(plane * size, size), size)]
        half = size // 2
        return self.ref.at[pl.ds(pl.multiple_of(plane * size + part * half, half), half)]

    def send(self, rows, place, plane):
        return push(rows, rows, self.sent.at[place], self.here.at[place], plane=plane)

    def first(self):
        own = self.rows(self.spot.plane)
        return [self.send(own, 0, self.across), self.send(own, 1, self.along)]

    def second(self):
        return [
            self.send(self.rows(self.along, 0), 2, self.across),
            self.send(self.rows(self.across, 1), 3, self.along),
        ]

    def start(self):
        for copy in self.first():
            copy.start()

    def relay(self):
        first, second = self.first(), self.second()
        first[1].wait_recv()
        second[0].start()
        first[0].wait_recv()
        second[1].start()

    def finish(self):
        for copy in self.second():
            copy.wait_recv()

    def finish_sends(self):
        for copy in self.first() + self.second():
            copy.wait_send()


class Gather:
    def __init__(self, spot, part, size, landed, sent, here):
        self.spot, self.part, self.size, self.landed = spot, part, size, landed
        self.sent, self.here = sent, here
        self.across, self.along, self.diagonal = spot.beside()

    def rows(self, plane, side):
        half = self.size // 2
        return self.part.at[pl.ds(pl.multiple_of(plane * self.size + side * half, half), half)]

    def send(self, rows, place, plane):
        return push(
            rows, self.landed.at[place], self.sent.at[place], self.here.at[place], plane=plane
        )

    def first(self):
        return [
            self.send(self.rows(self.diagonal, 0), 0, self.across),
            self.send(self.rows(self.diagonal, 1), 1, self.along),
            self.send(self.rows(self.across, 0), 2, self.across),
            self.send(self.rows(self.along, 1), 3, self.along),
        ]

    def second(self):
        return [
            self.send(self.rows(self.along, 0), 4, self.along),
            self.send(self.rows(self.across, 1), 5, self.across),
        ]

    def start(self):
        for copy in self.first():
            copy.start()

    def relay(self):
        first, second = self.first(), self.second()
        for side in range(2):
            first[side].wait_recv()
            held = self.rows(self.along if side == 0 else self.across, side)
            add_rows(held, [held, self.landed.at[side]], self.size // 2)
            second[side].start()

    def own(self):
        size = self.size
        return self.part.at[pl.ds(pl.multiple_of(self.spot.plane * size, size), size)]

    def finish(self):
        first, second = self.first(), self.second()
        half = self.size // 2
        for side in range(2):
            first[2 + side].wait_recv()
            second[side].wait_recv()
            held = self.rows(self.spot.plane, side)
            add_rows(held, [held, self.landed.at[2 + side], self.landed.at[4 + side]], half)

    def finish_sends(self):
        for copy in self.first() + self.second():
            copy.wait_send()


class RowSum:
    def __init__(self, spot, part, landed, sent, here):
        self.spot, self.part, self.landed = spot, part, landed
        self.sent, self.here = sent, here

    def rows(self, shard):
        return self.part.at[shard]

    def place(self, side, at, shard):
        if side == 0:
            return shard
        return jnp.where(shard == at, self.spot.n_shard, shard)

    def hop(self, side, shard):
        spot = self.spot
        to = spot.shard + (1 if side == 0 else -1)
        return push(
            self.rows(shard),
            self.landed.at[self.place(side, to, shard)],
            self.sent.at[side, shard],
            self.here.at[side, shard],
            shard=to,
        )

    def wait(self, side, shard):
        spot = self.spot
        push(
            self.rows(shard),
            self.landed.at[self.place(side, spot.shard, shard)],
            self.sent.at[side, shard],
            self.here.at[side, shard],
            shard=spot.shard,
        ).wait_recv()

    def start(self):
        spot, last = self.spot, self.spot.n_shard - 1
        for side in range(2):

            @pl.when(spot.shard == (0 if side == 0 else last))
            def _():
                for step in range(last):
                    self.hop(side, last - step if side == 0 else step).start()

    def relay(self, turn):
        spot, last = self.spot, self.spot.n_shard - 1
        for side in range(2):
            depth = spot.shard if side == 0 else last - spot.shard
            shard = last - turn + spot.shard if side == 0 else turn - last + spot.shard

            @pl.when(jnp.logical_and(depth >= 1, depth <= turn))
            def _():
                self.wait(side, shard)
                held = self.rows(shard)
                came = self.landed.at[self.place(side, spot.shard, shard)]
                add_rows(held, [held, came], held.shape[0])
                self.hop(side, shard).start()

    def finish(self, target):
        spot, last = self.spot, self.spot.n_shard - 1
        held = self.rows(spot.shard)
        first = self.landed.at[self.place(0, spot.shard, spot.shard)]
        second = self.landed.at[self.place(1, spot.shard, spot.shard)]

        @pl.when(spot.shard >= 1)
        def _():
            self.wait(0, spot.shard)

        @pl.when(spot.shard < last)
        def _():
            self.wait(1, spot.shard)

        @pl.when(spot.shard == 0)
        def _():
            add_rows(target, [held, second], held.shape[0])

        @pl.when(spot.shard == last)
        def _():
            add_rows(target, [held, first], held.shape[0])

        @pl.when(jnp.logical_and(spot.shard >= 1, spot.shard < last))
        def _():
            add_rows(target, [held, first, second], held.shape[0])

    def finish_sends(self):
        spot = self.spot
        for shard in range(spot.n_shard):
            for side in range(2):

                @pl.when(spot.shard < shard if side == 0 else spot.shard > shard)
                def _():
                    self.hop(side, shard).wait_send()


class Chain:
    def __init__(self, spot, ref, block, sent, here, pair_sent, pair_here):
        self.spot, self.ref, self.block = spot, ref, block
        self.sent, self.here = sent, here
        self.pair_sent, self.pair_here = pair_sent, pair_here

    def rows(self, shard, core):
        start = pl.multiple_of((shard * 2 + core) * self.block, self.block)
        return self.ref.at[pl.ds(start, self.block)]

    def hop(self, side, dist):
        spot = self.spot
        sign = 1 if side == 0 else -1
        rows = self.rows(spot.shard - sign * dist, spot.core)
        return push(
            rows, rows, self.sent.at[side, dist], self.here.at[side, dist], shard=spot.shard + sign
        )

    def pair(self, side, dist):
        spot = self.spot
        sign = 1 if side == 0 else -1
        rows = self.rows(spot.shard - sign * dist, spot.core)
        return push(
            rows,
            rows,
            self.pair_sent.at[side, dist],
            self.pair_here.at[side, dist],
            core=1 - spot.core,
        )

    def holds(self, side, dist):
        spot = self.spot
        return spot.shard >= dist if side == 0 else spot.shard + dist < spot.n_shard

    def goes(self, side, dist):
        spot = self.spot
        more = spot.shard + 1 < spot.n_shard if side == 0 else spot.shard >= 1
        return jnp.logical_and(self.holds(side, dist), more)

    def start(self):
        for side in range(2):

            @pl.when(self.goes(side, 0))
            def _():
                self.hop(side, 0).start()

        self.pair(0, 0).start()

    def step(self, dist):
        for side in range(2):

            @pl.when(self.holds(side, dist))
            def _():
                self.hop(side, dist - 1).wait_recv()
                if dist + 1 < self.spot.n_shard:

                    @pl.when(self.goes(side, dist))
                    def _():
                        self.hop(side, dist).start()

                self.pair(side, dist).start()

    def finish_pairs(self):
        self.pair(0, 0).wait_recv()
        for dist in range(1, self.spot.n_shard):
            for side in range(2):

                @pl.when(self.holds(side, dist))
                def _():
                    self.pair(side, dist).wait_recv()

    def finish_sends(self):
        self.pair(0, 0).wait_send()
        for side in range(2):
            for dist in range(self.spot.n_shard - 1):

                @pl.when(self.goes(side, dist))
                def _():
                    self.hop(side, dist).wait_send()

            for dist in range(1, self.spot.n_shard):

                @pl.when(self.holds(side, dist))
                def _():
                    self.pair(side, dist).wait_send()


def forward_kernel(
    n_plane,
    n_shard,
    x_ref,
    dy_ref,
    pos_ref,
    vec_ref,
    freq_ref,
    wq_ref,
    wu_ref,
    wd_ref,
    wo_ref,
    x_out,
    dy_out,
    one_out,
    two_out,
    hid_out,
    gup_out,
    back_out,
    wq_out,
    wu_out,
    wd_out,
    wo_out,
    vec_out,
    moments_out,
    x_all,
    dy_all,
    one,
    two,
    wq_all,
    wu_all,
    wd_all,
    wo_all,
    vec_all,
    pos_all,
    full_vec,
    wu_raw,
    wd_raw,
    wo_raw,
    wq_cut,
    wu_cut,
    wo_cut,
    to_heads,
    heads,
    from_heads,
    back,
    grad_k,
    grad_v,
    cos_head,
    sin_head,
    place_head,
    cos_row,
    sin_row,
    key_row,
    probs,
    slope,
    attention,
    moments,
    loads,
    stores,
    local,
    x_sent,
    x_here,
    x_pair_sent,
    x_pair_here,
    dy_sent,
    dy_here,
    dy_pair_sent,
    dy_pair_here,
    pos_sent,
    pos_here,
    cols_sent,
    cols_here,
    flat_sent,
    flat_here,
    spread_sent,
    spread_here,
    swap_sent,
    swap_here,
    head_sent,
    head_here,
):
    spot = Spot(n_plane, n_shard)
    plane, core, shard, slot = spot.plane, spot.core, spot.shard, spot.slot
    f32, bf16 = jnp.float32, jnp.bfloat16
    block = x_ref.shape[0]
    pair = 2 * block
    n_slice = 2 * n_shard
    rows_in, rows_down = wq_ref.shape[0], wd_ref.shape[0]
    width = x_ref.shape[1]
    n_group = n_slice * block

    def piece(ref, at, size):
        return ref.at[pl.ds(pl.multiple_of(at * size, size), size)]

    chain_x = Chain(spot, x_all, block, x_sent, x_here, x_pair_sent, x_pair_here)
    chain_dy = Chain(spot, dy_all, block, dy_sent, dy_here, dy_pair_sent, dy_pair_here)

    raw = [
        pltpu.make_async_copy(source, held, loads.at[place])
        for place, (source, held) in enumerate(
            [
                (wq_ref, wu_raw.at[:, pl.ds(0, wq_ref.shape[1])]),
                (wu_ref, wu_raw),
                (wd_ref, wd_raw),
                (wo_ref, wo_raw),
                (x_ref, chain_x.rows(shard, core)),
                (dy_ref, chain_dy.rows(shard, core)),
                (pos_ref, pos_all.at[shard]),
                (vec_ref, vec_all.at[plane, slot]),
            ]
        )
    ]
    for place, copy in enumerate(raw):
        if place != 1:
            copy.start()
    spot.greet(spot.owner())

    index = plane * n_slice + slot
    wq_own = piece(wq_all, index, rows_in)
    wu_own = piece(wu_all, index, rows_in)

    def to_group(place, source, target):
        return [
            push(
                source(device["core"] * n_shard + device["shard"]),
                target,
                cols_sent.at[place, turn_at],
                cols_here.at[place, turn_at],
                **device,
            )
            for turn_at, device in spot.group()
        ]

    cols_q = to_group(0, lambda to: wq_cut.at[to], wq_own)
    cols_u = to_group(1, lambda to: wu_cut.at[to], wu_own)
    cols_v = to_group(2, lambda to: vec_all.at[plane, slot], vec_all.at[plane, slot])

    def to_planes(place, ref):
        return [
            push(ref, ref, flat_sent.at[place, turn_at], flat_here.at[place, turn_at], plane=to)
            for turn_at, to in spot.planes()
        ]

    group_rows = n_slice * rows_in
    spread_d = Spread(spot, wd_all, rows_down, spread_sent.at[0], spread_here.at[0])
    spread_q = Spread(spot, wq_all, group_rows, spread_sent.at[1], spread_here.at[1])
    spread_u = Spread(spot, wu_all, group_rows, spread_sent.at[2], spread_here.at[2])
    flat_v = to_planes(0, vec_all.at[plane])
    flat_o = to_planes(1, piece(wo_all, plane, rows_in))
    pos_push = [
        push(
            pos_all.at[shard],
            pos_all.at[shard],
            pos_sent.at[turn_at],
            pos_here.at[turn_at],
            shard=to,
        )
        for turn_at, to in spot.along()
    ]

    raw[6].wait()
    raw[7].wait()
    for copy in cols_v + pos_push:
        copy.start()

    raw[4].wait()
    chain_x.start()
    raw[0].wait()
    for to in range(n_slice):
        for part in range(3):
            wq_cut[to, :, part * HD : (part + 1) * HD] = wu_raw[
                :, part * width + to * HD : part * width + (to + 1) * HD
            ].astype(bf16)
    raw[1].start()
    for copy in cols_q:
        copy.start()
    keep_q = pltpu.make_async_copy(wq_cut.at[slot], wq_own, local.at[0])
    keep_q.start()
    for copy in cols_v:
        copy.wait_recv()
    for copy in flat_v:
        copy.start()
    raw[2].wait()

    down_at = plane * rows_down

    @pl.loop(0, rows_down // 32)
    def _(step):
        at = pl.multiple_of(step * 32, 32)
        wd_all[pl.ds(pl.multiple_of(down_at + at, 32), 32), :] = wd_raw[pl.ds(at, 32), :].astype(bf16)

    spread_d.start()
    raw[1].wait()
    for to in range(n_slice):
        for part in range(n_plane):
            wu_cut[to, :, part * rows_down : (part + 1) * rows_down] = wu_raw[
                :, part * width + to * rows_down : part * width + (to + 1) * rows_down
            ].astype(bf16)
    for copy in cols_u:
        copy.start()
    keep_u = pltpu.make_async_copy(wu_cut.at[slot], wu_own, local.at[1])
    keep_u.start()
    raw[3].wait()
    wo_cut[...] = wo_raw[...].astype(bf16)
    head_rows = piece(wo_all, shard, rows_in)
    to_head = push(wo_cut, head_rows, head_sent, head_here, **spot.keeper())
    own_head = pltpu.make_async_copy(wo_cut, head_rows, head_sent)

    @pl.when(spot.head_here)
    def _():
        own_head.start()

    @pl.when(jnp.logical_not(spot.head_here))
    def _():
        to_head.start()

    for copy in pos_push:
        copy.wait_recv()
    freq = freq_ref[...]
    own_blocks = 2 * plane

    @pl.loop(0, n_shard)
    def _(seq):
        for half in range(2):
            at = pl.ds(pl.multiple_of(seq * pair + half * block, block), block)
            cosine, sine, _ = turn_tables(pos_all[seq, pl.ds(own_blocks + half, 1), :], freq)
            cos_row[at, :] = cosine
            sin_row[at, :] = sine

    raw[5].wait()
    for copy in flat_v:
        copy.wait_recv()
    n_vec, lanes = vec_all.shape[2:]
    lane = lax.broadcasted_iota(jnp.int32, (n_vec, lanes), 1)
    for p in range(n_plane):
        for t in range(0, n_slice, 2):
            at = (p * n_slice + t) * (lanes // 2)
            full_vec[:, at : at + lanes] = jnp.where(
                lane < lanes // 2, vec_all[p, t], pltpu.roll(vec_all[p, t + 1], lanes // 2, 1)
            )
    save_vec = pltpu.make_async_copy(full_vec, vec_out, stores.at[0])
    save_vec.start()

    def norm_rows(seq):
        @pl.loop(0, pair // 32)
        def _(step):
            at = pl.ds(pl.multiple_of(seq * pair + step * 32, 32), 32)
            tokens = x_all[at, :].astype(f32)
            mean = jnp.mean(tokens, axis=-1, keepdims=True)
            center = tokens - mean
            scale = lax.rsqrt(jnp.mean(center * center, axis=-1, keepdims=True) + 1e-05)
            lane = lax.broadcasted_iota(jnp.int32, (32, moments.shape[1]), 1)
            moments[at, :] = jnp.where(lane < 1, mean, scale)
            hat = center * scale
            one[at, :] = (hat * full_vec[0:1, :] + full_vec[1:2, :]).astype(bf16)
            two[at, :] = (hat * full_vec[2:3, :] + full_vec[3:4, :]).astype(bf16)

    def norm_came(dist):
        for side in range(2):

            @pl.when(chain_x.holds(side, dist))
            def _():
                chain_x.pair(side, dist).wait_recv()
                norm_rows(shard - dist if side == 0 else shard + dist)

    chain_x.step(1)
    chain_x.pair(0, 0).wait_recv()
    norm_rows(shard)
    spread_d.relay()
    keep_q.wait()
    for copy in cols_q:
        copy.wait_recv()
    spread_q.start()
    norm_came(1)
    chain_x.step(2)
    chain_dy.start()
    spread_q.relay()
    norm_came(2)
    keep_u.wait()
    for copy in cols_u:
        copy.wait_recv()
    spread_u.start()

    @pl.loop(0, n_plane)
    def _(part):
        for half in range(2):
            at = pl.ds(pl.multiple_of(part * pair + half * block, block), block)
            cosine, sine, places = turn_tables(pos_all[plane, pl.ds(2 * part + half, 1), :], freq)
            cos_head[at, :] = cosine
            sin_head[at, :] = sine
            place_head[at, :] = places

    for at in range(pos_all.shape[1]):
        key_row[:, at * block : (at + 1) * block] = pos_all[plane, pl.ds(at, 1), :].astype(f32)

    for dist in range(3, n_shard):
        chain_x.step(dist)

    @pl.when(spot.head_here)
    def _():
        own_head.wait()

    @pl.when(jnp.logical_not(spot.head_here))
    def _():
        to_head.wait_recv()

    for copy in flat_o:
        copy.start()


    chain_dy.step(1)
    for dist in range(3, n_shard):
        norm_came(dist)
    save_x = pltpu.make_async_copy(x_all, x_out, stores.at[1])
    save_x.start()
    spread_u.relay()
    chain_dy.step(2)
    save_moments = pltpu.make_async_copy(moments, moments_out, stores.at[12])
    save_moments.start()
    save_one = pltpu.make_async_copy(one, one_out, stores.at[2])
    save_one.start()
    save_two = pltpu.make_async_copy(two, two_out, stores.at[3])
    save_two.start()

    spread_q.finish()
    save_wq = pltpu.make_async_copy(wq_all, wq_out, stores.at[4])
    save_wq.start()
    head_lanes = pl.ds(pl.multiple_of(slot * HD, HD), HD)

    def swap(place, source, target, cols, to, turn_at):
        def piece_of(ref, at):
            return ref.at[pl.ds(pl.multiple_of(at * pair, pair), pair), cols]

        return push(
            piece_of(source, to),
            piece_of(target, plane),
            swap_sent.at[place, turn_at - 1],
            swap_here.at[place, turn_at - 1],
            plane=to,
        )

    def keep_own(place, source, target, cols):
        at = pl.ds(pl.multiple_of(plane * pair, pair), pair)
        return pltpu.make_async_copy(source.at[at, cols], target.at[at, cols], local.at[place])

    def swaps(place, source, target, cols):
        return [
            swap(place, source, target, cols, lax.rem(plane + turn_at, n_plane), turn_at)
            for turn_at in range(1, n_plane)
        ]

    qkv_cols = pl.ds(0, 3 * HD)
    q_cols, kv_cols, o_cols = pl.ds(0, HD), pl.ds(HD, 2 * HD), pl.ds(3 * HD, HD)

    for step in range(2):
        at = slice(step * 2 * pair, (step + 1) * 2 * pair)
        heads_now = dot(one[at, :], wq_all[...])
        for part in range(3):
            cols = slice(part * HD, (part + 1) * HD)
            value = heads_now[:, cols] + full_vec[4 + part : 5 + part, head_lanes]
            if part < 2:
                value = turn(value, cos_row[at, :], sin_row[at, :])
            to_heads[at, cols] = value.astype(bf16)

    for copy in swaps(0, to_heads, heads, qkv_cols):
        copy.start()
    keep_qkv = keep_own(2, to_heads, heads, qkv_cols)
    keep_qkv.start()

    spread_u.finish()
    save_wu = pltpu.make_async_copy(wu_all, wu_out, stores.at[8])
    save_wu.start()
    save_one.wait()
    up_lanes = pl.ds(pl.multiple_of(slot * rows_down, rows_down), rows_down)
    n_hid = n_plane * rows_down

    def hidden_rows(step):
        at = pl.ds(pl.multiple_of(step * pair, pair), pair)
        hidden = dot(two[at, :], wu_all[...])
        for part in range(n_plane):
            cols = slice(part * rows_down, (part + 1) * rows_down)
            value = hidden[:, cols] + full_vec[8 + part : 9 + part, up_lanes]
            half = 0.5 + 0.5 * lax.erf(value * 0.7071067811865476)
            slope[at, cols] = half + value * (0.3989422804014327 * jnp.exp(-0.5 * value * value))
            one[at, cols] = (value * half).astype(bf16)

    @pl.loop(0, n_shard // 2)
    def _(step):
        hidden_rows(step)

    for dist in range(3, n_shard):
        chain_dy.step(dist)

    @pl.loop(n_shard // 2, n_shard)
    def _(step):
        hidden_rows(step)

    save_hid = pltpu.make_async_copy(one.at[:, 0:n_hid], hid_out, stores.at[9])
    save_hid.start()

    chain_dy.finish_pairs()
    save_dy = pltpu.make_async_copy(dy_all, dy_out, stores.at[5])
    save_dy.start()
    for copy in flat_o:
        copy.wait_recv()
    save_wo = pltpu.make_async_copy(wo_all, wo_out, stores.at[6])
    save_wo.start()

    @pl.loop(0, 2)
    def _(step):
        at = pl.ds(pl.multiple_of(step * 2 * pair, 2 * pair), 2 * pair)
        to_heads[at, 3 * HD : 4 * HD] = dot(dy_all[at, :], wo_all[...], 1, 1).astype(bf16)

    for copy in swaps(1, to_heads, heads, o_cols):
        copy.start()
    keep_o = keep_own(3, to_heads, heads, o_cols)
    keep_o.start()

    grad_k[...] = jnp.zeros_like(grad_k)
    grad_v[...] = jnp.zeros_like(grad_v)
    scale = HD ** (-0.5)
    keep_qkv.wait()
    for copy in swaps(0, to_heads, heads, qkv_cols):
        copy.wait_recv()

    @pl.loop(0, n_plane)
    def _(part):
        at = pl.ds(pl.multiple_of(part * pair, pair), pair)
        places = place_head[at, 0:1]
        scores = dot(heads[at, 0:HD], heads[:, HD : 2 * HD], 1, 1) * scale
        scores = jnp.where(key_row[...] <= places, scores, -1e30)
        weights = jnp.exp(scores - jnp.max(scores, axis=-1, keepdims=True))
        share = weights / jnp.sum(weights, axis=-1, keepdims=True)
        probs[at, :] = share
        value = dot(share.astype(bf16), heads[:, 2 * HD : 3 * HD])
        attention[at, :] = value
        from_heads[at, 3 * HD : 4 * HD] = value.astype(bf16)

    for copy in swaps(2, from_heads, back, o_cols):
        copy.start()

    keep_o.wait()
    for copy in swaps(1, to_heads, heads, o_cols):
        copy.wait_recv()

    @pl.loop(0, n_plane)
    def _(step):
        turn_at = lax.rem(step + 1, n_plane)
        part = lax.rem(plane + turn_at, n_plane)
        at = pl.ds(pl.multiple_of(part * pair, pair), pair)
        grad_out = heads[at, 3 * HD : 4 * HD]
        delta = jnp.sum(grad_out.astype(f32) * attention[at, :], axis=-1, keepdims=True)
        grad_prob = dot(grad_out, heads[:, 2 * HD : 3 * HD], 1, 1)
        share = probs[at, :]
        dscore = (share * (grad_prob - delta)).astype(bf16)
        grad_q = dot(dscore, heads[:, HD : 2 * HD]) * scale
        from_heads[at, 0:HD] = turn(grad_q, cos_head[at, :], -sin_head[at, :]).astype(bf16)

        @pl.when(turn_at > 0)
        def _():
            swap(3, from_heads, back, q_cols, part, turn_at).start()

        grad_k[...] += dot(dscore, heads[at, 0:HD], 0, 0)
        grad_v[...] += dot(share.astype(bf16), grad_out, 0, 0)

    @pl.loop(0, n_plane)
    def _(step):
        turn_at = lax.rem(step + 1, n_plane)
        part = lax.rem(plane + turn_at, n_plane)
        at = pl.ds(pl.multiple_of(part * pair, pair), pair)
        turned = turn(grad_k[at, :] * scale, cos_head[at, :], -sin_head[at, :])
        from_heads[at, HD : 2 * HD] = turned.astype(bf16)
        from_heads[at, 2 * HD : 3 * HD] = grad_v[at, :].astype(bf16)

        @pl.when(turn_at > 0)
        def _():
            swap(4, from_heads, back, kv_cols, part, turn_at).start()

    keep_back = keep_own(2, from_heads, back, pl.ds(0, 4 * HD))
    keep_back.start()

    spread_d.finish()
    save_wd = pltpu.make_async_copy(wd_all, wd_out, stores.at[7])
    save_wd.start()

    @pl.loop(0, n_shard)
    def _(step):
        at = pl.ds(pl.multiple_of(step * pair, pair), pair)
        one[at, n_hid : 2 * n_hid] = (dot(dy_all[at, :], wd_all[...], 1, 1) * slope[at, :]).astype(
            bf16
        )

    save_gup = pltpu.make_async_copy(one.at[:, n_hid : 2 * n_hid], gup_out, stores.at[10])
    save_gup.start()
    keep_back.wait()
    again = (
        swaps(2, from_heads, back, o_cols)
        + swaps(3, from_heads, back, q_cols)
        + swaps(4, from_heads, back, kv_cols)
    )
    for copy in again:
        copy.wait_recv()
    save_back = pltpu.make_async_copy(back, back_out, stores.at[11])
    save_back.start()

    @pl.when(jnp.logical_not(spot.head_here))
    def _():
        to_head.wait_send()

    chain_x.finish_sends()
    chain_dy.finish_sends()
    for copy in cols_q + cols_u + cols_v + pos_push:
        copy.wait_send()
    for spread in [spread_d, spread_q, spread_u]:
        spread.finish_sends()
    again += swaps(0, to_heads, heads, qkv_cols) + swaps(1, to_heads, heads, o_cols)
    for copy in flat_v + flat_o + again:
        copy.wait_send()
    for copy in [
        save_vec,
        save_moments,
        save_x,
        save_two,
        save_wq,
        save_dy,
        save_wo,
        save_wd,
        save_wu,
        save_hid,
        save_gup,
        save_back,
    ]:
        copy.wait()


def forward_all(n_plane, n_shard, x, dy, pos, vec, freq, wq, wu, wd, wo):
    f32, bf16 = jnp.float32, jnp.bfloat16
    n_slice = 2 * n_shard
    block, width = x.shape
    rows_in, rows_down = wq.shape[0], wd.shape[0]
    group = n_slice * block
    n_hid = n_plane * rows_down
    cols_q = 3 * HD
    n_vec, lanes = vec.shape
    dma = pltpu.SemaphoreType.DMA
    vmem = pltpu.VMEM
    shape = jax.ShapeDtypeStruct
    anywhere = pl.BlockSpec(memory_space=pl.ANY)
    far, near = n_shard - 1, n_plane - 1
    return pl.pallas_call(
        partial(forward_kernel, n_plane, n_shard),
        out_shape=[
            shape((group, width), bf16),
            shape((group, width), bf16),
            shape((group, width), bf16),
            shape((group, width), bf16),
            shape((group, n_hid), bf16),
            shape((group, n_hid), bf16),
            shape((group, 4 * HD), bf16),
            shape((width, cols_q), bf16),
            shape((width, n_hid), bf16),
            shape((n_hid, width), bf16),
            shape((HD, width), bf16),
            shape((n_vec, width), f32),
            shape((group, block), f32),
        ],
        in_specs=[anywhere] * 4 + [pl.BlockSpec(memory_space=vmem)] + [anywhere] * 4,
        out_specs=[anywhere] * 13,
        scratch_shapes=[
            vmem((group, width), bf16),
            vmem((group, width), bf16),
            vmem((group, width), bf16),
            vmem((group, width), bf16),
            vmem((width, cols_q), bf16),
            vmem((width, n_hid), bf16),
            vmem((n_hid, width), bf16),
            vmem((HD, width), bf16),
            vmem((n_plane, n_slice, n_vec, lanes), f32),
            vmem((n_shard, *pos.shape), jnp.int32),
            vmem((n_vec, width), f32),
            vmem(wu.shape, f32),
            vmem(wd.shape, f32),
            vmem(wo.shape, f32),
            vmem((n_slice, rows_in, cols_q), bf16),
            vmem((n_slice, rows_in, n_hid), bf16),
            vmem(wo.shape, bf16),
            vmem((group, 4 * HD), bf16),
            vmem((group, 4 * HD), bf16),
            vmem((group, 4 * HD), bf16),
            vmem((group, 4 * HD), bf16),
            vmem((group, HD), f32),
            vmem((group, HD), f32),
            *([vmem((group, block), f32)] * 5),
            vmem((1, group), f32),
            vmem((group, group), f32),
            vmem((group, n_hid), f32),
            vmem((group, HD), f32),
            vmem((group, block), f32),
            dma((8,)),
            dma((13,)),
            dma((4,)),
            *([dma((2, n_shard))] * 8),
            dma((far,)),
            dma((far,)),
            dma((3, n_slice - 1)),
            dma((3, n_slice - 1)),
            dma((2, near)),
            dma((2, near)),
            dma((3, 4)),
            dma((3, 4)),
            dma((5, near)),
            dma((5, near)),
            dma,
            dma,
        ],
        compiler_params=pltpu.CompilerParams(
            collective_id=0, has_side_effects=True, vmem_limit_bytes=VMEM_BYTES
        ),
        name="forward_all",
    )(x, dy, pos, vec, freq, wq, wu, wd, wo)


def add_rows(target, terms, rows):
    columns = target.shape[1]
    chunk = min(rows, 64 if columns <= 1024 else 32)

    @pl.loop(0, rows // chunk)
    def _(step):
        at = pl.ds(pl.multiple_of(step * chunk, chunk), chunk)
        for start in range(0, columns, 256):
            cols = slice(start, start + 256)
            total = terms[0][at, cols].astype(jnp.float32)
            for term in terms[1:]:
                total = total + term[at, cols].astype(jnp.float32)
            target[at, cols] = total.astype(target.dtype)


def backward_kernel(
    n_plane,
    n_shard,
    x_ref,
    dy_ref,
    one_ref,
    two_ref,
    hid_ref,
    gup_ref,
    back_ref,
    wq_ref,
    wu_ref,
    wd_ref,
    wo_ref,
    vec_ref,
    moments_ref,
    out_sum,
    hat_sum,
    dq_sum,
    du_sum,
    dd_sum,
    do_sum,
    vec_sum,
    big_one,
    big_two,
    big_three,
    x_rows,
    hid,
    gup,
    back,
    wq,
    wo,
    vec,
    moments,
    rows_part,
    other_half,
    theirs,
    parts,
    q_part,
    u_part,
    o_part,
    v_part,
    q_in,
    u_in,
    d_in,
    o_in,
    v_in,
    o_mid,
    v_mid,
    v_end,
    loads,
    local,
    pair_sent,
    pair_here,
    rows_sent,
    rows_here,
    flat_sent,
    flat_here,
    sum_sent,
    sum_here,
    cols_sent,
    cols_here,
    head_sent,
    head_here,
    x_sem,
    free,
):
    spot = Spot(n_plane, n_shard)
    plane, core, shard, slot = spot.plane, spot.core, spot.shard, spot.slot
    f32, bf16 = jnp.float32, jnp.bfloat16
    n_slice = 2 * n_shard
    n_group, width = dy_ref.shape
    block = n_group // n_slice
    pair = 2 * block
    rows_down = width // n_slice
    cols_q = 3 * HD
    n_hid = hid_ref.shape[1]
    rows_plane = width // n_plane
    rows_in = rows_plane // n_slice

    def load(source, target, place):
        copy = pltpu.make_async_copy(source, target, loads.at[place])
        copy.start()
        return copy

    def plane_rows(ref, at):
        return ref.at[pl.ds(pl.multiple_of(at * pair, pair), pair)]

    load_two = load(two_ref, big_three, 0)
    load_hid = load(hid_ref, hid, 1)
    load_dy = load(dy_ref, big_one, 2)
    load_back = load(back_ref, back, 3)
    load_wo = load(wo_ref, wo, 4)
    load_wd = load(wd_ref, big_two, 5)
    load_gup = load(gup_ref, gup, 7)
    load_wq = load(wq_ref, wq, 8)
    load_vec = load(vec_ref, vec, 9)
    load_moments = load(moments_ref, moments, 10)
    spot.greet(spot.keeper())

    def flat(place, source, target):
        return [
            push(
                source(to),
                target.at[turn_at],
                flat_sent.at[place, turn_at],
                flat_here.at[place, turn_at],
                plane=to,
            )
            for turn_at, to in spot.planes()
        ]

    def at_plane(ref, size):
        return lambda to: ref.at[pl.ds(pl.multiple_of(to * size, size), size)]

    sum_u = Gather(spot, u_part, rows_plane, u_in, sum_sent.at[0], sum_here.at[0])
    sum_q = Gather(spot, q_part, rows_plane, q_in, sum_sent.at[1], sum_here.at[1])
    sum_d = Gather(spot, big_two, rows_down, d_in, sum_sent.at[2], sum_here.at[2])
    flat_o = flat(0, at_plane(o_part, rows_in), o_in)
    flat_v = flat(
        1,
        lambda to: v_part.at[:, pl.ds(pl.multiple_of(to * rows_plane, rows_plane), rows_plane)],
        v_in,
    )

    def weight_grad(left, right, target, columns):
        @pl.loop(0, left.shape[1] // 512)
        def _(step):
            at = pl.ds(pl.multiple_of(step * 512, 512), 512)
            turned = left[:, at].T
            for start in range(0, columns, n_group):
                cols = slice(start, min(start + n_group, columns))
                target[at, cols] = dot(turned, right[:, cols]).astype(bf16)

    sums = [
        RowSum(spot, rows_part.at[place], parts.at[place], rows_sent.at[place], rows_here.at[place])
        for place in range(2)
    ]

    def pair_push(place, seq):
        return push(
            other_half.at[seq],
            theirs.at[seq],
            pair_sent.at[place, seq],
            pair_here.at[place, seq],
            core=1 - core,
        )

    def put(place, seq, cols, total):
        first, second = total[:block], total[block:]
        rows_part[place, seq, :, cols] = jnp.where(core == 0, first, second).astype(bf16)
        other_half[seq, :, cols] = jnp.where(core == 0, second, first).astype(bf16)

    def add_pairs(place):
        @pl.loop(0, n_shard)
        def _(seq):
            pair_push(place, seq).wait_recv()
            held = rows_part.at[place, seq]
            add_rows(held, [held, theirs.at[seq]], block)

        sums[place].start()

    def add_shards(place, target):
        sums[place].finish(sums[place].rows(shard))
        copy = pltpu.make_async_copy(sums[place].rows(shard), target, local.at[2, 1 + place])
        copy.start()
        return copy

    def regroup(place, held, target, wide):
        base = pl.multiple_of(plane * rows_plane, rows_plane)
        parts_here = held.shape[1] // wide

        def rows(to, part):
            start = pl.multiple_of(base + to * rows_in, rows_in)
            return held.at[pl.ds(start, rows_in), pl.ds(part * wide, wide)]

        def lands(part):
            start = pl.multiple_of(part * width + slot * wide, wide)
            return target.at[:, pl.ds(start, wide)]

        copies = []
        for turn_at, device in spot.group():
            to = device["core"] * n_shard + device["shard"]
            for part in range(parts_here):
                copies.append(
                    push(
                        rows(to, part),
                        lands(part),
                        cols_sent.at[place, turn_at, part],
                        cols_here.at[place, turn_at, part],
                        **device,
                    )
                )
        keeps = [
            pltpu.make_async_copy(rows(slot, part), lands(part), local.at[place, part])
            for part in range(parts_here)
        ]
        for copy in copies + keeps:
            copy.start()
        return copies, keeps

    load_two.wait()
    load_gup.wait()
    weight_grad(big_three, gup, u_part, n_hid)
    sum_u.start()

    load_wu = [
        load(
            wu_ref.at[pl.ds(part * n_group, n_group)],
            big_three.at[:, pl.ds(part * n_hid, n_hid)],
            11 + part,
        )
        for part in range(width // n_group)
    ]

    load_hid.wait()
    load_back.wait()
    load_wo.wait()
    load_wd.wait()

    @pl.loop(0, n_shard)
    def _(seq):
        at = pl.ds(pl.multiple_of(seq * pair, pair), pair)
        for start in range(0, width, n_group):
            cols = slice(start, start + n_group)
            total = dot(back[at, cols_q : cols_q + HD], wo[:, cols])
            put(0, seq, cols, total + dot(hid[at, :], big_two[:, cols]))
        pair_push(0, seq).start()

    add_pairs(0)
    pl.semaphore_signal(free, inc=1, device_id=dict(core=1 - core), device_id_type=MESH)

    def x_load(seq):
        return pltpu.make_async_copy(plane_rows(x_ref, seq), x_rows, x_sem)

    x_load(0).start()
    v_part[...] = jnp.zeros_like(v_part)
    load_wq.wait()
    load_vec.wait()
    for copy in load_wu:
        copy.wait()
    load_moments.wait()
    for seq in range(n_shard):
        pair_push(0, seq).wait_send()
    pl.semaphore_wait(free, 1)

    def norm_rows(seq):
        at = pl.ds(pl.multiple_of(seq * pair, pair), pair)
        mean, scale = moments[at, 0:1], moments[at, 1:2]
        for start in range(0, width, 512):
            cols = slice(start, start + 512)
            up_rows = slice(start % n_group, start % n_group + 512)
            up_cols = slice(start // n_group * n_hid, (start // n_group + 1) * n_hid)
            grad_one = dot(back[at, 0:cols_q], wq[cols, :], 1, 1)
            grad_two = dot(gup[at, :], big_three[up_rows, up_cols], 1, 1)
            if start == 0:
                x_load(seq).wait()
            hat = (x_rows[:, cols].astype(f32) - mean) * scale
            v_part[0:1, cols] += jnp.sum(grad_one * hat, axis=0, keepdims=True)
            v_part[1:2, cols] += jnp.sum(grad_one, axis=0, keepdims=True)
            v_part[2:3, cols] += jnp.sum(grad_two * hat, axis=0, keepdims=True)
            v_part[3:4, cols] += jnp.sum(grad_two, axis=0, keepdims=True)
            put(1, seq, cols, grad_one * vec[0:1, cols] + grad_two * vec[2:3, cols])
        pair_push(1, seq).start()

        @pl.when(seq + 1 < n_shard)
        def _():
            x_load(seq + 1).start()


    @pl.loop(0, n_shard // 2)
    def _(seq):
        norm_rows(seq)

    sum_u.relay()
    sums[0].relay(1)

    @pl.loop(n_shard // 2, n_shard)
    def _(seq):
        norm_rows(seq)

    load_one = load(one_ref, big_three, 6)
    add_pairs(1)
    sum_u.finish()
    cols_u, keep_u = regroup(0, u_part, du_sum, rows_down)

    load_one.wait()
    weight_grad(big_three, back, q_part, cols_q)
    sum_q.start()
    sums[0].relay(2)
    sums[1].relay(1)

    load_dy.wait()
    weight_grad(hid, big_one, big_two, width)
    sum_q.relay()
    sum_d.start()
    attn = back[:, cols_q : cols_q + HD]
    half = width // 2
    for part in range(2):
        cols = slice(part * half, (part + 1) * half)
        o_part[:, cols] = dot(attn, big_one[:, cols], 0, 0).astype(bf16)
    for copy in flat_o:
        copy.start()

    own = pl.ds(pl.multiple_of((shard * 2 + core) * block, block), block)
    column_out = jnp.sum(big_one[own, :].astype(f32), axis=0, keepdims=True)
    v_part[7:8, :] = column_out
    v_part[12:13, :] = column_out
    lanes = pl.ds(pl.multiple_of(slot * HD, HD), HD)
    for part in range(3):
        cols = slice(part * HD, (part + 1) * HD)
        v_part[4 + part : 5 + part, lanes] = jnp.sum(
            back[:, cols].astype(f32), axis=0, keepdims=True
        )
    lanes = pl.ds(pl.multiple_of(slot * rows_down, rows_down), rows_down)
    for part in range(n_plane):
        cols = slice(part * rows_down, (part + 1) * rows_down)
        v_part[8 + part : 9 + part, lanes] = jnp.sum(
            gup[:, cols].astype(f32), axis=0, keepdims=True
        )
    for copy in flat_v:
        copy.start()
    sums[1].relay(2)
    save_out = add_shards(0, out_sum)
    sum_q.finish()
    cols_q_copies, keep_q = regroup(1, q_part, dq_sum, HD)
    save_hat = add_shards(1, hat_sum)
    sum_d.relay()

    for copy in flat_o:
        copy.wait_recv()
    mine = o_part.at[pl.ds(pl.multiple_of(plane * rows_in, rows_in), rows_in)]
    add_rows(o_mid, [mine] + [o_in.at[turn_at] for turn_at in range(n_plane - 1)], rows_in)
    to_owner = push(
        o_mid,
        do_sum,
        head_sent,
        head_here,
        plane=spot.owner_plane,
        core=spot.owner_core,
        shard=plane,
    )
    own_rows = pltpu.make_async_copy(o_mid, do_sum, head_sent)

    @pl.when(spot.head_here)
    def _():
        own_rows.start()

    @pl.when(jnp.logical_not(spot.head_here))
    def _():
        to_owner.start()

    for copy in flat_v:
        copy.wait_recv()
    total = v_part[:, pl.ds(pl.multiple_of(plane * rows_plane, rows_plane), rows_plane)]
    for turn_at in range(n_plane - 1):
        total = total + v_in[turn_at]
    v_mid[...] = total
    wide = 2 * rows_in

    def lanes_of(device):
        half_slot = device["core"] * n_shard + device["shard"]
        return pl.ds(pl.multiple_of(lax.div(half_slot, 2) * wide, wide), wide)

    v_end[slot] = v_mid[:, lanes_of(spot.turned(0))]
    cols_v = []
    for turn_at, device in spot.group():
        cols_v.append(
            push(
                v_mid.at[:, lanes_of(device)],
                v_end.at[slot],
                cols_sent.at[2, turn_at, 0],
                cols_here.at[2, turn_at, 0],
                **device,
            )
        )
    for copy in cols_v:
        copy.start()

    save_sums = [save_out, save_hat]
    sum_d.finish()
    save_d = pltpu.make_async_copy(sum_d.own(), dd_sum, local.at[2, 0])
    save_d.start()
    for copy in cols_v:
        copy.wait_recv()
    total = v_end[0]
    for other in range(1, n_slice):
        total = total + v_end[other]
    odd = lax.rem(slot, 2) == 1
    vec_sum[...] = jnp.where(odd, pltpu.roll(total, rows_in, 1), total)

    for copy in keep_u + keep_q:
        copy.wait()
    for copy in cols_u + cols_q_copies:
        copy.wait_recv()

    @pl.when(spot.head_here)
    def _():
        own_rows.wait()

    @pl.when(jnp.logical_not(spot.head_here))
    def _():
        to_owner.wait_recv()
        to_owner.wait_send()

    for seq in range(n_shard):
        pair_push(1, seq).wait_send()
    for place in range(2):
        sums[place].finish_sends()
    for copy in save_sums + [save_d]:
        copy.wait()
    for total in [sum_u, sum_q, sum_d]:
        total.finish_sends()
    for copy in flat_o + flat_v + cols_u + cols_q_copies + cols_v:
        copy.wait_send()


def backward_all(n_plane, n_shard, *arrays):
    x, dy, _, _, hid, _, back, wq, _, _, wo, vec, moments = arrays
    f32, bf16 = jnp.float32, jnp.bfloat16
    n_slice = 2 * n_shard
    group, width = dy.shape
    block = group // n_slice
    rows_down = width // n_slice
    rows_plane = width // n_plane
    rows_in = rows_plane // n_slice
    cols_q, n_hid = 3 * HD, hid.shape[1]
    n_vec = 16
    dma = pltpu.SemaphoreType.DMA
    vmem = pltpu.VMEM
    shape = jax.ShapeDtypeStruct
    near = n_plane - 1
    inside = pl.BlockSpec(memory_space=vmem)
    anywhere = pl.BlockSpec(memory_space=pl.ANY)
    return pl.pallas_call(
        partial(backward_kernel, n_plane, n_shard),
        out_shape=[
            shape((block, width), bf16),
            shape((block, width), bf16),
            shape((rows_in, n_slice * cols_q), bf16),
            shape((rows_in, n_slice * n_hid), bf16),
            shape((rows_down, width), bf16),
            shape((rows_in, width), bf16),
            shape((n_vec, 2 * rows_in), f32),
        ],
        in_specs=[anywhere] * 13,
        out_specs=[anywhere] * 6 + [inside],
        scratch_shapes=[
            vmem((group, width), bf16),
            vmem((group, width), bf16),
            vmem((group, width), bf16),
            vmem((2 * block, width), bf16),
            vmem(hid.shape, bf16),
            vmem(hid.shape, bf16),
            vmem(back.shape, bf16),
            vmem(wq.shape, bf16),
            vmem(wo.shape, bf16),
            vmem(vec.shape, f32),
            vmem(moments.shape, f32),
            vmem((2, n_shard, block, width), bf16),
            vmem((n_shard, block, width), bf16),
            vmem((n_shard, block, width), bf16),
            vmem((2, n_shard + 1, block, width), bf16),
            vmem((width, cols_q), bf16),
            vmem((width, n_hid), bf16),
            vmem(wo.shape, bf16),
            vmem((n_vec, width), f32),
            vmem((6, rows_plane // 2, cols_q), bf16),
            vmem((6, rows_plane // 2, n_hid), bf16),
            vmem((6, rows_down // 2, width), bf16),
            vmem((near, rows_in, width), bf16),
            vmem((near, n_vec, rows_plane), f32),
            vmem((rows_in, width), bf16),
            vmem((n_vec, rows_plane), f32),
            vmem((n_slice, n_vec, 2 * rows_in), f32),
            dma((13,)),
            dma((3, n_plane)),
            dma((2, n_shard)),
            dma((2, n_shard)),
            dma((2, 2, n_shard)),
            dma((2, 2, n_shard)),
            dma((2, near)),
            dma((2, near)),
            dma((3, 6)),
            dma((3, 6)),
            dma((3, n_slice - 1, n_plane)),
            dma((3, n_slice - 1, n_plane)),
            dma,
            dma,
            dma,
            pltpu.SemaphoreType.REGULAR,
        ],
        compiler_params=pltpu.CompilerParams(
            collective_id=1, has_side_effects=True, vmem_limit_bytes=59 * 1024 * 1024
        ),
        name="backward_all",
    )(*arrays)


def fast_device(
    layer_input,
    out_grad,
    positions,
    w_qkv,
    w_dense,
    w_up,
    w_down,
    vectors,
    m_qkv,
    m_dense,
    m_up,
    m_down,
    m_vectors,
    v_qkv,
    v_dense,
    v_up,
    v_down,
    v_vectors,
):
    bf16 = jnp.bfloat16
    f32 = jnp.float32
    n_plane = lax.axis_size("plane")
    n_shard = lax.axis_size("shard")
    block_rows = layer_input.shape[1]
    n_vec, vec_cols = vectors.shape

    half_rot = ROT // 2
    inverse = 10000.0 ** (-jnp.arange(0, ROT, 2).astype(f32) / ROT)
    freq = jnp.pad(jnp.concatenate([inverse, inverse]), (0, 128 - 2 * half_rot))[None]
    kept = forward_all(
        n_plane,
        n_shard,
        layer_input[0],
        out_grad[0],
        positions.reshape(-1, block_rows),
        jnp.pad(vectors, ((0, 16 - n_vec), (0, 128 - vec_cols))),
        freq,
        w_qkv,
        w_up,
        w_down,
        w_dense,
    )
    branches, grad_hat, part_qkv, part_up, part_down, part_dense, part_vec = backward_all(
        n_plane, n_shard, *kept
    )
    full_vec = kept[-2]
    branches = branches.astype(f32)
    grad_hat = grad_hat.astype(f32)
    own_tokens = layer_input[0].astype(f32)
    grad_rows = out_grad[0].astype(f32)
    layer_output = (own_tokens + branches + full_vec[7] + full_vec[12]).astype(bf16)[None]
    own_center = own_tokens - jnp.mean(own_tokens, axis=-1, keepdims=True)
    own_inv = lax.rsqrt(jnp.mean(own_center * own_center, axis=-1, keepdims=True) + 1e-05)
    own_hat = own_center * own_inv
    grad_input = (
        grad_rows
        + own_inv
        * (
            grad_hat
            - jnp.mean(grad_hat, axis=-1, keepdims=True)
            - own_hat * jnp.mean(grad_hat * own_hat, axis=-1, keepdims=True)
        )
    )[None]
    grad_vectors = part_vec[:n_vec, :vec_cols]
    grad_dense = part_dense.astype(f32)
    grad_down = part_down.astype(f32)
    grad_qkv = part_qkv.astype(f32)
    grad_up = part_up.astype(f32)
    new_qkv, second_qkv = adam_step(w_qkv, grad_qkv, m_qkv, v_qkv, 4.0 * (D // 2) ** (-0.5), 0.1)
    new_dense, second_dense = adam_step(
        w_dense, grad_dense, m_dense, v_dense, 4.0 * (D // 32) ** (-0.5), 0.1
    )
    new_up, second_up = adam_step(w_up, grad_up, m_up, v_up, 4.0 * D ** (-0.5), 0.1)
    new_down, second_down = adam_step(w_down, grad_down, m_down, v_down, 4.0 * FF ** (-0.5), 0.1)
    new_vectors, second_vectors = adam_step(vectors, grad_vectors, m_vectors, v_vectors, 1.0, 0.0)
    return (
        layer_output,
        grad_input,
        grad_qkv,
        grad_dense,
        grad_up,
        grad_down,
        grad_vectors,
        second_qkv,
        second_dense,
        second_up,
        second_down,
        second_vectors,
        new_qkv,
        new_dense,
        new_up,
        new_down,
        new_vectors,
    )


def solution(mesh):
    n_ctx, n_shard = mesh.devices.shape
    if n_ctx == 2 * n_shard and n_ctx == H:
        device_mesh = Mesh(
            mesh.devices.reshape(n_shard, 2, n_shard), ("plane", "core", "shard")
        )
        ctx, body = ("plane", "core"), fast_device
    else:
        device_mesh, ctx, body = mesh, ("ctx",), general_device
    rows = P("shard", ctx, None)
    weight = P((*ctx, "shard"), None)
    vector = P(None, (*ctx, "shard"))
    matrices = (weight,) * 4 + (vector,)
    in_specs = (rows, rows, P("shard", None)) + matrices * 3
    out_specs = (rows, rows) + matrices * 3
    return jax.shard_map(
        body, mesh=device_mesh, in_specs=in_specs, out_specs=out_specs, check_vma=False
    )
```
